32 devices in a mesh: dp: 8 (over z, y), chan: 4 (over x, core).
Axes of the slice: x: 2, y: 2, z: 4, core: 2. Of those that a mesh axis runs over, the one named last changes fastest.
Arguments:
- images: bfloat16 [64, 256, 256], P(None, 'dp'), may hold values from -14 to 14
- mask: int32 [64, 64], P('dp'), may hold values from 0 to 1, as said below
- cotangent: bfloat16 [64, 64, 512], P('dp', None, 'chan'), may hold values from -14 to 14
- w_first: float32 [2304, 512], P('dp', 'chan'), may hold values from -0.125 to 0.125
- w_second: float32 [4608, 512], P('dp', 'chan'), may hold values from -0.09375 to 0.09375
- w_proj: float32 [256, 512], P('dp', 'chan'), may hold values from -0.375 to 0.375
- norm_params: float32 [6, 512], P(None, 'chan'), may hold values from -2.8 to 2.8, as said below
- mom_first: float32 [2304, 512], P('dp', 'chan'), may hold values from -0.0625 to 0.0625
- mom_second: float32 [4608, 512], P('dp', 'chan'), may hold values from -0.046875 to 0.046875
- mom_proj: float32 [256, 512], P('dp', 'chan'), may hold values from -0.1875 to 0.1875
- mom_norm: float32 [6, 512], P(None, 'chan'), may hold values from -1.8 to 1.8
- avg_first: float32 [2304, 512], P('dp', 'chan'), may hold values from -0.125 to 0.125
- avg_second: float32 [4608, 512], P('dp', 'chan'), may hold values from -0.09375 to 0.09375
- avg_proj: float32 [256, 512], P('dp', 'chan'), may hold values from -0.375 to 0.375
- avg_norm: float32 [6, 512], P(None, 'chan'), may hold values from 0.5 to 1.5
Outputs:
- output: bfloat16 [64, 64, 512], P('dp', None, 'chan')
- grad_images: bfloat16 [64, 256, 256], P(None, 'dp', 'chan')
- new_first: float32 [2304, 512], P('dp', 'chan')
- new_mom_first: float32 [2304, 512], P('dp', 'chan')
- new_avg_first: float32 [2304, 512], P('dp', 'chan')
- new_second: float32 [4608, 512], P('dp', 'chan')
- new_mom_second: float32 [4608, 512], P('dp', 'chan')
- new_avg_second: float32 [4608, 512], P('dp', 'chan')
- new_proj: float32 [256, 512], P('dp', 'chan')
- new_mom_proj: float32 [256, 512], P('dp', 'chan')
- new_avg_proj: float32 [256, 512], P('dp', 'chan')
- new_norm: float32 [6, 512], P(None, 'chan')
- new_mom_norm: float32 [6, 512], P(None, 'chan')
- new_avg_norm: float32 [6, 512], P(None, 'chan')
The draws below stay inside these ranges and needn't reach their ends.
Inputs may be any that keep to these rules, and one draw needn't show every extreme that they name: `mask`: each image's valid output pixels form a rectangle of h by w pixels at its top-left corner, with h and w at least 3. So every gradient of an output-side array is zero outside that rectangle, grad_hidden is zero outside the first h + 1 rows and w + 1 columns of its image, and the input's gradient is zero outside the first 2 h rows and 2 w columns of its image; a program may send only the pixels outside these zero regions. `norm_params`: rows 0, 2 and 4 are positive.
All inputs are finite; a program needn't handle non-finite values.
Results may differ from the reference program's by a relative error of at most 0.0075.
Values may be sent and summed in bfloat16 or wider, within the bound.
No kernel may reach another device: no remote copies, remote signals or barrier semaphores. Data moves between devices by JAX's collectives and lax.ppermute only.
A program may use at most 64 MiB of HBM per device.

```python
from functools import partial
import jax
import jax.numpy as jnp
from jax import lax

D_IN = 256
D_OUT = 512
B_DEV = 8
IN_SIDE = 16
OUT_SIDE = 8
IN_PIX = 256
OUT_PIX = 64
BATCH = 64


def channel_scale(key, width, ratio):
    rough = jax.random.uniform(key, (width,), jnp.float32, 0.8, 1.25)
    ramp = jnp.arange(width, dtype=jnp.float32) / (width - 1)
    return jnp.exp(jnp.log(0.6) + jnp.log(ratio) * ramp) * rough


def draw_images(key, part):
    key = jax.random.fold_in(key, 11)
    scale_key, value_key = jax.random.split(key)
    scales = channel_scale(scale_key, D_IN, 3.0)
    values = jnp.clip(jax.random.normal(value_key, (BATCH, IN_PIX, D_IN), jnp.float32), -6.0, 6.0)
    return (values * scales).astype(jnp.bfloat16)


def draw_cotangent(key, part):
    key = jax.random.fold_in(key, 12)
    scale_key, value_key = jax.random.split(key)
    scales = channel_scale(scale_key, D_OUT, 3.0)
    values = jnp.clip(jax.random.normal(value_key, (BATCH, OUT_PIX, D_OUT), jnp.float32), -6.0, 6.0)
    return (values * scales).astype(jnp.bfloat16)


def draw_norm_params(key, part):
    key = jax.random.fold_in(key, 13)
    rough_key, shift_key = jax.random.split(key)
    ramp = jnp.arange(D_OUT, dtype=jnp.float32) / (D_OUT - 1)
    rising = jnp.exp(jnp.log(0.6) + jnp.log(3.0) * ramp)
    rough = jax.random.uniform(rough_key, (6, D_OUT), jnp.float32, 0.8, 1.25)
    gains = rising * rough
    shifts = 0.3 * jnp.clip(jax.random.normal(shift_key, (6, D_OUT), jnp.float32), -4.0, 4.0) * gains
    rows = jnp.arange(6)[:, None]
    return jnp.where(rows % 2 == 0, gains, shifts).astype(jnp.float32)


def draw_mask(key, part):
    key = jax.random.fold_in(key, 14)
    height_key, width_key = jax.random.split(key)
    groups = BATCH // B_DEV
    group_of = jnp.arange(BATCH, dtype=jnp.int32) // B_DEV
    half = OUT_SIDE // 2
    top = half + half * group_of // max(groups - 1, 1)
    heights = top - jax.random.randint(height_key, (BATCH,), 0, 2)
    widths = top - jax.random.randint(width_key, (BATCH,), 0, 2)
    places = jnp.arange(OUT_PIX, dtype=jnp.int32)
    inside = (places[None, :] // OUT_SIDE < heights[:, None]) & (places[None, :] % OUT_SIDE < widths[:, None])
    return inside.astype(jnp.int32)


def block_scale(key, dims, cuts, low, high):
    level, own = 1.0, jax.random.fold_in(key, 6)
    for position, shards_of in cuts:
        draws = jnp.exp(jax.random.uniform(jax.random.fold_in(own, position), (shards_of,), jnp.float32, low / len(cuts), high / len(cuts)))
        level = level * jnp.repeat(draws, dims[position] // shards_of).reshape([-1 if axis == position else 1 for axis in range(len(dims))])
    return level


def scatter_about(own_key, dims, scale, bound, cuts=(), kind=jnp.bfloat16):
    factor_of = block_scale(own_key, dims, cuts, -0.22, 0.18) if cuts else 1.0
    values = jax.random.normal(own_key, dims, jnp.float32) * scale * factor_of
    return jnp.minimum(jnp.maximum(values, -bound), bound).astype(kind)


def setup_inputs(seed: int = 0) -> dict:
    keys = jax.random.split(jax.random.key(seed), 16)
    return {
        "images": draw_images(jax.random.fold_in(keys[15], 71), 0),
        "mask": draw_mask(jax.random.fold_in(keys[15], 71), 0),
        "cotangent": draw_cotangent(jax.random.fold_in(keys[15], 71), 0),
        "w_first": scatter_about(keys[3], (9 * D_IN, D_OUT), (9 * D_IN) ** -0.5, 0.125, ((0, 8), (1, 4)), jnp.float32),
        "w_second": scatter_about(keys[4], (9 * D_OUT, D_OUT), (9 * D_OUT) ** -0.5, 0.09375, ((0, 8), (1, 4)), jnp.float32),
        "w_proj": scatter_about(keys[5], (D_IN, D_OUT), D_IN ** -0.5, 0.375, ((0, 8), (1, 4)), jnp.float32),
        "norm_params": draw_norm_params(jax.random.fold_in(keys[15], 71), 0),
        "mom_first": scatter_about(keys[7], (9 * D_IN, D_OUT), (36 * D_IN) ** -0.5, 0.0625, ((0, 8), (1, 4)), jnp.float32),
        "mom_second": scatter_about(keys[8], (9 * D_OUT, D_OUT), (36 * D_OUT) ** -0.5, 0.046875, ((0, 8), (1, 4)), jnp.float32),
        "mom_proj": scatter_about(keys[9], (D_IN, D_OUT), (4 * D_IN) ** -0.5, 0.1875, ((0, 8), (1, 4)), jnp.float32),
        "mom_norm": scatter_about(keys[10], (6, D_OUT), 0.3, 1.8, ((1, 4),), jnp.float32),
        "avg_first": scatter_about(keys[11], (9 * D_IN, D_OUT), (9 * D_IN) ** -0.5, 0.125, ((0, 8), (1, 4)), jnp.float32),
        "avg_second": scatter_about(keys[12], (9 * D_OUT, D_OUT), (9 * D_OUT) ** -0.5, 0.09375, ((0, 8), (1, 4)), jnp.float32),
        "avg_proj": scatter_about(keys[13], (D_IN, D_OUT), D_IN ** -0.5, 0.375, ((0, 8), (1, 4)), jnp.float32),
        "avg_norm": jnp.clip(1.0 + 0.1 * jax.random.normal(keys[14], (6, D_OUT), jnp.float32), 0.5, 1.5),
    }


epsilon = 1e-05
learn_rate = 0.4
trust_coef = 0.5
momentum = 0.5
avg_decay = 0.6
weight_decay = 5e-05
tiny_term = 1e-06

@jax.custom_vjp
def low(v):
    return lax.optimization_barrier(v.astype(jnp.bfloat16)).astype(jnp.float32)

@jax.custom_vjp
def low_back(v):
    return v

def low_keep(v):
    return (low(v), None)

def low_pass(kept, grad):
    return (grad,)

def back_keep(v):
    return (v, None)

def back_low(kept, grad):
    return (low(grad),)
low.defvjp(low_keep, low_pass)
low_back.defvjp(back_keep, back_low)

def kernel_of(weight_rows):
    inputs_count = weight_rows.shape[0] // 9
    return jnp.transpose(weight_rows.reshape(inputs_count, 3, 3, weight_rows.shape[1]), (1, 2, 0, 3))

def convolve(pixels, weight_rows, stride):
    return lax.conv_general_dilated(pixels, kernel_of(weight_rows), (stride, stride), ((1, 1), (1, 1)), dimension_numbers=('NHWC', 'HWIO', 'NHWC'), precision=lax.Precision.HIGHEST)

def normalize(values, gain_row, shift_row, validity, pixel_count):
    total = lax.optimization_barrier(jnp.sum(validity * values, axis=(0, 1, 2)))
    squares = lax.optimization_barrier(jnp.sum(validity * values * values, axis=(0, 1, 2)))
    center = total / pixel_count
    spread = squares / pixel_count - center * center
    return (values - center) * lax.rsqrt(spread + epsilon) * gain_row + shift_row

def forward(inputs, first, second, proj, params, validity, pixel_count):
    conv_first = low_back(convolve(inputs, low(first), 2))
    lin_first = normalize(conv_first, params[0], params[1], validity, pixel_count)
    hidden = low(jax.nn.silu(lin_first) * validity)
    conv_second = low_back(convolve(hidden, low(second), 1))
    strided = inputs[:, ::2, ::2, :]
    conv_proj = low_back(jnp.einsum('bhwi,io->bhwo', strided, low(proj), precision=lax.Precision.HIGHEST))
    summed = normalize(conv_second, params[2], params[3], validity, pixel_count) + normalize(conv_proj, params[4], params[5], validity, pixel_count)
    return jax.nn.silu(summed) * validity

def update(weight, grad, moment, average, weight_sq, grad_sq):
    weight_len = jnp.sqrt(weight_sq)
    trust = trust_coef * weight_len / (jnp.sqrt(grad_sq) + weight_decay * weight_len + tiny_term)
    step = trust * (grad + weight_decay * weight)
    moment_new = momentum * moment + step
    weight_new = weight - learn_rate * (step + momentum * moment_new)
    average_new = avg_decay * average + (1.0 - avg_decay) * weight_new
    return (weight_new, moment_new, average_new)

def reference(images, mask, cotangent, w_first, w_second, w_proj, norm_params, mom_first, mom_second, mom_proj, mom_norm, avg_first, avg_second, avg_proj, avg_norm):
    images_total = images.shape[0]
    inputs = images.astype(jnp.float32).reshape(images_total, IN_SIDE, IN_SIDE, D_IN)
    validity = mask.astype(jnp.float32).reshape(images_total, OUT_SIDE, OUT_SIDE, 1)
    pixel_count = jnp.sum(validity)
    result, pullback = jax.vjp(partial(forward, validity=validity, pixel_count=pixel_count), inputs, w_first, w_second, w_proj, norm_params)
    back = cotangent.astype(jnp.float32).reshape(images_total, OUT_SIDE, OUT_SIDE, D_OUT)
    grad_inputs, grad_first, grad_second, grad_proj, grad_norm = pullback(back)
    first_new, first_mom, first_avg = update(w_first, grad_first, mom_first, avg_first, jnp.sum(w_first * w_first), jnp.sum(grad_first * grad_first))
    second_new, second_mom, second_avg = update(w_second, grad_second, mom_second, avg_second, jnp.sum(w_second * w_second), jnp.sum(grad_second * grad_second))
    proj_new, proj_mom, proj_avg = update(w_proj, grad_proj, mom_proj, avg_proj, jnp.sum(w_proj * w_proj), jnp.sum(grad_proj * grad_proj))
    norm_new, norm_mom, norm_avg = update(norm_params, grad_norm, mom_norm, avg_norm, lax.optimization_barrier(jnp.sum(norm_params * norm_params, axis=1, keepdims=True)), lax.optimization_barrier(jnp.sum(grad_norm * grad_norm, axis=1, keepdims=True)))
    output = result.astype(jnp.bfloat16).reshape(images_total, OUT_PIX, D_OUT)
    grad_images = grad_inputs.astype(jnp.bfloat16).reshape(images_total, IN_PIX, D_IN)
    return (output, grad_images, first_new, first_mom, first_avg, second_new, second_mom, second_avg, proj_new, proj_mom, proj_avg, norm_new, norm_mom, norm_avg)
```

```python
import jax
import jax.numpy as jnp
from jax import lax
from jax.experimental import pallas as pl
from jax.experimental.pallas import tpu as pltpu
from jax.sharding import PartitionSpec as P

BF = jnp.bfloat16
F32 = jnp.float32

epsilon = 1e-05
learn_rate = 0.4
trust_coef = 0.5
momentum = 0.5
avg_decay = 0.6
weight_decay = 5e-05
tiny_term = 1e-06

SIDE = 8


def dot(a, b):
    return jnp.dot(a, b, preferred_element_type=F32)


def dot_nt(a, b):
    return lax.dot_general(a, b, (((1,), (1,)), ((), ())), preferred_element_type=F32)


def dot_tn(a, b):
    return lax.dot_general(a, b, (((0,), (0,)), ((), ())), preferred_element_type=F32)


def shift_col(x, step):
    rows, lanes = x.shape
    grouped = x.reshape(rows // SIDE, SIDE, lanes)
    rolled = pltpu.roll(grouped, step % SIDE, 1)
    col = lax.broadcasted_iota(jnp.int32, grouped.shape, 1)
    edge = 0 if step > 0 else SIDE - 1
    return jnp.where(col == edge, 0.0, rolled).reshape(rows, lanes)


def shift_row(x, step):
    part = x.shape[0] // SIDE
    blank = jnp.zeros((part, x.shape[1]), x.dtype)
    if step > 0:
        return jnp.concatenate([blank, x[:-part]], axis=0)
    return jnp.concatenate([x[part:], blank], axis=0)


def call(body, outs, *args, flops=0, limit=32):
    moved = sum(a.size * a.dtype.itemsize for a in args)
    moved += sum(o.size * o.dtype.itemsize for o in outs)
    spec = pl.BlockSpec(memory_space=pltpu.VMEM)
    return pl.pallas_call(
        body,
        out_shape=outs,
        in_specs=[spec] * len(args),
        out_specs=[spec] * len(outs),
        compiler_params=pltpu.CompilerParams(vmem_limit_bytes=limit * 2**20),
        cost_estimate=pl.CostEstimate(flops=flops, bytes_accessed=moved, transcendentals=0),
        name=body.__name__,
    )(*args)


def shape(dims, dtype=F32):
    return jax.ShapeDtypeStruct(tuple(dims), dtype)


def col_sum(x):
    return jnp.sum(x, axis=0, keepdims=True)


def rows_of(*rows):
    pad = SIDE - len(rows)
    tail = [jnp.zeros((pad, rows[0].shape[1]), F32)] if pad else []
    return jnp.concatenate(list(rows) + tail, axis=0)


def mean_inverse(total, squares, count):
    center = total / count
    spread = squares / count - center * center
    return center, lax.rsqrt(spread + epsilon)


def slope(v):
    sigma = jax.nn.sigmoid(v)
    return sigma * (1.0 + v * (1.0 - sigma))


def pack_first_body(w_ref, p_ref, out_ref):
    depth = p_ref.shape[0]
    for tap in range(9):
        block = w_ref[pl.ds(tap, depth, stride=9), :].astype(BF)
        out_ref[:, tap] = jnp.broadcast_to(block[None], (out_ref.shape[0],) + block.shape)
    block = p_ref[...].astype(BF)
    out_ref[:, 9] = jnp.broadcast_to(block[None], (out_ref.shape[0],) + block.shape)


def pack_second_body(w_ref, out_ref):
    depth = w_ref.shape[0] // 9
    for tap in range(9):
        block = w_ref[pl.ds(tap, depth, stride=9), :].astype(BF)
        out_ref[:, tap] = jnp.broadcast_to(block[None], (out_ref.shape[0],) + block.shape)


def tap_major(w):
    return w.reshape(-1, 9, w.shape[1]).transpose(1, 0, 2)


def conv_first_body(x_ref, w_ref, m_ref, n_ref, z_ref, zp_ref, ph_ref, pay_ref):
    owners, lanes = x_ref.shape[0], x_ref.shape[4] // 2
    phases = []
    for phase in range(4):
        pr, pc = phase // 2, phase % 2
        pieces = [
            x_ref[k, r, pr, :, pc * lanes : (pc + 1) * lanes]
            for r in range(SIDE)
            for k in range(owners)
        ]
        phases.append(jnp.concatenate(pieces, axis=0))
        ph_ref[phase] = phases[-1]

    def taps(*which):
        return jnp.concatenate([w_ref[:, t].reshape(lanes, -1) for t in which], axis=1)

    wide = w_ref.shape[3]
    y00 = dot(phases[0], taps(4, 9))
    y01 = dot(phases[1], taps(5, 3))
    y10 = dot(phases[2], taps(7, 1))
    y11 = dot(phases[3], taps(8, 6, 2, 0))
    here = y00[:, :wide] + y01[:, :wide] + y10[:, :wide] + y11[:, :wide]
    left = y01[:, wide:] + y11[:, wide : 2 * wide]
    above = y10[:, wide:] + y11[:, 2 * wide : 3 * wide]
    corner = y11[:, 3 * wide :]
    z = here + shift_row(above, 1) + shift_col(left + shift_row(corner, 1), 1)
    zp = y00[:, wide:]
    valid = m_ref[...]
    z_ref[...] = z.astype(BF)
    zp_ref[...] = zp
    vz, vzp = valid * z, valid * zp
    rows = rows_of(
        col_sum(vz),
        col_sum(vz * z),
        col_sum(valid),
        n_ref[0:1],
        n_ref[1:2],
        col_sum(vzp),
        col_sum(vzp * zp),
    )
    pay_ref[...] = jnp.broadcast_to(rows[None], pay_ref.shape)


def first_norm(z, rows):
    count = rows[2:3]
    center, inverse = mean_inverse(rows[0:1], rows[1:2], count)
    hat = (z - center) * inverse
    return hat, inverse, hat * rows[3:4] + rows[4:5]


def first_totals(r_ref, k):
    total = jnp.sum(r_ref[:, k], axis=0)
    return jnp.concatenate([total[0:3], r_ref[0, k, 3:5], total[5:8]], axis=0)


def conv_second_body(z_ref, r_ref, m_ref, w_ref, h_ref, z2_ref, pay_ref):
    blocks, wide = z_ref.shape[0], z_ref.shape[2]
    valid = m_ref[...]
    hidden = []
    for k in range(blocks):
        _, _, lin = first_norm(z_ref[k].astype(F32), first_totals(r_ref, k))
        hidden.append((lin * jax.nn.sigmoid(lin) * valid).astype(BF))
        h_ref[:, k * wide : (k + 1) * wide] = hidden[-1]
    hidden = jnp.concatenate(hidden, axis=1)
    sums = []
    for col in range(3):
        w = jnp.concatenate(
            [w_ref[:, 3 * row + col].reshape(hidden.shape[1], wide) for row in range(3)], axis=1
        )
        y = dot(hidden, w)
        sums.append(
            shift_row(y[:, :wide], 1) + y[:, wide : 2 * wide] + shift_row(y[:, 2 * wide :], -1)
        )
    z2 = sums[1] + shift_col(sums[0], 1) + shift_col(sums[2], -1)
    z2_ref[...] = z2
    vz = valid * z2
    rows = rows_of(col_sum(vz), col_sum(vz * z2))
    pay_ref[...] = jnp.broadcast_to(rows[None], pay_ref.shape)


def first_slopes_body(z_ref, r_ref, m_ref, hat_ref, slope_ref):
    for k in range(z_ref.shape[0]):
        hat, _, lin = first_norm(z_ref[k].astype(F32), first_totals(r_ref, k))
        hat_ref[k] = hat
        slope_ref[k] = slope(lin) * m_ref[...]


def output_body(z2_ref, zp_ref, r2_ref, r1_ref, m_ref, n_ref, cot_ref, out_ref, e_ref, pay_ref):
    total, first = jnp.sum(r2_ref[...], axis=0), jnp.sum(r1_ref[...], axis=0)
    count = first[2:3]
    center2, inverse2 = mean_inverse(total[0:1], total[1:2], count)
    center_p, inverse_p = mean_inverse(first[5:6], first[6:7], count)
    hat2 = (z2_ref[...] - center2) * inverse2
    hat_p = (zp_ref[...] - center_p) * inverse_p
    summed = hat2 * n_ref[2:3] + n_ref[3:4] + (hat_p * n_ref[4:5] + n_ref[5:6])
    sigma = jax.nn.sigmoid(summed)
    valid = m_ref[...]
    out_ref[...] = (summed * sigma * valid).astype(BF)
    e = cot_ref[...].astype(F32) * valid * (sigma * (1.0 + summed * (1.0 - sigma)))
    e_ref[...] = e
    rows = rows_of(col_sum(e), col_sum(e * hat2), col_sum(e * hat_p))
    pay_ref[...] = jnp.broadcast_to(rows[None], pay_ref.shape)


def grad_hidden_body(
    z2_ref, zp_ref, e_ref, r2_ref, r1_ref, r3_ref, m_ref, n_ref, w_ref, hat_ref, slope_ref,
    gh_ref, gp_ref, q_ref, pay_ref, tot_ref,
):
    total, first = jnp.sum(r2_ref[...], axis=0), jnp.sum(r1_ref[...], axis=0)
    back = jnp.sum(r3_ref[...], axis=0)
    tot_ref[...] = back
    count = first[2:3]
    valid, e = m_ref[...], e_ref[...]
    center2, inverse2 = mean_inverse(total[0:1], total[1:2], count)
    center_p, inverse_p = mean_inverse(first[5:6], first[6:7], count)
    hat2 = (z2_ref[...] - center2) * inverse2
    hat_p = (zp_ref[...] - center_p) * inverse_p
    share = 1.0 / count
    g2 = n_ref[2:3] * inverse2 * (e - valid * ((back[0:1] + hat2 * back[1:2]) * share))
    gp = n_ref[4:5] * inverse_p * (e - valid * ((back[0:1] + hat_p * back[2:3]) * share))
    gp_ref[...] = gp.astype(BF)
    wide = g2.shape[1]
    for col, moved in enumerate((shift_col(g2, -1), g2, shift_col(g2, 1))):
        moved = moved.astype(BF)
        for row, step in enumerate((-1, 0, 1)):
            tap = 3 * row + col
            q_ref[:, tap * wide : (tap + 1) * wide] = shift_row(moved, step) if step else moved
    q = q_ref[...]
    blocks = gh_ref.shape[0]
    depth = q.shape[0]
    depth = w_ref.shape[0] * w_ref.shape[2]
    w = jnp.concatenate([w_ref[:, t].reshape(depth, wide) for t in range(9)], axis=1)
    part = depth // blocks
    for k in range(blocks):
        gh = dot_nt(q, w[k * part : (k + 1) * part])
        gh_ref[k] = gh.astype(BF)
        b = gh * slope_ref[k]
        rows = rows_of(col_sum(b), col_sum(b * hat_ref[k]))
        pay_ref[:, k] = jnp.broadcast_to(rows[None], (pay_ref.shape[0],) + rows.shape)


def grad_second_body(h_ref, q_ref, x_ref, gp_ref, g_ref):
    groups, rows, wide = g_ref.shape
    share = h_ref.shape[1] // groups
    h = h_ref[...]
    for tap in range(9):
        g = dot_tn(h, q_ref[:, tap * wide : (tap + 1) * wide]).astype(BF)
        g_ref[:, tap * share : (tap + 1) * share] = g.reshape(groups, share, wide)
    g = dot_tn(x_ref[0], gp_ref[...]).astype(BF)
    g_ref[:, 9 * share :] = g.reshape(groups, rows - 9 * share, wide)


def grad_first_body(gh_ref, r4_ref, r1_ref, hat_ref, slope_ref, m_ref, n_ref, x_ref, q_ref, g_ref, tot_ref):
    first, back = jnp.sum(r1_ref[...], axis=0), jnp.sum(r4_ref[...], axis=0)
    tot_ref[...] = back
    count = first[2:3]
    _, inverse = mean_inverse(first[0:1], first[1:2], count)
    gh = gh_ref[0].astype(F32)
    for k in range(1, gh_ref.shape[0]):
        gh = gh + gh_ref[k].astype(F32)
    hat = hat_ref[...]
    b = gh * slope_ref[...]
    g = n_ref[0:1] * inverse * (b - m_ref[...] * ((back[0:1] + hat * back[1:2]) / count))
    wide = g.shape[1]
    here, left = g.astype(BF), shift_col(g, -1).astype(BF)
    q_ref[:, :wide] = here
    q_ref[:, wide : 2 * wide] = left
    q_ref[:, 2 * wide : 3 * wide] = shift_row(here, -1)
    q_ref[:, 3 * wide :] = shift_row(left, -1)
    q = q_ref[...]
    groups = g_ref.shape[0]
    share = x_ref.shape[2] // groups

    def put(tap, grad):
        g_ref[:, tap * share : (tap + 1) * share] = grad.astype(BF).reshape(groups, share, wide)

    put(4, dot_tn(x_ref[0], q[:, :wide]))
    both = dot_tn(x_ref[1], q[:, : 2 * wide])
    put(5, both[:, :wide])
    put(3, both[:, wide:])
    both = dot_tn(x_ref[2], jnp.concatenate([q[:, :wide], q[:, 2 * wide : 3 * wide]], axis=1))
    put(7, both[:, :wide])
    put(1, both[:, wide:])
    four = dot_tn(x_ref[3], q)
    for place, tap in enumerate((8, 6, 2, 0)):
        put(tap, four[:, place * wide : (place + 1) * wide])


def grad_images_body(q_ref, gp_ref, w_ref, out_ref):
    blocks, sides, _, part, wide = out_ref.shape
    q, gp = q_ref[...], gp_ref[...]
    depth = w_ref.shape[0] * w_ref.shape[2]

    def taps(*which):
        return jnp.concatenate([w_ref[:, t].reshape(depth, wide) for t in which], axis=1)

    here, left, above = q[:, :wide], q[:, wide : 2 * wide], q[:, 2 * wide : 3 * wide]
    d00 = dot_nt(jnp.concatenate([here, gp], axis=1), taps(4, 9))
    d01 = dot_nt(jnp.concatenate([here, left], axis=1), taps(5, 3))
    d10 = dot_nt(jnp.concatenate([here, above], axis=1), taps(7, 1))
    d11 = dot_nt(q, taps(8, 6, 2, 0))
    half = wide // 2
    for pr, (even, odd) in enumerate(((d00, d01), (d10, d11))):
        for k in range(blocks):
            cut = slice(k * half, (k + 1) * half)
            pair = jnp.concatenate([even[:, cut], odd[:, cut]], axis=1).astype(BF)
            out_ref[k, :, pr] = pair.reshape(sides, part, wide)


def sum_blocks_body(x_ref, o_ref):
    total = x_ref[0].astype(F32)
    for k in range(1, x_ref.shape[0]):
        total = total + x_ref[k].astype(F32)
    o_ref[...] = total.astype(o_ref.dtype)


def lane_sum(x):
    return jnp.sum(col_sum(x), axis=1, keepdims=True)


def reduce_second_body(x_ref, g_ref, gp_ref):
    total = x_ref[0].astype(F32)
    for k in range(1, x_ref.shape[0]):
        total = total + x_ref[k].astype(F32)
    depth = g_ref.shape[0] // 9
    for tap in range(9):
        g_ref[pl.ds(tap, depth, stride=9), :] = total[tap * depth : (tap + 1) * depth]
    gp_ref[...] = total[9 * depth :]


def reduce_first_body(
    x_ref, g2_ref, gp_ref, w1_ref, w2_ref, wp_ref, t3_ref, t4_ref, n_ref, g_ref, pay_ref
):
    total = x_ref[0].astype(F32)
    for k in range(1, x_ref.shape[0]):
        total = total + x_ref[k].astype(F32)
    depth = g_ref.shape[0] // 9
    for tap in range(9):
        g_ref[pl.ds(tap, depth, stride=9), :] = total[tap * depth : (tap + 1) * depth]
    conv = []
    for v in (w1_ref[...], total, w2_ref[...], g2_ref[...], wp_ref[...], gp_ref[...]):
        conv.append(lane_sum(v * v))
    n = n_ref[...]
    gn = norm_grad(t3_ref, t4_ref)
    one = jnp.sum(n * n, axis=1, keepdims=True)
    two = jnp.sum(gn * gn, axis=1, keepdims=True)
    blank = jnp.zeros((2, 1), F32)
    cols = [jnp.concatenate(conv + [blank], axis=0)]
    cols += [jnp.concatenate([v, blank], axis=0) for v in (one, two)]
    lane = lax.broadcasted_iota(jnp.int32, pay_ref.shape[1:], 1)
    block = jnp.zeros(pay_ref.shape[1:], F32)
    for place, col in enumerate(cols):
        block = jnp.where(lane == place, col, block)
    pay_ref[...] = jnp.broadcast_to(block[None], pay_ref.shape)


def norm_grad(t3_ref, t4_ref):
    return jnp.concatenate(
        [t4_ref[1:2], t4_ref[0:1], t3_ref[1:2], t3_ref[0:1], t3_ref[2:3], t3_ref[0:1]], axis=0
    )


def step_of(w, g, m, a, weight_sq, grad_sq):
    weight_len = jnp.sqrt(weight_sq)
    trust = trust_coef * weight_len / (jnp.sqrt(grad_sq) + weight_decay * weight_len + tiny_term)
    step = trust * (g + weight_decay * w)
    m_new = momentum * m + step
    w_new = w - learn_rate * (step + momentum * m_new)
    return w_new, m_new, avg_decay * a + (1.0 - avg_decay) * w_new


def make_update_body(dp_count):
    def update_body(*refs):
        r6_ref, t3_ref, t4_ref = refs[:3]
        ins, outs = refs[3:18], refs[18:]
        total = jnp.sum(r6_ref[...], axis=0)
        for place in range(3):
            w, g, m, a = (ref[...] for ref in ins[4 * place : 4 * place + 4])
            weight_sq, grad_sq = total[2 * place : 2 * place + 1, 0:1], total[2 * place + 1 : 2 * place + 2, 0:1]
            for ref, value in zip(outs[3 * place :], step_of(w, g, m, a, weight_sq, grad_sq)):
                ref[...] = value
        w, m, a = (ref[...] for ref in ins[12:15])
        weight_sq, grad_sq = total[0:6, 1:2] / dp_count, total[0:6, 2:3] / dp_count
        g = norm_grad(t3_ref, t4_ref)
        for ref, value in zip(outs[9:], step_of(w, g, m, a, weight_sq, grad_sq)):
            ref[...] = value

    return update_body


def exchange(blocks, axes):
    return lax.all_to_all(blocks, axes, 0, 0)


def per_device(
    images, mask, cotangent, w_first, w_second, w_proj, norm_params, mom_first, mom_second,
    mom_proj, mom_norm, avg_first, avg_second, avg_proj, avg_norm,
):
    everyone = ("dp", "chan")
    dp_count, ch_count = lax.axis_size("dp"), lax.axis_size("chan")
    n_all = dp_count * ch_count
    me = lax.axis_index("chan")
    batch = mask.shape[0]
    pix_here, d_in = images.shape[1], images.shape[2]
    wide = w_first.shape[1]
    d_out = wide * ch_count
    pix = SIDE * SIDE * batch
    whole_rows = pix_here == 4 * SIDE
    first_here, second_here = d_in // dp_count, d_out // dp_count
    aligned = first_here % 16 == 0
    groups = dp_count if aligned else 1

    if aligned:
        (packed,) = call(
            pack_first_body, [shape((dp_count, 10, first_here, wide), BF)], w_first, w_proj
        )
    else:
        packed = jnp.concatenate([tap_major(w_first), w_proj[None]], axis=0).astype(BF)
        packed = jnp.broadcast_to(packed[None], (dp_count,) + packed.shape)
    taps_first = exchange(packed, "dp")

    share = batch // ch_count
    mine = images.reshape(dp_count, ch_count, share, pix_here, d_in)
    mine = lax.dynamic_index_in_dim(mine, me, 1, keepdims=False)
    if whole_rows:
        mine = mine.reshape(dp_count, share, 2, SIDE, 2 * d_in).transpose(0, 2, 1, 3, 4)
        mine = mine.reshape(dp_count, 2, share * SIDE, 2 * d_in)
        pixels = lax.all_gather(exchange(mine, "dp"), "chan")
    else:
        pixels = lax.all_gather(exchange(mine, "dp"), "chan")
        part = pix_here // 2
        pixels = pixels.reshape(ch_count, SIDE, 2, SIDE // part, share, part, 2 * d_in)
        pixels = pixels.transpose(0, 1, 2, 4, 3, 5, 6)
        pixels = pixels.reshape(ch_count, SIDE, 2, share * SIDE, 2 * d_in)

    if aligned:
        (packed,) = call(pack_second_body, [shape((dp_count, 9, second_here, wide), BF)], w_second)
    else:
        packed = tap_major(w_second).astype(BF)
        packed = jnp.broadcast_to(packed[None], (dp_count,) + packed.shape)
    taps_second = exchange(packed, "dp")
    if not aligned:
        taps_first = taps_first.transpose(1, 0, 2, 3).reshape(1, 10, d_in, wide)
        taps_second = taps_second.transpose(1, 0, 2, 3).reshape(1, 9, d_out, wide)

    valid = mask.reshape(batch, SIDE, SIDE).transpose(1, 0, 2).reshape(pix, 1).astype(F32)
    valid = jnp.broadcast_to(valid, (pix, wide))
    cot = cotangent.reshape(batch, SIDE, SIDE, wide).transpose(1, 0, 2, 3).reshape(pix, wide)

    macs = pix * 9 * wide * d_in
    z_own, z_proj, phases, pay = call(
        conv_first_body,
        [
            shape((pix, wide), BF),
            shape((pix, wide)),
            shape((4, pix, d_in), BF),
            shape((n_all, SIDE, wide)),
        ],
        pixels,
        taps_first,
        valid,
        norm_params,
        flops=2 * macs,
    )
    got1 = exchange(pay, everyone).reshape(dp_count, ch_count, SIDE, wide)
    z_all = lax.all_gather(z_own, "chan")
    got1_own = lax.dynamic_index_in_dim(got1, me, 1, keepdims=False)

    hidden, z_second, pay = call(
        conv_second_body,
        [shape((pix, d_out), BF), shape((pix, wide)), shape((dp_count, SIDE, wide))],
        z_all,
        got1,
        valid,
        taps_second,
        flops=4 * macs,
    )
    got2 = exchange(pay, "dp")
    hats, slopes = call(
        first_slopes_body, [shape((ch_count, pix, wide))] * 2, z_all, got1, valid
    )
    hat_own = lax.dynamic_index_in_dim(hats, me, 0, keepdims=False)
    slope_own = lax.dynamic_index_in_dim(slopes, me, 0, keepdims=False)

    out, e, pay = call(
        output_body,
        [shape((pix, wide), BF), shape((pix, wide)), shape((dp_count, SIDE, wide))],
        z_second,
        z_proj,
        got2,
        got1_own,
        valid,
        norm_params,
        cot,
    )
    got3 = exchange(pay, "dp")
    output = out.reshape(SIDE, batch, SIDE, wide).transpose(1, 0, 2, 3)
    output = output.reshape(batch, SIDE * SIDE, wide)

    partial, g_proj_out, spread, pay, total3 = call(
        grad_hidden_body,
        [
            shape((ch_count, pix, wide), BF),
            shape((pix, wide), BF),
            shape((pix, 9 * wide), BF),
            shape((dp_count, ch_count, SIDE, wide)),
            shape((SIDE, wide)),
        ],
        z_second,
        z_proj,
        e,
        got2,
        got1_own,
        got3,
        valid,
        norm_params,
        taps_second,
        hats,
        slopes,
        flops=4 * macs,
    )
    got4 = exchange(pay.reshape(n_all, SIDE, wide), everyone)
    blocks = exchange(partial, "chan")

    rows_second = 9 * (d_out // groups) + d_in // groups
    (grad_second,) = call(
        grad_second_body,
        [shape((groups, rows_second, wide), BF)],
        hidden,
        spread,
        phases,
        g_proj_out,
        flops=4 * macs,
    )
    if not aligned:
        pieces = grad_second.reshape(rows_second, wide)
        conv = pieces[: 9 * d_out].reshape(9, dp_count, second_here, wide).transpose(1, 0, 2, 3)
        grad_second = jnp.concatenate(
            [
                conv.reshape(dp_count, 9 * second_here, wide),
                pieces[9 * d_out :].reshape(dp_count, first_here, wide),
            ],
            axis=1,
        )
    got_second = exchange(grad_second, "dp")

    moved, grad_first, total4 = call(
        grad_first_body,
        [
            shape((pix, 4 * wide), BF),
            shape((groups, 9 * (d_in // groups), wide), BF),
            shape((SIDE, wide)),
        ],
        blocks,
        got4,
        got1_own,
        hat_own,
        slope_own,
        valid,
        norm_params,
        phases,
        flops=2 * macs,
    )
    if not aligned:
        grad_first = grad_first.reshape(9, dp_count, first_here, wide).transpose(1, 0, 2, 3)
        grad_first = grad_first.reshape(dp_count, 9 * first_here, wide)
    got_first = exchange(grad_first, "dp")

    (image_blocks,) = call(
        grad_images_body,
        [shape((ch_count, SIDE, 2, batch * SIDE, wide), BF)],
        moved,
        g_proj_out,
        taps_first,
        flops=2 * macs,
    )
    image_blocks = exchange(image_blocks, "chan")
    (image_own,) = call(
        sum_blocks_body, [shape((SIDE, 2, batch * SIDE, wide), BF)], image_blocks
    )
    half = wide // 2
    if whole_rows:
        got = exchange(image_own, "dp").reshape(dp_count, 2, batch, SIDE, 2, half)
        grad_images = got.transpose(0, 2, 1, 3, 4, 5)
    else:
        part = pix_here // 2
        image_own = image_own.reshape(SIDE, 2, batch, SIDE // part, part, wide)
        image_own = image_own.transpose(0, 1, 3, 2, 4, 5).reshape(dp_count, batch, part, wide)
        grad_images = exchange(image_own, "dp")
    grad_images = grad_images.reshape(dp_count * batch, pix_here, half)

    reduced_second, reduced_proj = call(
        reduce_second_body, [shape(w_second.shape), shape(w_proj.shape)], got_second
    )
    reduced_first, pay = call(
        reduce_first_body,
        [shape(w_first.shape), shape((n_all, SIDE, wide))],
        got_first,
        reduced_second,
        reduced_proj,
        w_first,
        w_second,
        w_proj,
        total3,
        total4,
        norm_params,
    )
    got6 = exchange(pay, everyone)

    conv = (
        (w_first, reduced_first, mom_first, avg_first),
        (w_second, reduced_second, mom_second, avg_second),
        (w_proj, reduced_proj, mom_proj, avg_proj),
    )
    results = call(
        make_update_body(dp_count),
        [shape(part[0].shape) for part in conv for _ in range(3)] + [shape(norm_params.shape)] * 3,
        got6,
        total3,
        total4,
        *(array for part in conv for array in part),
        norm_params,
        mom_norm,
        avg_norm,
    )
    return (output, grad_images, *results)


def solution(mesh):
    rows, cols, batch = P("dp", "chan"), P(None, "chan"), P("dp", None, "chan")
    weights = (rows, rows, rows, cols)
    in_specs = (P(None, "dp", None), P("dp", None), batch) + weights * 3
    out_specs = (batch, P(None, "dp", "chan")) + (rows,) * 9 + (cols,) * 3
    return jax.shard_map(
        per_device, mesh=mesh, in_specs=in_specs, out_specs=out_specs, check_vma=False
    )
```

```python
import jax
import jax.numpy as jnp
from jax import lax
from jax.experimental import pallas as pl
from jax.experimental.pallas import tpu as pltpu
from jax.sharding import PartitionSpec as P

BF = jnp.bfloat16
F32 = jnp.float32

epsilon = 1e-05
learn_rate = 0.4
trust_coef = 0.5
momentum = 0.5
avg_decay = 0.6
weight_decay = 5e-05
tiny_term = 1e-06

SIDE = 8
TAIL = 16


class whole:
    def __init__(self, array):
        self.arrays, self.dims, self.dtype = [array], array.shape, array.dtype

    def copies(self):
        return len(self.arrays)

    def plan(self, refs, local):
        return [(refs[0], local)]


class stack(whole):
    def __init__(self, arrays, slot):
        self.arrays, self.dtype = list(arrays), arrays[0].dtype
        self.dims, self.slot = (len(arrays),) + arrays[0].shape, slot

    def plan(self, refs, local):
        return [(ref, local.at[self.slot(k)]) for k, ref in enumerate(refs)]


class pick(whole):
    def __init__(self, array, index):
        self.arrays, self.dtype, self.index = [array], array.dtype, index
        self.dims = array.shape[1:]

    def plan(self, refs, local):
        return [(refs[0].at[self.index()], local)]


class result:
    def __init__(self, dims, dtype=F32):
        self.dims, self.dtype = tuple(dims), dtype
        self.outs = [jax.ShapeDtypeStruct(self.dims, dtype)]

    def copies(self):
        return len(self.outs)

    def plan(self, local, refs):
        return [(local, refs[0])]


class split(result):
    def __init__(self, slots, dims, dtype=F32, part=None):
        self.dims, self.dtype, self.slots = tuple(dims), dtype, slots
        self.outs = [jax.ShapeDtypeStruct(self.dims[1:], dtype) for _ in slots]

    def plan(self, local, refs):
        return [(local.at[slot()], ref) for slot, ref in zip(self.slots, refs)]


class parts_of(result):
    def __init__(self, source, slots, count, dims, dtype):
        self.source, self.slots, self.count, self.dims = source, slots, count, None
        dims = (count,) + tuple(dims[1:])
        self.outs = [jax.ShapeDtypeStruct(dims, dtype) for _ in slots]

    def plan(self, local, refs):
        return [
            (local.at[pl.ds(slot(), self.count)], ref) for slot, ref in zip(self.slots, refs)
        ]


class Taken:
    def __init__(self, local, copies):
        self.local, self.copies, self.waited = local, copies, False

    def ref(self):
        if not self.waited:
            for copy in self.copies:
                copy.wait()
            self.waited = True
        return self.local

    def __getitem__(self, index):
        return self.ref()[index]

    @property
    def shape(self):
        return self.local.shape


class Given:
    def __init__(self, local, copies, source=None):
        self.local, self.copies, self.sent, self.source = local, copies, False, source

    def send(self):
        if not self.sent:
            if self.source is not None:
                self.source.ref()
            for copy in self.copies:
                copy.start()
            self.sent = True

    def __setitem__(self, index, value):
        self.local[index] = value

    @property
    def shape(self):
        return self.local.shape


def call(body, takes, gives, scratch=(), flops=0, limit=40, later=()):
    takes = [t if isinstance(t, whole) else whole(t) for t in takes]
    arrays = [a for t in takes for a in t.arrays]
    outs = [o for g in gives for o in g.outs]
    n_later, n_in, n_out = len(later), len(arrays), len(outs)
    n_copies = sum(t.copies() for t in takes) + sum(g.copies() for g in gives)

    def kernel(*refs):
        refs = refs[n_later:]
        ins, res = list(refs[:n_in]), list(refs[n_in : n_in + n_out])
        local = list(refs[n_in + n_out : -1])
        sems = refs[-1]
        used = 0
        taken, given = [], []
        for t in takes:
            mine, ins = ins[: len(t.arrays)], ins[len(t.arrays) :]
            copies = []
            for a, b in t.plan(mine, local[0]):
                copies.append(pltpu.make_async_copy(a, b, sems.at[used]))
                used += 1
            for copy in copies:
                copy.start()
            taken.append(Taken(local.pop(0), copies))
        for g in gives:
            mine, res = res[: len(g.outs)], res[len(g.outs) :]
            copies = []
            source = taken[g.source] if g.dims is None else None
            place = source.local if source else local.pop(0)
            for a, b in g.plan(place, mine):
                copies.append(pltpu.make_async_copy(a, b, sems.at[used]))
                used += 1
            given.append(Given(place, copies, source))
        body(*taken, *given, *local)
        for t in taken:
            t.ref()
        for g in given:
            g.send()
        for g in given:
            for copy in g.copies:
                copy.wait()

    moved = sum(a.size * a.dtype.itemsize for a in arrays + outs)
    spec = pl.BlockSpec(memory_space=pltpu.HBM)
    values = pl.pallas_call(
        kernel,
        out_shape=[pltpu.HBM(o.shape, o.dtype) for o in outs],
        in_specs=[spec] * (n_later + n_in),
        out_specs=[spec] * n_out,
        scratch_shapes=[pltpu.VMEM(t.dims, t.dtype) for t in takes]
        + [pltpu.VMEM(g.dims, g.dtype) for g in gives if g.dims is not None]
        + [pltpu.VMEM(dims, dtype) for dims, dtype in scratch]
        + [pltpu.SemaphoreType.DMA((n_copies,))],
        compiler_params=pltpu.CompilerParams(vmem_limit_bytes=limit * 2**20),
        cost_estimate=pl.CostEstimate(flops=flops, bytes_accessed=moved, transcendentals=0),
        name=body.__name__,
    )(*(pltpu.with_memory_space_constraint(a, pltpu.HBM) for a in [*later, *arrays]))
    return list(values)


def dot(a, b):
    return jnp.dot(a, b, preferred_element_type=F32)


def dot_nt(a, b):
    return lax.dot_general(a, b, (((1,), (1,)), ((), ())), preferred_element_type=F32)


def dot_tn(a, b):
    return lax.dot_general(a, b, (((0,), (0,)), ((), ())), preferred_element_type=F32)


def shift_col(x, step):
    rows, lanes = x.shape
    grouped = x.reshape(rows // SIDE, SIDE, lanes)
    rolled = pltpu.roll(grouped, step % SIDE, 1)
    col = lax.broadcasted_iota(jnp.int32, grouped.shape, 1)
    edge = 0 if step > 0 else SIDE - 1
    return jnp.where(col == edge, 0.0, rolled).reshape(rows, lanes)


def shift_row(x, step):
    part = x.shape[0] // SIDE
    blank = jnp.zeros((part, x.shape[1]), x.dtype)
    if step > 0:
        return jnp.concatenate([blank, x[:-part]], axis=0)
    return jnp.concatenate([x[part:], blank], axis=0)


def swap_orders(x, batch):
    pieces = [
        x[(b * SIDE + r) * SIDE : (b * SIDE + r + 1) * SIDE] for r in range(SIDE) for b in range(batch)
    ]
    return jnp.concatenate(pieces, axis=0)


def swap_back(x, batch):
    pieces = [
        x[(r * batch + b) * SIDE : (r * batch + b + 1) * SIDE] for b in range(batch) for r in range(SIDE)
    ]
    return jnp.concatenate(pieces, axis=0)


def col_sum(x):
    return jnp.sum(x, axis=0, keepdims=True)


def lane_sum(x):
    return jnp.sum(col_sum(x), axis=1, keepdims=True)


def rows_of(*rows):
    pad = SIDE - len(rows)
    tail = [jnp.zeros((pad, rows[0].shape[1]), F32)] if pad else []
    return jnp.concatenate(list(rows) + tail, axis=0)


def spread_rows(out, rows):
    out[...] = jnp.broadcast_to(rows[None], out.shape)


def mean_inverse(total, squares, count):
    center = total / count
    spread = squares / count - center * center
    return center, lax.rsqrt(spread + epsilon)


def slope(v):
    sigma = jax.nn.sigmoid(v)
    return sigma * (1.0 + v * (1.0 - sigma))


def add_up(pieces):
    total = pieces[0].astype(F32)
    for piece in pieces[1:]:
        total = total + piece.astype(F32)
    return total


def three_rows(values):
    high = values.astype(BF).astype(F32)
    rest = values - high
    middle = rest.astype(BF).astype(F32)
    low = rest - middle
    blank = jnp.zeros((TAIL - 3 * values.shape[0], values.shape[1]), F32)
    return jnp.concatenate([high, middle, low, blank], axis=0).astype(BF)


def one_row(parts, count):
    return parts[:count] + parts[count : 2 * count] + parts[2 * count : 3 * count]


def tail_sums(blocks, count):
    return one_row(jnp.sum(blocks[:, -TAIL:].astype(F32), axis=0), count)


def pixels_of(blocks):
    data = blocks[:, :-TAIL]
    return data.reshape(-1, data.shape[2]).astype(F32)


def expand_mask(inside):
    images, wide = inside.shape
    dims = (images, SIDE, wide)
    lane = lax.broadcasted_iota(jnp.int32, dims, 2)
    col = lax.broadcasted_iota(jnp.int32, dims, 1)
    picked = jnp.where(lane == col, jnp.broadcast_to(inside[:, None, :], dims), 0.0)
    return jnp.broadcast_to(jnp.sum(picked, axis=2, keepdims=True), dims).reshape(-1, wide)


def widen(mask, wide):
    return jnp.concatenate(
        [mask, jnp.zeros((mask.shape[0], wide - mask.shape[1]), mask.dtype)], axis=1
    )


def lane_row(x):
    return col_sum(x * x)


def pack_weights(w, p, mask, w_next, out, out_next, rows):
    depth, wide = p.shape
    w_ref = w.ref()
    inside = widen(mask[...].astype(F32), wide)
    blank = jnp.zeros((TAIL - inside.shape[0], wide), F32)
    pieces = [w_ref[pl.ds(tap, depth, stride=9), :] for tap in range(9)]
    rows_all = jnp.concatenate(pieces + [p[...], inside, blank], axis=0).astype(BF)
    out[...] = rows_all
    out.send()
    depth = out_next.shape[1]
    w_ref = w_next.ref()
    for tap in range(9):
        out_next[tap] = w_ref[pl.ds(tap, depth, stride=9), :].astype(BF)
    out_next.send()
    rows[...] = rows_of(lane_row(w[...]), lane_row(p[...]), lane_row(w_next[...]))


def pack_images(images, mask, even_out, odd_out, part_out, valid_out, scratch):
    count, pix, lanes = images.shape
    wide = valid_out.shape[1]
    half = count * pix // 2
    for k in range(lanes // wide):
        cut = slice(k * wide, (k + 1) * wide)
        scratch[k] = images[:, :, cut].astype(F32).reshape(count * pix, wide)
        for col in range(2):
            taken = scratch[k, pl.ds(col, half, stride=2), :].reshape(count, 2, SIDE, wide)
            odd = taken[:, 1].reshape(half // 2, wide).astype(BF)
            odd_out[col, :, cut] = odd
            part_out[col, :, cut] = odd
            even_out[col, :, cut] = taken[:, 0].reshape(half // 2, wide).astype(BF)
    part_out.send()
    inside = widen(mask[...].astype(F32), wide)
    part = inside.shape[0] * SIDE
    for row in range(SIDE):
        turned = pltpu.roll(inside, (wide - SIDE * row) % wide, 1)
        valid_out[row * part : (row + 1) * part] = expand_mask(turned)


def tap_major(w):
    return w.reshape(-1, 9, w.shape[1]).transpose(1, 0, 2)


def taps_of(w):
    def taps(*which):
        return jnp.concatenate([w[:, t].reshape(-1, w.shape[3]) for t in which], axis=1)

    return taps


def first_taps_of(w):
    depth = (w.shape[1] - TAIL) // 10

    def taps(*which):
        return jnp.concatenate(
            [w[:, t * depth : (t + 1) * depth].reshape(-1, w.shape[2]) for t in which], axis=1
        )

    return taps


def make_conv_first(mask_rides):
    def conv_first(*refs):
        w, x0, x1, xh, n = refs[:5]
        zb_out, zp_out, pay, sums_out, valid_out, w_out = refs[-6:]
        taps = first_taps_of(w)
        wide = w.shape[2]
        y00 = dot(x0[0], taps(4, 9))
        y01 = dot(x0[1], taps(5, 3))
        y10 = dot(x1[0], taps(7))
        y11 = dot(x1[1], taps(8, 6))
        yh0 = dot(xh[0], taps(1))
        yh1 = dot(xh[1], taps(2, 0))
        here = (y00[:, :wide] + y01[:, :wide]) + (y10 + y11[:, :wide]) + (yh0 + yh1[:, :wide])
        z = here + shift_col(y01[:, wide:] + y11[:, wide:] + yh1[:, wide:], 1)
        zp = y00[:, wide:]
        if mask_rides:
            inside = w[:, w.shape[1] - TAIL :].astype(F32)[:, :SIDE].reshape(-1, wide)
            turn = (wide - SIDE * lax.axis_index("dp")) % wide
            valid = expand_mask(pltpu.roll(inside, turn, 1))
        else:
            valid = refs[5][...]
        zb = z.astype(BF)
        vz, vzp = valid * z, valid * zp
        values = [col_sum(vz), col_sum(vz * z), col_sum(valid), n[0:1], n[1:2]]
        rows = three_rows(jnp.concatenate(values, axis=0))
        part = pay.shape[1] - TAIL
        pay[:, :part] = zb.reshape(SIDE, part, wide)
        pay[:, part:] = jnp.broadcast_to(rows[None], (SIDE, TAIL, wide))
        pay.send()
        w_out.send()
        zb_out[...] = zb
        zp_out[...] = zp
        sums_out[...] = rows_of(col_sum(vzp), col_sum(vzp * zp))
        valid_out[...] = valid

    return conv_first


def first_norm(z, rows):
    count = rows[2:3]
    center, inverse = mean_inverse(rows[0:1], rows[1:2], count)
    hat = (z - center) * inverse
    return hat, hat * rows[3:4] + rows[4:5], inverse


def conv_second(got, m, w, zp, sums, h_out, z2_out, pay, tot_out, w_out):
    blocks, wide = got.shape[0], got.shape[3]
    part = pay.shape[1] - TAIL
    pay[:, :part] = zp[...].astype(BF).reshape(SIDE, part, wide)
    valid = m[...]
    hidden = []
    for k in range(blocks):
        block = got[k]
        total = tail_sums(block, 5)
        own = one_row(got[k, 0, part:].astype(F32), 5)
        rows = rows_of(total[0:1], total[1:2], total[2:3], own[3:4], own[4:5])
        tot_out[k] = rows
        _, lin, _ = first_norm(pixels_of(block), rows)
        hidden.append((lin * jax.nn.sigmoid(lin) * valid).astype(BF))
        h_out[:, k * wide : (k + 1) * wide] = hidden[-1]
    hidden = jnp.concatenate(hidden, axis=1)
    taps = taps_of(w)
    moved = []
    for col in range(3):
        y = dot(hidden, taps(col, 3 + col, 6 + col))
        moved.append(
            shift_row(y[:, :wide], 1) + y[:, wide : 2 * wide] + shift_row(y[:, 2 * wide :], -1)
        )
    z2 = moved[1] + shift_col(moved[0], 1) + shift_col(moved[2], -1)
    vz = valid * z2
    rows = jnp.concatenate([col_sum(vz), col_sum(vz * z2), sums[0:1], sums[1:2]], axis=0)
    pay[:, part:] = jnp.broadcast_to(three_rows(rows)[None], (SIDE, TAIL, wide))
    pay.send()
    w_out.send()
    z2_out[...] = z2


def block_output(z2, got, tot1, m, n, cot, out, e_out, pay, tot_out):
    count = tot1[2:3]
    total = tail_sums(got[...], 4)
    tot_out[...] = rows_of(total[0:1], total[1:2], total[2:3], total[3:4])
    center2, inverse2 = mean_inverse(total[0:1], total[1:2], count)
    center_p, inverse_p = mean_inverse(total[2:3], total[3:4], count)
    hat2 = (z2[...] - center2) * inverse2
    hat_p = (pixels_of(got[...]) - center_p) * inverse_p
    summed = hat2 * n[2:3] + n[3:4] + (hat_p * n[4:5] + n[5:6])
    sigma = jax.nn.sigmoid(summed)
    valid = m[...]
    batch, pix, wide = out.shape
    back = swap_orders(cot[...].astype(F32).reshape(batch * pix, wide), batch)
    e = back * valid * (sigma * (1.0 + summed * (1.0 - sigma)))
    part = pay.shape[1] - TAIL
    pay[:, :part] = e.astype(BF).reshape(SIDE, part, wide)
    rows = jnp.concatenate([col_sum(e), col_sum(e * hat2), col_sum(e * hat_p)], axis=0)
    pay[:, part:] = jnp.broadcast_to(three_rows(rows)[None], (SIDE, TAIL, wide))
    pay.send()
    e_out[...] = e
    out[...] = swap_back(summed * sigma * valid, batch).astype(BF).reshape(out.shape)


def grad_outputs(z2, e, got, tot2, tot1, n, m, m_rows, zp, g2_out, gp_out, tot_out):
    count = tot1[2:3]
    center2, inverse2 = mean_inverse(tot2[0:1], tot2[1:2], count)
    center_p, inverse_p = mean_inverse(tot2[2:3], tot2[3:4], count)
    back = tail_sums(got[...], 3)
    tot_out[...] = rows_of(back[0:1], back[1:2], back[2:3])
    hat2 = (z2[...] - center2) * inverse2
    g2 = n[2:3] * inverse2 * (e[...] - m[...] * ((back[0:1] + hat2 * back[1:2]) / count))
    g2_out[...] = g2.astype(BF)
    g2_out.send()
    hat_p = (zp[...] - center_p) * inverse_p
    loss = m_rows[...] * ((back[0:1] + hat_p * back[2:3]) / count)
    gp_out[...] = (n[4:5] * inverse_p * (pixels_of(got[...]) - loss)).astype(BF)


def grad_hidden(w, g2, got, tot1, m, pay):
    blocks, _, wide = g2.shape
    depth = w.shape[1] * w.shape[3]
    moved = []
    for col in range(3):
        y = 0.0
        for k in range(blocks):
            block = w[k]
            taps = [block[:, 3 * row + col].reshape(depth, wide) for row in range(3)]
            y = y + dot_nt(g2[k], jnp.concatenate(taps, axis=0))
        moved.append(
            shift_row(y[:, :depth], -1) + y[:, depth : 2 * depth] + shift_row(y[:, 2 * depth :], 1)
        )
    gh = moved[1] + shift_col(moved[0], -1) + shift_col(moved[2], 1)
    part = pay.shape[1] - TAIL
    pay[:, :part] = gh.astype(BF).reshape(SIDE, part, depth)
    hat, lin, _ = first_norm(pixels_of(got[...]), tot1[...])
    b = gh * (slope(lin) * m[...])
    rows = three_rows(jnp.concatenate([col_sum(b), col_sum(b * hat)], axis=0))
    pay[:, part:] = jnp.broadcast_to(rows[None], (SIDE, TAIL, depth))


def grad_second(h, g2, x, gp, g_out):
    groups, rows, wide = g_out.shape
    share = h.shape[1] // groups
    h, g2 = h[...], g2[...].astype(F32)
    moved = [shift_col(g2, step).astype(BF) if step else g2.astype(BF) for step in (-1, 0, 1)]

    def put(rows, g):
        g_out[:, rows] = g.astype(BF).reshape(groups, -1, wide)

    for tap in range(9):
        step = tap // 3 - 1
        g = shift_row(moved[tap % 3], step) if step else moved[tap % 3]
        put(slice(tap * share, (tap + 1) * share), dot_tn(h, g))
    put(slice(9 * share, rows), dot_tn(x[...], gp[...]))


def grad_first(got, zb, tot1, n, m, x0, x1, xh, gp, g_out, blocks_out, tot_out):
    wide = got.shape[2]
    back, gh = tail_sums(got[...], 2), pixels_of(got[...])
    tot_out[...] = rows_of(back[0:1], back[1:2])
    count, valid = tot1[2:3], m[...]
    hat, lin, inverse = first_norm(zb[...].astype(F32), tot1[...])
    b = gh * (slope(lin) * valid)
    g = n[0:1] * inverse * (b - valid * ((back[0:1] + hat * back[1:2]) / count))
    here = g.astype(BF)
    g_out[0] = here
    g_out[1] = gp[...]
    g_out.send()
    both = jnp.concatenate([here, shift_col(g, -1).astype(BF)], axis=1)
    groups = blocks_out.shape[0]
    share = x0.shape[2] // groups

    def put(tap, grad):
        rows = grad.astype(BF).reshape(groups, share, wide)
        blocks_out[:, tap * share : (tap + 1) * share] = rows

    for x, plain, (right, left) in ((x0, 4, (5, 3)), (x1, 7, (8, 6)), (xh, 1, (2, 0))):
        put(plain, dot_tn(x[0], here))
        pair = dot_tn(x[1], both)
        put(right, pair[:, :wide])
        put(left, pair[:, wide:])


def grad_images(g, w, out, next_out):
    blocks, count = w.shape[0], w.shape[1]
    depth = (w.shape[2] - TAIL) // 10
    half, wide = count * depth, w.shape[3]

    def taps(k, *which):
        return jnp.concatenate(
            [w[k, :, t * depth : (t + 1) * depth].reshape(half, wide) for t in which], axis=0
        )

    plain, moved, proj = 0.0, 0.0, 0.0
    for k in range(blocks):
        plain = plain + dot_nt(g[k, 0], taps(k, 4, 5, 7, 8, 1, 2))
        moved = moved + dot_nt(g[k, 0], taps(k, 3, 3, 6, 6, 0, 0))
        proj = proj + dot_nt(g[k, 1], taps(k, 9, 9))
    lane = lax.broadcasted_iota(jnp.int32, moved.shape, 1) % (2 * half)
    total = plain + jnp.where(lane >= half, shift_col(moved, -1), 0.0)
    next_out[...] = total[:, 4 * half :].astype(BF)
    next_out.send()
    lane = lax.broadcasted_iota(jnp.int32, proj.shape, 1)
    out[0] = total[:, : 2 * half] + jnp.where(lane < half, proj, 0.0)
    out[1] = total[:, 2 * half : 4 * half]


def finish_images(own, come, out, scratch):
    images, pix, half = out.shape
    wide = own.shape[2]
    odd = own[1] + come[...].astype(F32)
    total = [part.reshape(images, 1, SIDE, wide) for part in (own[0], odd)]
    rows = images * pix // 2
    total = jnp.concatenate(total, axis=1).reshape(rows, wide)
    scratch[pl.ds(0, rows, stride=2), :] = total
    scratch[pl.ds(1, rows, stride=2), :] = pltpu.roll(total, half, 1)
    out[...] = scratch[...][:, :half].astype(BF).reshape(out.shape)


def reduce_second(*refs):
    *parts, g_out, gp_out, rows = refs
    total = add_up([part[...] for part in parts])
    depth = g_out.shape[0] // 9
    for tap in range(9):
        g_out.local[pl.ds(tap, depth, stride=9), :] = total[tap * depth : (tap + 1) * depth]
    conv, proj = total[: 9 * depth], total[9 * depth :]
    gp_out[...] = proj
    rows[...] = rows_of(lane_row(conv), lane_row(proj))


def reduce_first(x, sw, sg, t3, t4, n, g_out, pay):
    total = add_up([x[k] for k in range(x.shape[0])])
    depth = g_out.shape[0] // 9
    conv = [sw[0:1], lane_row(total), sw[2:3], sg[0:1], sw[1:2], sg[1:2]]
    nw, gn = n[...], norm_grad(t3, t4)
    blank = jnp.zeros((2, nw.shape[1]), F32)
    cols = [
        jnp.sum(jnp.concatenate(conv + [blank], axis=0), axis=1, keepdims=True),
        jnp.sum(jnp.concatenate([nw * nw, blank], axis=0), axis=1, keepdims=True),
        jnp.sum(jnp.concatenate([gn * gn, blank], axis=0), axis=1, keepdims=True),
    ]
    lane = lax.broadcasted_iota(jnp.int32, pay.shape[1:], 1)
    block = jnp.zeros(pay.shape[1:], F32)
    for place, col in enumerate(cols):
        block = jnp.where(lane == place, col, block)
    spread_rows(pay, block)
    pay.send()
    for tap in range(9):
        g_out.local[pl.ds(tap, depth, stride=9), :] = total[tap * depth : (tap + 1) * depth]


def norm_grad(t3, t4):
    return jnp.concatenate([t4[1:2], t4[0:1], t3[1:2], t3[0:1], t3[2:3], t3[0:1]], axis=0)


def step_of(w, g, m, a, weight_sq, grad_sq):
    weight_len = jnp.sqrt(weight_sq)
    trust = trust_coef * weight_len / (jnp.sqrt(grad_sq) + weight_decay * weight_len + tiny_term)
    step = trust * (g + weight_decay * w)
    m_new = momentum * m + step
    w_new = w - learn_rate * (step + momentum * m_new)
    return w_new, m_new, avg_decay * a + (1.0 - avg_decay) * w_new


def make_update(dp_count):
    def update(*refs):
        r6, t3, t4 = refs[:3]
        ins, outs = refs[3:18], refs[18:]
        total = jnp.sum(r6[...], axis=0)
        for place in range(3):
            w, g, m, a = (ref[...] for ref in ins[4 * place : 4 * place + 4])
            weight_sq = total[2 * place : 2 * place + 1, 0:1]
            grad_sq = total[2 * place + 1 : 2 * place + 2, 0:1]
            for ref, value in zip(outs[3 * place :], step_of(w, g, m, a, weight_sq, grad_sq)):
                ref[...] = value
                ref.send()
        w, m, a = (ref[...] for ref in ins[12:15])
        weight_sq, grad_sq = total[0:6, 1:2] / dp_count, total[0:6, 2:3] / dp_count
        g = norm_grad(t3, t4)
        for ref, value in zip(outs[9:], step_of(w, g, m, a, weight_sq, grad_sq)):
            ref[...] = value

    return update


def exchange(blocks, axes):
    return lax.all_to_all(blocks, axes, 0, 0)


def swap(array, axis, bits):
    return lax.ppermute(array, axis, [(i, i ^ bits) for i in range(lax.axis_size(axis))])


def away(axis, k):
    return lambda: lax.axis_index(axis) ^ k


def plain_parts(values):
    high = lax.reduce_precision(values, 8, 7)
    middle = lax.reduce_precision(values - high, 8, 7)
    low = values - high - middle
    blank = jnp.zeros((TAIL - 3 * values.shape[0], values.shape[1]), F32)
    return jnp.concatenate([high, middle, low, blank], axis=0).astype(BF)


def in_groups(taps, groups):
    return taps.reshape(taps.shape[0], groups, -1, taps.shape[2]).transpose(1, 0, 2, 3)


def regroup(blocks, taps, groups):
    blocks = blocks.reshape(blocks.shape[0], taps, -1, blocks.shape[2]).transpose(1, 0, 2, 3)
    blocks = in_groups(blocks.reshape(taps, -1, blocks.shape[3]), groups)
    return blocks.reshape(groups, -1, blocks.shape[3])


def as_messages(data, values):
    tail = jnp.zeros((data.shape[0], TAIL, data.shape[2]), BF).at[0].set(plain_parts(values))
    return jnp.concatenate([data.astype(BF), tail], axis=1)


def plain_forward(pay):
    part = pay.shape[1] - TAIL
    rows = one_row(pay[0, part:].astype(F32), 5)
    sums = lax.psum(rows[:3], "dp")
    own = as_messages(pay[:, :part], jnp.concatenate([sums, rows[3:]], axis=0))
    return lax.all_gather(own, "chan")


def plain_sums(pay, count):
    part = pay.shape[1] - TAIL
    return as_messages(
        pay[:, :part], lax.psum(one_row(pay[0, part:].astype(F32), count), "dp")
    )


def per_device(
    images, mask, cotangent, w_first, w_second, w_proj, norm_params, mom_first, mom_second,
    mom_proj, mom_norm, avg_first, avg_second, avg_proj, avg_norm,
):
    everyone = ("dp", "chan")
    dp_count, ch_count = lax.axis_size("dp"), lax.axis_size("chan")
    n_all = dp_count * ch_count
    batch = mask.shape[0]
    pix_here, d_in = images.shape[1], images.shape[2]
    wide = w_first.shape[1]
    d_out = wide * ch_count
    part = batch * SIDE
    pix = SIDE * part
    first_here, second_here = d_in // dp_count, d_out // dp_count
    eight = dp_count == SIDE and pix_here == 4 * SIDE
    groups = SIDE
    square_rows = result((SIDE, wide))
    pixel_pair = (2, pix, d_in)

    message = result((SIDE, part + TAIL, wide), BF)
    all_ch = [away("chan", k) for k in range(ch_count)]

    def slot_dp(k):
        return lax.axis_index("dp") ^ k

    def slot_ch(k):
        return lax.axis_index("chan") ^ k

    if eight:
        own, own_second, squares = call(
            pack_weights,
            [w_first, w_proj, mask, w_second],
            [
                result((10 * first_here + TAIL, wide), BF),
                result((9, second_here, wide), BF),
                square_rows,
            ],
        )
        taps_second = whole(lax.all_gather(own_second, "dp"))
        near = [swap(own, "dp", k) for k in (4, 1, 2, 3)]
        even, odd, send, valid = call(
            pack_images,
            [images, mask],
            [
                result(pixel_pair, BF),
                result(pixel_pair, BF),
                split([lambda: lax.axis_index("chan") % 2], pixel_pair, BF),
                result((pix, wide)),
            ],
            scratch=[((d_in // wide, images.shape[0] * pix_here, wide), F32)],
            later=[own],
        )
        come = lax.ppermute(send, "dp", [(i, i + 1) for i in range(dp_count - 1)])
        come, *near = lax.optimization_barrier((come, *near))
        pieces = [own, *near[1:], near[0]] + [swap(near[0], "dp", k) for k in (1, 2, 3)]
        taps_first, masks = stack(pieces, slot_dp), []
        halo = stack([come, swap(come, "chan", 1)], lambda k: (lax.axis_index("chan") % 2) ^ k)
    else:
        inside = mask.reshape(batch, SIDE, SIDE).transpose(1, 0, 2).reshape(pix, 1).astype(F32)
        valid = jnp.broadcast_to(inside, (pix, wide))
        masks = [valid]
        own = jnp.concatenate([tap_major(w_first), w_proj[None]], axis=0).astype(BF)
        own = in_groups(lax.all_gather(own, "dp", axis=1, tiled=True), groups)
        own = own.reshape(groups, 10 * d_in // groups, wide)
        taps_first = whole(jnp.pad(own, ((0, 0), (0, TAIL), (0, 0))))
        squares = jnp.zeros((SIDE, wide), F32).at[0].set(jnp.sum(w_first * w_first, axis=0))
        squares = squares.at[1].set(jnp.sum(w_proj * w_proj, axis=0))
        own = images.reshape(dp_count, batch, pix_here, d_in)
        own = exchange(own, "dp").transpose(1, 0, 2, 3)
        own = own.reshape(batch, SIDE, 2, SIDE, 2, d_in).transpose(2, 4, 1, 0, 3, 5)
        even, odd = own.reshape(2, 2, pix, d_in)
        halo = jnp.pad(odd, ((0, 0), (part, 0), (0, 0)))[:, :pix]

    macs = pix * 9 * wide * d_in
    per_block = groups // ch_count
    block_slots = [lambda k=k: (lax.axis_index("chan") ^ k) * per_block for k in range(ch_count)]
    z_rows, z_proj, pay, sums_proj, valid_rows, *turned_first = call(
        make_conv_first(eight),
        [taps_first, even, odd, halo, norm_params] + masks,
        [
            result((pix, wide), BF),
            result((pix, wide)),
            message,
            square_rows,
            result((pix, wide)),
            parts_of(0, block_slots, per_block, taps_first.dims, BF),
        ],
        flops=2 * macs,
    )
    if eight:
        got1_mine = exchange(pay, "dp")
        far = swap(got1_mine, "chan", 2)
        got1 = stack([got1_mine, swap(got1_mine, "chan", 1), far, swap(far, "chan", 1)], slot_ch)
    else:
        got1 = plain_forward(pay)
        own_second = lax.all_gather(tap_major(w_second).astype(BF), "dp", axis=1, tiled=True)
        taps_second = whole(in_groups(own_second, groups))
        squares = squares.at[2].set(jnp.sum(w_second * w_second, axis=0))

    hidden, z_second, pay, total1, *turned = call(
        conv_second,
        [got1, valid, taps_second, z_proj, sums_proj],
        [
            result((pix, d_out), BF),
            result((pix, wide)),
            message,
            result((ch_count, SIDE, wide)),
            parts_of(2, block_slots, per_block, taps_second.dims, BF),
        ],
        flops=4 * macs,
    )
    turned = turned[:1] + [swap(block, "chan", k) for k, block in enumerate(turned) if k]
    turned_first = turned_first[:1] + [
        swap(block, "chan", k) for k, block in enumerate(turned_first) if k
    ]
    total1_own = pick(total1, away("chan", 0))
    got2 = exchange(pay, "dp") if eight else plain_sums(pay, 4)
    output, e, pay, total2 = call(
        block_output,
        [z_second, got2, total1_own, valid, norm_params, cotangent],
        [result((batch, SIDE * SIDE, wide), BF), result((pix, wide)), message, square_rows],
    )
    got3 = exchange(pay, "dp") if eight else plain_sums(pay, 3)

    g_second_out, g_proj_out, total3 = call(
        grad_outputs,
        [z_second, e, got3, total2, total1_own, norm_params, valid, valid_rows, z_proj],
        [result((pix, wide), BF), result((pix, wide), BF), square_rows],
        later=turned[1:] + turned_first[1:],
    )
    far = swap(g_second_out, "chan", 2)
    g_all = [g_second_out, swap(g_second_out, "chan", 1), far, swap(far, "chan", 1)]

    rows_second = 9 * (d_out // groups) + d_in // groups
    takes = [hidden, g_second_out, pick(even, lambda: 0), g_proj_out]
    (grads,) = call(
        grad_second,
        takes,
        [result((groups, rows_second, wide), BF)],
        flops=4 * macs,
    )
    if eight:
        *g_all, grads = lax.optimization_barrier((*g_all, grads))
        grads = grads.reshape(groups * rows_second, wide)
        for axis_groups in ([[0, 2, 4, 6], [1, 3, 5, 7]], [[0, 1], [2, 3], [4, 5], [6, 7]]):
            grads = lax.psum_scatter(
                grads, "dp", scatter_dimension=0, axis_index_groups=axis_groups, tiled=True
            )
        takes = [grads]
    else:
        cut = 9 * (d_out // groups)
        grads = [regroup(grads[:, :cut], 9, dp_count), regroup(grads[:, cut:], 1, dp_count)]
        grads = jnp.concatenate(grads, axis=1)
        takes = [jnp.sum(exchange(grads, "dp").astype(F32), axis=0)]
    reduced_second, reduced_proj, squares_second = call(
        reduce_second, takes, [result(w_second.shape), result(w_proj.shape), square_rows]
    )

    got1_own = got1_mine if eight else pick(got1, away("chan", 0))
    (pay,) = call(
        grad_hidden,
        [stack(turned, slot_ch), stack(g_all, slot_ch), got1_own, total1_own, valid],
        [message],
        flops=4 * macs,
    )
    got4 = exchange(pay, "dp") if eight else plain_sums(pay, 2)

    g_first_out, grads, total4 = call(
        grad_first,
        [got4, z_rows, total1_own, norm_params, valid_rows, even, odd, halo, g_proj_out],
        [
            result((2, pix, wide), BF),
            result((groups, 9 * (d_in // groups), wide), BF),
            square_rows,
        ],
        flops=2 * macs,
    )
    if not eight:
        grads = regroup(grads, 9, dp_count)
    got_first = exchange(grads, "dp")

    far = swap(g_first_out, "chan", 2)
    g_all = [g_first_out, swap(g_first_out, "chan", 1), far, swap(far, "chan", 1)]
    own, above = call(
        grad_images,
        [stack(g_all, slot_ch), stack(turned_first, slot_ch)],
        [result((2, pix, wide)), result((pix, wide), BF)],
        flops=2 * macs,
    )
    half = wide // 2
    if eight:
        come = lax.ppermute(above, "dp", [(i + 1, i) for i in range(dp_count - 1)])
        (grad_pixels,) = call(
            finish_images,
            [own, come],
            [result((images.shape[0], pix_here, half), BF)],
            scratch=[((images.shape[0] * pix_here, wide), F32)],
        )
    else:
        cols = pix_here // 2
        above = jnp.pad(above, ((0, part), (0, 0)))[part:].astype(F32)
        total = jnp.stack([own[0], own[1] + above]).astype(BF)
        total = total.reshape(2, SIDE, batch, SIDE // cols, cols, wide)
        total = total.transpose(1, 0, 3, 2, 4, 5).reshape(dp_count, batch, cols, wide)
        grad_pixels = exchange(total, "dp").reshape(dp_count * batch, pix_here, half)

    reduced_first, pay = call(
        reduce_first,
        [got_first, squares, squares_second, total3, total4, norm_params],
        [result(w_first.shape), result((n_all, SIDE, wide))],
    )
    got6 = exchange(pay, everyone)

    conv = (
        (w_first, reduced_first, mom_first, avg_first),
        (w_second, reduced_second, mom_second, avg_second),
        (w_proj, reduced_proj, mom_proj, avg_proj),
    )
    results = call(
        make_update(dp_count),
        [got6, total3, total4, *(array for group in conv for array in group)]
        + [norm_params, mom_norm, avg_norm],
        [result(group[0].shape) for group in conv for _ in range(3)]
        + [result(norm_params.shape)] * 3,
    )
    return (output, grad_pixels, *results)


def solution(mesh):
    rows, cols, batch = P("dp", "chan"), P(None, "chan"), P("dp", None, "chan")
    weights = (rows, rows, rows, cols)
    in_specs = (P(None, "dp", None), P("dp", None), batch) + weights * 3
    out_specs = (batch, P(None, "dp", "chan")) + (rows,) * 9 + (cols,) * 3
    return jax.shard_map(
        per_device, mesh=mesh, in_specs=in_specs, out_specs=out_specs, check_vma=False
    )
```

```python
import jax
import jax.numpy as jnp
from jax import lax
from jax.experimental import pallas as pl
from jax.experimental.pallas import tpu as pltpu
from jax.sharding import PartitionSpec as P

BF = jnp.bfloat16
F32 = jnp.float32

epsilon = 1e-05
learn_rate = 0.4
trust_coef = 0.5
momentum = 0.5
avg_decay = 0.6
weight_decay = 5e-05
tiny_term = 1e-06

SIDE = 8
TAIL = 16
RING = [0, 2, 4, 6, 7, 5, 3, 1]


class whole:
    loose = 0

    def __init__(self, array):
        self.arrays, self.dims, self.dtype = [array], array.shape, array.dtype

    def copies(self):
        return len(self.arrays)

    def plan(self, refs, local):
        return [(refs[0], local)]


class fresh(whole):
    loose = 1


class stack(whole):
    def __init__(self, arrays, slot, loose=0):
        self.arrays, self.dtype, self.loose = list(arrays), arrays[0].dtype, loose
        self.dims, self.slot = (len(arrays),) + arrays[0].shape, slot

    def plan(self, refs, local):
        return [(ref, local.at[self.slot(k)]) for k, ref in enumerate(refs)]


class pick(whole):
    def __init__(self, array, index):
        self.arrays, self.dtype, self.index = [array], array.dtype, index
        self.dims = array.shape[1:]

    def plan(self, refs, local):
        return [(refs[0].at[self.index()], local)]


class spread(whole):
    def __init__(self, array, order, first, rows):
        self.arrays, self.dtype, self.order = [array], array.dtype, order
        self.first, self.rows = first, rows
        self.dims = (array.shape[0], rows) + array.shape[2:]

    def copies(self):
        return self.dims[0]

    def plan(self, refs, local):
        cut = pl.ds(self.first, self.rows)
        return [(refs[0].at[k, cut], local.at[place()]) for k, place in enumerate(self.order)]


class result:
    def __init__(self, dims, dtype=F32):
        self.dims, self.dtype = tuple(dims), dtype
        self.outs = [jax.ShapeDtypeStruct(self.dims, dtype)]

    def copies(self):
        return len(self.outs)

    def plan(self, local, refs):
        return [(local, refs[0])]


class split(result):
    def __init__(self, slots, dims, dtype=F32, part=None):
        self.dims, self.dtype, self.slots = tuple(dims), dtype, slots
        self.outs = [jax.ShapeDtypeStruct(self.dims[1:], dtype) for _ in slots]

    def plan(self, local, refs):
        return [(local.at[slot()], ref) for slot, ref in zip(self.slots, refs)]


class parts_of(result):
    dims = None

    def __init__(self, source, slots, count, first, rows, array):
        self.source, self.slots, self.count, self.cut = source, slots, count, pl.ds(first, rows)
        dims = (count, rows) + array.shape[2:]
        self.outs = [jax.ShapeDtypeStruct(dims, array.dtype) for _ in slots]

    def plan(self, local, refs):
        return [
            (local.at[pl.ds(slot(), self.count), self.cut], ref)
            for slot, ref in zip(self.slots, refs)
        ]


class Taken:
    def __init__(self, local, copies):
        self.local, self.copies, self.waited = local, copies, False

    def ref(self):
        if not self.waited:
            for copy in self.copies:
                copy.wait()
            self.waited = True
        return self.local

    def __getitem__(self, index):
        return self.ref()[index]

    @property
    def shape(self):
        return self.local.shape


class Given:
    def __init__(self, local, copies):
        self.local, self.copies, self.sent = local, copies, False

    def send(self):
        if not self.sent:
            for copy in self.copies:
                copy.start()
            self.sent = True

    def __setitem__(self, index, value):
        self.local[index] = value

    @property
    def shape(self):
        return self.local.shape


def call(body, takes, gives, scratch=(), flops=0, limit=40, later=()):
    takes = [t if isinstance(t, whole) else whole(t) for t in takes]
    arrays = [a for t in takes for a in t.arrays]
    pinned = [True] * len(later)
    for t in takes:
        pinned += [True] * (len(t.arrays) - t.loose) + [False] * t.loose
    outs = [o for g in gives for o in g.outs]
    n_later, n_in, n_out = len(later), len(arrays), len(outs)
    n_copies = sum(t.copies() for t in takes) + sum(g.copies() for g in gives)

    def kernel(*refs):
        refs = refs[n_later:]
        ins, res = list(refs[:n_in]), list(refs[n_in : n_in + n_out])
        local = list(refs[n_in + n_out : -1])
        sems = refs[-1]
        used = 0
        taken, given = [], []
        for t in takes:
            mine, ins = ins[: len(t.arrays)], ins[len(t.arrays) :]
            copies = []
            for a, b in t.plan(mine, local[0]):
                copies.append(pltpu.make_async_copy(a, b, sems.at[used]))
                used += 1
            for copy in copies:
                copy.start()
            taken.append(Taken(local.pop(0), copies))
        for g in gives:
            mine, res = res[: len(g.outs)], res[len(g.outs) :]
            copies = []
            place = taken[g.source].local if g.dims is None else local.pop(0)
            for a, b in g.plan(place, mine):
                copies.append(pltpu.make_async_copy(a, b, sems.at[used]))
                used += 1
            given.append(Given(place, copies))
        body(*taken, *given, *local)
        for t in taken:
            t.ref()
        for g in given:
            g.send()
        for g in given:
            for copy in g.copies:
                copy.wait()

    moved = sum(a.size * a.dtype.itemsize for a in arrays + outs)
    spec = pl.BlockSpec(memory_space=pltpu.HBM)
    loose = pl.BlockSpec(memory_space=pl.ANY)
    operands = [
        pltpu.with_memory_space_constraint(a, pltpu.HBM) if pin else a
        for a, pin in zip([*later, *arrays], pinned)
    ]
    values = pl.pallas_call(
        kernel,
        out_shape=[pltpu.HBM(o.shape, o.dtype) for o in outs],
        in_specs=[spec if pin else loose for pin in pinned],
        out_specs=[spec] * n_out,
        scratch_shapes=[pltpu.VMEM(t.dims, t.dtype) for t in takes]
        + [pltpu.VMEM(g.dims, g.dtype) for g in gives if g.dims is not None]
        + [pltpu.VMEM(dims, dtype) for dims, dtype in scratch]
        + [pltpu.SemaphoreType.DMA((n_copies,))],
        compiler_params=pltpu.CompilerParams(vmem_limit_bytes=limit * 2**20),
        cost_estimate=pl.CostEstimate(flops=flops, bytes_accessed=moved, transcendentals=0),
        name=body.__name__,
    )(*operands)
    return list(values)


def dot(a, b):
    return jnp.dot(a, b, preferred_element_type=F32)


def dot_nt(a, b):
    return lax.dot_general(a, b, (((1,), (1,)), ((), ())), preferred_element_type=F32)


def dot_tn(a, b):
    return lax.dot_general(a, b, (((0,), (0,)), ((), ())), preferred_element_type=F32)


def shift_col(x, step):
    rows, lanes = x.shape
    grouped = x.reshape(rows // SIDE, SIDE, lanes)
    rolled = pltpu.roll(grouped, step % SIDE, 1)
    col = lax.broadcasted_iota(jnp.int32, grouped.shape, 1)
    edge = 0 if step > 0 else SIDE - 1
    return jnp.where(col == edge, 0.0, rolled).reshape(rows, lanes)


def shift_row(x, step):
    part = x.shape[0] // SIDE
    blank = jnp.zeros((part, x.shape[1]), x.dtype)
    if step > 0:
        return jnp.concatenate([blank, x[:-part]], axis=0)
    return jnp.concatenate([x[part:], blank], axis=0)


def swap_orders(x, batch):
    pieces = [
        x[(b * SIDE + r) * SIDE : (b * SIDE + r + 1) * SIDE] for r in range(SIDE) for b in range(batch)
    ]
    return jnp.concatenate(pieces, axis=0)


def swap_back(x, batch):
    pieces = [
        x[(r * batch + b) * SIDE : (r * batch + b + 1) * SIDE] for b in range(batch) for r in range(SIDE)
    ]
    return jnp.concatenate(pieces, axis=0)


def col_sum(x):
    return jnp.sum(x, axis=0, keepdims=True)


def lane_sum(x):
    return jnp.sum(col_sum(x), axis=1, keepdims=True)


def rows_of(*rows):
    pad = SIDE - len(rows)
    tail = [jnp.zeros((pad, rows[0].shape[1]), F32)] if pad else []
    return jnp.concatenate(list(rows) + tail, axis=0)


def spread_rows(out, rows):
    out[...] = jnp.broadcast_to(rows[None], out.shape)


def mean_inverse(total, squares, count):
    center = total / count
    spread = squares / count - center * center
    return center, lax.rsqrt(spread + epsilon)


def slope(v):
    sigma = jax.nn.sigmoid(v)
    return sigma * (1.0 + v * (1.0 - sigma))


def add_up(pieces):
    total = pieces[0].astype(F32)
    for piece in pieces[1:]:
        total = total + piece.astype(F32)
    return total


def three_rows(values):
    high = values.astype(BF).astype(F32)
    rest = values - high
    middle = rest.astype(BF).astype(F32)
    low = rest - middle
    blank = jnp.zeros((TAIL - 3 * values.shape[0], values.shape[1]), F32)
    return jnp.concatenate([high, middle, low, blank], axis=0).astype(BF)


def one_row(parts, count):
    return parts[:count] + parts[count : 2 * count] + parts[2 * count : 3 * count]


def tail_sums(blocks, count):
    return one_row(jnp.sum(blocks[:, -TAIL:].astype(F32), axis=0), count)


def pixels_of(blocks):
    data = blocks[:, :-TAIL]
    return data.reshape(-1, data.shape[2]).astype(F32)


def expand_mask(inside):
    images, wide = inside.shape
    dims = (images, SIDE, wide)
    lane = lax.broadcasted_iota(jnp.int32, dims, 2)
    col = lax.broadcasted_iota(jnp.int32, dims, 1)
    picked = jnp.where(lane == col, jnp.broadcast_to(inside[:, None, :], dims), 0.0)
    return jnp.broadcast_to(jnp.sum(picked, axis=2, keepdims=True), dims).reshape(-1, wide)


def widen(mask, wide):
    return jnp.concatenate(
        [mask, jnp.zeros((mask.shape[0], wide - mask.shape[1]), mask.dtype)], axis=1
    )


def lane_row(x):
    return col_sum(x * x)


def pack_weights(w, p, mask, w_next, out, rows):
    depth, wide = p.shape
    w_ref, next_ref = w.ref(), w_next.ref()
    inside = widen(mask[...].astype(F32), wide)
    blank = jnp.zeros((TAIL - inside.shape[0], wide), F32)
    pieces = [w_ref[pl.ds(tap, depth, stride=9), :] for tap in range(9)] + [p[...], inside, blank]
    depth = w_next.shape[0] // 9
    pieces += [next_ref[pl.ds(tap, depth, stride=9), :] for tap in range(9)]
    out[...] = jnp.concatenate(pieces, axis=0).astype(BF)
    out.send()
    rows[...] = rows_of(lane_row(w[...]), lane_row(p[...]), lane_row(w_next[...]))


def pack_images(images, mask, even_out, odd_out, part_out, valid_out, scratch):
    count, pix, lanes = images.shape
    wide = valid_out.shape[1]
    half = count * pix // 2
    for k in range(lanes // wide):
        cut = slice(k * wide, (k + 1) * wide)
        scratch[k] = images[:, :, cut].astype(F32).reshape(count * pix, wide)
        for col in range(2):
            taken = scratch[k, pl.ds(col, half, stride=2), :].reshape(count, 2, SIDE, wide)
            odd = taken[:, 1].reshape(half // 2, wide).astype(BF)
            odd_out[col, :, cut] = odd
            part_out[col * (lanes // wide) + k] = odd
            even_out[col, :, cut] = taken[:, 0].reshape(half // 2, wide).astype(BF)
    part_out.send()
    inside = widen(mask[...].astype(F32), wide)
    part = inside.shape[0] * SIDE
    for row in range(SIDE):
        turned = pltpu.roll(inside, (wide - SIDE * row) % wide, 1)
        valid_out[row * part : (row + 1) * part] = expand_mask(turned)


def tap_major(w):
    return w.reshape(-1, 9, w.shape[1]).transpose(1, 0, 2)


def taps_of(w, depth, first=0):
    def taps(*which):
        starts = [first + t * depth for t in which]
        return jnp.concatenate(
            [w[:, a : a + depth].reshape(-1, w.shape[2]) for a in starts], axis=1
        )

    return taps


def halo_of(blocks):
    half = blocks.shape[0] // 2
    return [
        jnp.concatenate([blocks[col * half + k] for k in range(half)], axis=1) for col in range(2)
    ]


def make_conv_first(mask_rides):
    def conv_first(*refs):
        w, x0, x1, xh, n = refs[:5]
        zb_out, zp_out, pay, sums_out, valid_out = refs[-5:]
        taps = taps_of(w, (w.shape[1] - TAIL) // 10)
        wide = w.shape[2]
        y00 = dot(x0[0], taps(4, 9))
        y01 = dot(x0[1], taps(5, 3))
        y10 = dot(x1[0], taps(7))
        y11 = dot(x1[1], taps(8, 6))
        xh = halo_of(xh)
        yh0 = dot(xh[0], taps(1))
        yh1 = dot(xh[1], taps(2, 0))
        here = (y00[:, :wide] + y01[:, :wide]) + (y10 + y11[:, :wide]) + (yh0 + yh1[:, :wide])
        z = here + shift_col(y01[:, wide:] + y11[:, wide:] + yh1[:, wide:], 1)
        zp = y00[:, wide:]
        if mask_rides:
            inside = w[:, w.shape[1] - TAIL :].astype(F32)[:, :SIDE].reshape(-1, wide)
            turn = (wide - SIDE * lax.axis_index("dp")) % wide
            valid = expand_mask(pltpu.roll(inside, turn, 1))
        else:
            valid = refs[5][...]
        zb = z.astype(BF)
        vz, vzp = valid * z, valid * zp
        values = [col_sum(vz), col_sum(vz * z), col_sum(valid), n[0:1], n[1:2]]
        rows = three_rows(jnp.concatenate(values, axis=0))
        part = pay.shape[1] - TAIL
        pay[:, :part] = zb.reshape(SIDE, part, wide)
        pay[:, part:] = jnp.broadcast_to(rows[None], (SIDE, TAIL, wide))
        pay.send()
        zb_out[...] = zb
        zp_out[...] = zp
        sums_out[...] = rows_of(col_sum(vzp), col_sum(vzp * zp))
        valid_out[...] = valid

    return conv_first


def hand_on(w, *outs):
    w.ref()


def first_norm(z, rows):
    count = rows[2:3]
    center, inverse = mean_inverse(rows[0:1], rows[1:2], count)
    hat = (z - center) * inverse
    return hat, hat * rows[3:4] + rows[4:5], inverse


def conv_second(got, m, w, zp, sums, h_out, z2_out, pay, tot_out):
    blocks, wide = got.shape[0], got.shape[3]
    part = pay.shape[1] - TAIL
    pay[:, :part] = zp[...].astype(BF).reshape(SIDE, part, wide)
    valid = m[...]
    hidden = []
    for k in range(blocks):
        block = got[k]
        total = tail_sums(block, 5)
        own = one_row(got[k, 0, part:].astype(F32), 5)
        rows = rows_of(total[0:1], total[1:2], total[2:3], own[3:4], own[4:5])
        tot_out[k] = rows
        _, lin, _ = first_norm(pixels_of(block), rows)
        hidden.append((lin * jax.nn.sigmoid(lin) * valid).astype(BF))
        h_out[:, k * wide : (k + 1) * wide] = hidden[-1]
    hidden = jnp.concatenate(hidden, axis=1)
    depth = hidden.shape[1] // w.shape[0]
    taps = taps_of(w, depth)
    moved = []
    for col in range(3):
        y = dot(hidden, taps(col, 3 + col, 6 + col))
        moved.append(
            shift_row(y[:, :wide], 1) + y[:, wide : 2 * wide] + shift_row(y[:, 2 * wide :], -1)
        )
    z2 = moved[1] + shift_col(moved[0], 1) + shift_col(moved[2], -1)
    vz = valid * z2
    rows = jnp.concatenate([col_sum(vz), col_sum(vz * z2), sums[0:1], sums[1:2]], axis=0)
    pay[:, part:] = jnp.broadcast_to(three_rows(rows)[None], (SIDE, TAIL, wide))
    pay.send()
    z2_out[...] = z2


def block_output(z2, got, tot1, m, n, cot, out, e_out, pay, tot_out):
    count = tot1[2:3]
    total = tail_sums(got[...], 4)
    tot_out[...] = rows_of(total[0:1], total[1:2], total[2:3], total[3:4])
    center2, inverse2 = mean_inverse(total[0:1], total[1:2], count)
    center_p, inverse_p = mean_inverse(total[2:3], total[3:4], count)
    hat2 = (z2[...] - center2) * inverse2
    hat_p = (pixels_of(got[...]) - center_p) * inverse_p
    summed = hat2 * n[2:3] + n[3:4] + (hat_p * n[4:5] + n[5:6])
    sigma = jax.nn.sigmoid(summed)
    valid = m[...]
    batch, pix, wide = out.shape
    back = swap_orders(cot[...].astype(F32).reshape(batch * pix, wide), batch)
    e = back * valid * (sigma * (1.0 + summed * (1.0 - sigma)))
    part = pay.shape[1] - TAIL
    pay[:, :part] = e.astype(BF).reshape(SIDE, part, wide)
    rows = jnp.concatenate([col_sum(e), col_sum(e * hat2), col_sum(e * hat_p)], axis=0)
    pay[:, part:] = jnp.broadcast_to(three_rows(rows)[None], (SIDE, TAIL, wide))
    pay.send()
    e_out[...] = e
    out[...] = swap_back(summed * sigma * valid, batch).astype(BF).reshape(out.shape)


def grad_outputs(z2, e, got, tot2, tot1, n, m, m_rows, zp, g2_out, gp_out, tot_out):
    count = tot1[2:3]
    center2, inverse2 = mean_inverse(tot2[0:1], tot2[1:2], count)
    center_p, inverse_p = mean_inverse(tot2[2:3], tot2[3:4], count)
    back = tail_sums(got[...], 3)
    tot_out[...] = rows_of(back[0:1], back[1:2], back[2:3])
    hat2 = (z2[...] - center2) * inverse2
    g2 = n[2:3] * inverse2 * (e[...] - m[...] * ((back[0:1] + hat2 * back[1:2]) / count))
    g2_out[...] = g2.astype(BF)
    g2_out.send()
    hat_p = (zp[...] - center_p) * inverse_p
    loss = m_rows[...] * ((back[0:1] + hat_p * back[2:3]) / count)
    gp_out[...] = (n[4:5] * inverse_p * (pixels_of(got[...]) - loss)).astype(BF)


def grad_hidden(w, g2, got, tot1, m, pay):
    blocks, _, wide = g2.shape
    count, part = w.shape[1], w.shape[2] // 9
    depth = count * part
    moved = []
    for col in range(3):
        y = 0.0
        for k in range(blocks):
            starts = [(3 * row + col) * part for row in range(3)]
            taps = [w[k, :, a : a + part].reshape(depth, wide) for a in starts]
            y = y + dot_nt(g2[k], jnp.concatenate(taps, axis=0))
        moved.append(
            shift_row(y[:, :depth], -1) + y[:, depth : 2 * depth] + shift_row(y[:, 2 * depth :], 1)
        )
    gh = moved[1] + shift_col(moved[0], -1) + shift_col(moved[2], 1)
    part = pay.shape[1] - TAIL
    pay[:, :part] = gh.astype(BF).reshape(SIDE, part, depth)
    hat, lin, _ = first_norm(pixels_of(got[...]), tot1[...])
    b = gh * (slope(lin) * m[...])
    rows = three_rows(jnp.concatenate([col_sum(b), col_sum(b * hat)], axis=0))
    pay[:, part:] = jnp.broadcast_to(rows[None], (SIDE, TAIL, depth))


def make_grad_second(on_ring):
    def grad_second(h, g2, x, gp, g_out):
        places = list(range(g_out.shape[0]))
        if on_ring:
            last, turn = len(RING) - 1, turn_round()
            places = [RING.index(k) for k in places]
            places = [p + turn * (last - 2 * p) for p in places]
        grad_second_in(places, h, g2, x, gp, g_out)

    return grad_second


def grad_second_in(places, h, g2, x, gp, g_out):
    groups, rows, wide = g_out.shape
    share = h.shape[1] // groups
    h, g2 = h[...], g2[...].astype(F32)
    moved = [shift_col(g2, step).astype(BF) if step else g2.astype(BF) for step in (-1, 0, 1)]

    def put(rows, g):
        g = g.astype(BF).reshape(groups, -1, wide)
        for k, place in enumerate(places):
            g_out[place, rows] = g[k]

    for tap in range(9):
        step = tap // 3 - 1
        g = shift_row(moved[tap % 3], step) if step else moved[tap % 3]
        put(slice(tap * share, (tap + 1) * share), dot_tn(h, g))
    put(slice(9 * share, rows), dot_tn(x[...], gp[...]))


def grad_first(got, zb, tot1, n, m, x0, x1, xh, gp, g_out, blocks_out, tot_out):
    wide = got.shape[2]
    back, gh = tail_sums(got[...], 2), pixels_of(got[...])
    tot_out[...] = rows_of(back[0:1], back[1:2])
    count, valid = tot1[2:3], m[...]
    hat, lin, inverse = first_norm(zb[...].astype(F32), tot1[...])
    b = gh * (slope(lin) * valid)
    g = n[0:1] * inverse * (b - valid * ((back[0:1] + hat * back[1:2]) / count))
    here = g.astype(BF)
    g_out[0] = here
    g_out[1] = gp[...]
    g_out.send()
    both = jnp.concatenate([here, shift_col(g, -1).astype(BF)], axis=1)
    groups = blocks_out.shape[0]
    share = x0.shape[2] // groups

    def put(tap, grad):
        rows = grad.astype(BF).reshape(groups, share, wide)
        blocks_out[:, tap * share : (tap + 1) * share] = rows

    for x, plain, (right, left) in ((x0, 4, (5, 3)), (x1, 7, (8, 6)), (halo_of(xh), 1, (2, 0))):
        put(plain, dot_tn(x[0], here))
        pair = dot_tn(x[1], both)
        put(right, pair[:, :wide])
        put(left, pair[:, wide:])


def grad_images(g, w, out, next_out):
    blocks, count = w.shape[0], w.shape[1]
    depth = (w.shape[2] - TAIL) // 10
    half, wide = count * depth, w.shape[3]

    def taps(k, *which):
        return jnp.concatenate(
            [w[k, :, t * depth : (t + 1) * depth].reshape(half, wide) for t in which], axis=0
        )

    plain, moved, proj = 0.0, 0.0, 0.0
    for k in range(blocks):
        plain = plain + dot_nt(g[k, 0], taps(k, 4, 5, 7, 8, 1, 2))
        moved = moved + dot_nt(g[k, 0], taps(k, 3, 3, 6, 6, 0, 0))
        proj = proj + dot_nt(g[k, 1], taps(k, 9, 9))
    lane = lax.broadcasted_iota(jnp.int32, moved.shape, 1) % (2 * half)
    total = plain + jnp.where(lane >= half, shift_col(moved, -1), 0.0)
    next_out[...] = total[:, 4 * half :].astype(BF)
    next_out.send()
    lane = lax.broadcasted_iota(jnp.int32, proj.shape, 1)
    out[0] = total[:, : 2 * half] + jnp.where(lane < half, proj, 0.0)
    out[1] = total[:, 2 * half : 4 * half]


def finish_images(own, come, out, scratch):
    images, pix, half = out.shape
    wide = own.shape[2]
    odd = own[1] + come[...].astype(F32)
    total = [part.reshape(images, 1, SIDE, wide) for part in (own[0], odd)]
    rows = images * pix // 2
    total = jnp.concatenate(total, axis=1).reshape(rows, wide)
    scratch[pl.ds(0, rows, stride=2), :] = total
    scratch[pl.ds(1, rows, stride=2), :] = pltpu.roll(total, half, 1)
    out[...] = scratch[...][:, :half].astype(BF).reshape(out.shape)


def put_rows(out, total):
    depth = out.shape[0] // 9
    for tap in range(9):
        out.local[pl.ds(tap, depth, stride=9), :] = total[tap * depth : (tap + 1) * depth]


def reduce_all(second, x, sw, t3, t4, n, g1_out, g2_out, gp_out, pay):
    second = second[...].astype(F32)
    cut = g2_out.shape[0]
    conv, proj = second[:cut], second[cut:]
    parts = [lane_row(conv), lane_row(proj)]
    first = add_up([x[k] for k in range(x.shape[0])])
    rows = [sw[0:1], lane_row(first), sw[2:3], parts[0], sw[1:2], parts[1]]
    nw, gn = n[...], norm_grad(t3, t4)
    blank = jnp.zeros((2, nw.shape[1]), F32)
    cols = [
        jnp.sum(jnp.concatenate(rows + [blank], axis=0), axis=1, keepdims=True),
        jnp.sum(jnp.concatenate([nw * nw, blank], axis=0), axis=1, keepdims=True),
        jnp.sum(jnp.concatenate([gn * gn, blank], axis=0), axis=1, keepdims=True),
    ]
    lane = lax.broadcasted_iota(jnp.int32, pay.shape[1:], 1)
    block = jnp.zeros(pay.shape[1:], F32)
    for place, col in enumerate(cols):
        block = jnp.where(lane == place, col, block)
    spread_rows(pay, block)
    pay.send()
    gp_out[...] = proj
    put_rows(g2_out, conv)
    g2_out.send()
    put_rows(g1_out, first)


def norm_grad(t3, t4):
    return jnp.concatenate([t4[1:2], t4[0:1], t3[1:2], t3[0:1], t3[2:3], t3[0:1]], axis=0)


def step_of(w, g, m, a, weight_sq, grad_sq):
    weight_len = jnp.sqrt(weight_sq)
    trust = trust_coef * weight_len / (jnp.sqrt(grad_sq) + weight_decay * weight_len + tiny_term)
    step = trust * (g + weight_decay * w)
    m_new = momentum * m + step
    w_new = w - learn_rate * (step + momentum * m_new)
    return w_new, m_new, avg_decay * a + (1.0 - avg_decay) * w_new


def make_update(dp_count):
    def update(*refs):
        r6, t3, t4 = refs[:3]
        ins, outs = refs[3:18], refs[18:]
        total = jnp.sum(r6[...], axis=0)
        for place in range(3):
            w, g, m, a = (ref[...] for ref in ins[4 * place : 4 * place + 4])
            weight_sq = total[2 * place : 2 * place + 1, 0:1]
            grad_sq = total[2 * place + 1 : 2 * place + 2, 0:1]
            for ref, value in zip(outs[3 * place :], step_of(w, g, m, a, weight_sq, grad_sq)):
                ref[...] = value
                ref.send()
        w, m, a = (ref[...] for ref in ins[12:15])
        weight_sq, grad_sq = total[0:6, 1:2] / dp_count, total[0:6, 2:3] / dp_count
        g = norm_grad(t3, t4)
        for ref, value in zip(outs[9:], step_of(w, g, m, a, weight_sq, grad_sq)):
            ref[...] = value

    return update


def exchange(blocks, axes):
    groups = [list(range(lax.axis_size(axes)))]
    return lax.all_to_all(blocks, axes, 0, 0, axis_index_groups=groups)


def rings():
    count = lax.axis_size("chan")
    return [[(d ^ (c % 2)) * count + c for d in RING] for c in range(count)]


def turn_round():
    return lax.axis_index("chan") % 2


def swap(array, axis, bits):
    return lax.ppermute(array, axis, [(i, i ^ bits) for i in range(lax.axis_size(axis))])


def away(axis, k):
    return lambda: lax.axis_index(axis) ^ k


def plain_parts(values):
    high = lax.reduce_precision(values, 8, 7)
    middle = lax.reduce_precision(values - high, 8, 7)
    low = values - high - middle
    blank = jnp.zeros((TAIL - 3 * values.shape[0], values.shape[1]), F32)
    return jnp.concatenate([high, middle, low, blank], axis=0).astype(BF)


def in_groups(taps, groups):
    return taps.reshape(taps.shape[0], groups, -1, taps.shape[2]).transpose(1, 0, 2, 3)


def regroup(blocks, taps, groups):
    blocks = blocks.reshape(blocks.shape[0], taps, -1, blocks.shape[2]).transpose(1, 0, 2, 3)
    blocks = in_groups(blocks.reshape(taps, -1, blocks.shape[3]), groups)
    return blocks.reshape(groups, -1, blocks.shape[3])


def as_messages(data, values):
    tail = jnp.zeros((data.shape[0], TAIL, data.shape[2]), BF).at[0].set(plain_parts(values))
    return jnp.concatenate([data.astype(BF), tail], axis=1)


def plain_forward(pay):
    part = pay.shape[1] - TAIL
    rows = one_row(pay[0, part:].astype(F32), 5)
    sums = lax.psum(rows[:3], "dp")
    own = as_messages(pay[:, :part], jnp.concatenate([sums, rows[3:]], axis=0))
    return lax.all_gather(own, "chan")


def plain_sums(pay, count):
    part = pay.shape[1] - TAIL
    return as_messages(
        pay[:, :part], lax.psum(one_row(pay[0, part:].astype(F32), count), "dp")
    )


def per_device(
    images, mask, cotangent, w_first, w_second, w_proj, norm_params, mom_first, mom_second,
    mom_proj, mom_norm, avg_first, avg_second, avg_proj, avg_norm,
):
    everyone = ("dp", "chan")
    dp_count, ch_count = lax.axis_size("dp"), lax.axis_size("chan")
    n_all = dp_count * ch_count
    batch = mask.shape[0]
    pix_here, d_in = images.shape[1], images.shape[2]
    wide = w_first.shape[1]
    d_out = wide * ch_count
    part = batch * SIDE
    pix = SIDE * part
    first_here, second_here = d_in // dp_count, d_out // dp_count
    eight = dp_count == SIDE and pix_here == 4 * SIDE
    groups = SIDE
    square_rows = result((SIDE, wide))
    pixel_pair = (2, pix, d_in)

    message = result((SIDE, part + TAIL, wide), BF)
    all_ch = [away("chan", k) for k in range(ch_count)]

    def slot_dp(k):
        return lax.axis_index("dp") ^ k

    def slot_ch(k):
        return lax.axis_index("chan") ^ k

    first_rows, second_rows = 10 * d_in // groups + TAIL, 9 * d_out // groups
    if eight:
        even, odd, send, valid = call(
            pack_images,
            [images, mask],
            [
                result(pixel_pair, BF),
                result(pixel_pair, BF),
                split([away("chan", 0)], (ch_count, pix, wide), BF),
                result((pix, wide)),
            ],
            scratch=[((d_in // wide, images.shape[0] * pix_here, wide), F32)],
        )
        come = lax.ppermute(send, "dp", [(i, i + 1) for i in range(dp_count - 1)])
        own, squares = call(
            pack_weights,
            [w_first, w_proj, mask, w_second],
            [result((first_rows + second_rows, wide), BF), square_rows],
        )
        gathered = lax.all_gather(own, everyone, axis_index_groups=rings())
        order, masks = [lambda d=d: d ^ turn_round() for d in RING], []
        far = swap(come, "chan", 2)
        halo = stack([come, swap(come, "chan", 1), far, swap(far, "chan", 1)], slot_ch)
    else:
        inside = mask.reshape(batch, SIDE, SIDE).transpose(1, 0, 2).reshape(pix, 1).astype(F32)
        valid = jnp.broadcast_to(inside, (pix, wide))
        masks = [valid]
        own = jnp.concatenate([tap_major(w_first), w_proj[None]], axis=0).astype(BF)
        own = in_groups(lax.all_gather(own, "dp", axis=1, tiled=True), groups)
        own = jnp.pad(own.reshape(groups, -1, wide), ((0, 0), (0, TAIL), (0, 0)))
        next = lax.all_gather(tap_major(w_second).astype(BF), "dp", axis=1, tiled=True)
        next = in_groups(next, groups).reshape(groups, -1, wide)
        gathered = jnp.concatenate([own, next], axis=1)
        order = [lambda g=g: g for g in range(groups)]
        squares = jnp.zeros((SIDE, wide), F32).at[0].set(jnp.sum(w_first * w_first, axis=0))
        squares = squares.at[1].set(jnp.sum(w_proj * w_proj, axis=0))
        squares = squares.at[2].set(jnp.sum(w_second * w_second, axis=0))
        own = images.reshape(dp_count, batch, pix_here, d_in)
        own = exchange(own, "dp").transpose(1, 0, 2, 3)
        own = own.reshape(batch, SIDE, 2, SIDE, 2, d_in).transpose(2, 4, 1, 0, 3, 5)
        even, odd = own.reshape(2, 2, pix, d_in)
        halo = jnp.pad(odd, ((0, 0), (part, 0), (0, 0)))[:, :pix]
        halo = halo.reshape(2, pix, 2, wide).transpose(0, 2, 1, 3).reshape(ch_count, pix, wide)

    macs = pix * 9 * wide * d_in
    per_block = groups // ch_count

    block_slots = [lambda k=k: (lax.axis_index("chan") ^ k) * per_block for k in range(ch_count)]
    z_rows, z_proj, pay, sums_proj, valid_rows = call(
        make_conv_first(eight),
        [spread(gathered, order, 0, first_rows), even, odd, halo, norm_params] + masks,
        [
            result((pix, wide), BF),
            result((pix, wide)),
            message,
            square_rows,
            result((pix, wide)),
        ],
        flops=2 * macs,
    )
    if eight:
        got1_mine = exchange(pay, "dp")
        far = swap(got1_mine, "chan", 2)
        got1 = stack([got1_mine, swap(got1_mine, "chan", 1), far, swap(far, "chan", 1)], slot_ch)
    else:
        got1 = plain_forward(pay)

    hidden, z_second, pay, total1 = call(
        conv_second,
        [got1, valid, spread(gathered, order, first_rows, second_rows), z_proj, sums_proj],
        [
            result((pix, d_out), BF),
            result((pix, wide)),
            message,
            result((ch_count, SIDE, wide)),
        ],
        flops=4 * macs,
    )
    turned = call(
        hand_on,
        [spread(gathered, order, 0, first_rows + second_rows)],
        [
            parts_of(0, block_slots, per_block, 0, first_rows, gathered),
            parts_of(0, block_slots, per_block, first_rows, second_rows, gathered),
        ],
        later=[z_second],
    )
    turned_first, turned = turned[:ch_count], turned[ch_count:]
    turned = turned[:1] + [swap(block, "chan", k) for k, block in enumerate(turned) if k]
    total1_own = pick(total1, away("chan", 0))
    got2 = exchange(pay, "dp") if eight else plain_sums(pay, 4)
    output, e, pay, total2 = call(
        block_output,
        [z_second, fresh(got2), total1_own, valid, norm_params, cotangent],
        [result((batch, SIDE * SIDE, wide), BF), result((pix, wide)), message, square_rows],
    )
    got3 = exchange(pay, "dp") if eight else plain_sums(pay, 3)

    g_second_out, g_proj_out, total3 = call(
        grad_outputs,
        [z_second, e, fresh(got3), total2, total1_own, norm_params, valid, valid_rows, z_proj],
        [result((pix, wide), BF), result((pix, wide), BF), square_rows],
        later=turned[1:],
    )
    rows_second = 9 * (d_out // groups) + d_in // groups
    takes = [hidden, g_second_out, pick(even, lambda: 0), g_proj_out]
    (grads,) = call(
        make_grad_second(eight),
        takes,
        [result((groups, rows_second, wide), BF)],
        flops=4 * macs,
    )
    far = swap(g_second_out, "chan", 2)
    far, grads = lax.optimization_barrier((far, grads))
    g_all = [g_second_out, swap(g_second_out, "chan", 1), far, swap(far, "chan", 1)]
    if eight:
        grads = lax.psum_scatter(
            grads.reshape(groups * rows_second, wide),
            everyone,
            scatter_dimension=0,
            axis_index_groups=rings(),
            tiled=True,
        )
        grads_second = grads
    else:
        cut = 9 * (d_out // groups)
        grads = [regroup(grads[:, :cut], 9, dp_count), regroup(grads[:, cut:], 1, dp_count)]
        grads = jnp.concatenate(grads, axis=1)
        grads_second = jnp.sum(exchange(grads, "dp").astype(F32), axis=0)

    got1_own = got1_mine if eight else pick(got1, away("chan", 0))
    (pay,) = call(
        grad_hidden,
        [
            stack(turned, slot_ch),
            stack(g_all, slot_ch, 3),
            got1_own,
            total1_own,
            valid,
        ],
        [message],
        flops=4 * macs,
    )
    pay, *turned_first = lax.optimization_barrier((pay, *turned_first))
    turned_first = turned_first[:1] + [
        swap(block, "chan", k) for k, block in enumerate(turned_first) if k
    ]
    got4 = exchange(pay, "dp") if eight else plain_sums(pay, 2)

    g_first_out, grads, total4 = call(
        grad_first,
        [fresh(got4), z_rows, total1_own, norm_params, valid_rows, even, odd, halo, g_proj_out],
        [
            result((2, pix, wide), BF),
            result((groups, 9 * (d_in // groups), wide), BF),
            square_rows,
        ],
        flops=2 * macs,
    )
    if not eight:
        grads = regroup(grads, 9, dp_count)
    got_first = exchange(grads, "dp")

    far = swap(g_first_out, "chan", 2)
    g_all = [g_first_out, swap(g_first_out, "chan", 1), far, swap(far, "chan", 1)]
    got_first, *g_all = lax.optimization_barrier((got_first, *g_all))
    reduced_first, reduced_second, reduced_proj, pay = call(
        reduce_all,
        [grads_second, fresh(got_first), squares, total3, total4, norm_params],
        [
            result(w_first.shape),
            result(w_second.shape),
            result(w_proj.shape),
            result((n_all, SIDE, wide)),
        ],
    )
    got6 = exchange(pay, everyone)

    own, above = call(
        grad_images,
        [stack(g_all, slot_ch, 3), stack(turned_first, slot_ch)],
        [result((2, pix, wide)), result((pix, wide), BF)],
        flops=2 * macs,
        later=[pay],
    )
    conv = (
        (w_first, reduced_first, mom_first, avg_first),
        (w_second, reduced_second, mom_second, avg_second),
        (w_proj, reduced_proj, mom_proj, avg_proj),
    )
    results = call(
        make_update(dp_count),
        [fresh(got6), total3, total4, *(array for group in conv for array in group)]
        + [norm_params, mom_norm, avg_norm],
        [result(group[0].shape) for group in conv for _ in range(3)]
        + [result(norm_params.shape)] * 3,
    )
    half = wide // 2
    if eight:
        come = lax.ppermute(above, "dp", [(i + 1, i) for i in range(dp_count - 1)])
        (grad_pixels,) = call(
            finish_images,
            [own, come],
            [result((images.shape[0], pix_here, half), BF)],
            scratch=[((images.shape[0] * pix_here, wide), F32)],
            later=results[:1],
        )
    else:
        cols = pix_here // 2
        below = jnp.pad(above, ((0, part), (0, 0)))[part:].astype(F32)
        total = jnp.stack([own[0], own[1] + below]).astype(BF)
        total = total.reshape(2, SIDE, batch, SIDE // cols, cols, wide)
        total = total.transpose(1, 0, 3, 2, 4, 5).reshape(dp_count, batch, cols, wide)
        grad_pixels = exchange(total, "dp").reshape(dp_count * batch, pix_here, half)

    return (output, grad_pixels, *results)


def solution(mesh):
    rows, cols, batch = P("dp", "chan"), P(None, "chan"), P("dp", None, "chan")
    weights = (rows, rows, rows, cols)
    in_specs = (P(None, "dp", None), P("dp", None), batch) + weights * 3
    out_specs = (batch, P(None, "dp", "chan")) + (rows,) * 9 + (cols,) * 3
    return jax.shard_map(
        per_device, mesh=mesh, in_specs=in_specs, out_specs=out_specs, check_vma=False
    )
```

```python
import jax
import jax.numpy as jnp
from jax import lax
from jax.experimental import pallas as pl
from jax.experimental.pallas import tpu as pltpu
from jax.sharding import PartitionSpec as P

BF = jnp.bfloat16
F32 = jnp.float32

epsilon = 1e-05
learn_rate = 0.4
trust_coef = 0.5
momentum = 0.5
avg_decay = 0.6
weight_decay = 5e-05
tiny_term = 1e-06

SIDE = 8
TAIL = 16
RING = [0, 2, 4, 6, 7, 5, 3, 1]


class whole:
    loose = 0

    def __init__(self, array):
        self.arrays, self.dims, self.dtype = [array], array.shape, array.dtype

    def copies(self):
        return len(self.arrays)

    def plan(self, refs, local):
        return [(refs[0], local)]


class fresh(whole):
    loose = 1


class stack(whole):
    def __init__(self, arrays, slot, loose=0):
        self.arrays, self.dtype, self.loose = list(arrays), arrays[0].dtype, loose
        self.dims, self.slot = (len(arrays),) + arrays[0].shape, slot

    def plan(self, refs, local):
        return [(ref, local.at[self.slot(k)]) for k, ref in enumerate(refs)]


class pick(whole):
    def __init__(self, array, index):
        self.arrays, self.dtype, self.index = [array], array.dtype, index
        self.dims = array.shape[1:]

    def plan(self, refs, local):
        return [(refs[0].at[self.index()], local)]


class spread(whole):
    def __init__(self, array, order, first, rows):
        self.arrays, self.dtype, self.order = [array], array.dtype, order
        self.first, self.rows = first, rows
        self.dims = (array.shape[0], rows) + array.shape[2:]

    def copies(self):
        return self.dims[0]

    def plan(self, refs, local):
        cut = pl.ds(self.first, self.rows)
        return [(refs[0].at[k, cut], local.at[place()]) for k, place in enumerate(self.order)]


class result:
    def __init__(self, dims, dtype=F32):
        self.dims, self.dtype = tuple(dims), dtype
        self.outs = [jax.ShapeDtypeStruct(self.dims, dtype)]

    def copies(self):
        return len(self.outs)

    def plan(self, local, refs):
        return [(local, refs[0])]


class split(result):
    def __init__(self, slots, dims, dtype=F32, part=None):
        self.dims, self.dtype, self.slots = tuple(dims), dtype, slots
        self.outs = [jax.ShapeDtypeStruct(self.dims[1:], dtype) for _ in slots]

    def plan(self, local, refs):
        return [(local.at[slot()], ref) for slot, ref in zip(self.slots, refs)]


class parts_of(result):
    dims = None

    def __init__(self, source, slots, count, first, rows, array):
        self.source, self.slots, self.count, self.cut = source, slots, count, pl.ds(first, rows)
        dims = (count, rows) + array.shape[2:]
        self.outs = [jax.ShapeDtypeStruct(dims, array.dtype) for _ in slots]

    def plan(self, local, refs):
        return [
            (local.at[pl.ds(slot(), self.count), self.cut], ref)
            for slot, ref in zip(self.slots, refs)
        ]


class Taken:
    def __init__(self, local, copies):
        self.local, self.copies, self.waited = local, copies, False

    def ref(self):
        if not self.waited:
            for copy in self.copies:
                copy.wait()
            self.waited = True
        return self.local

    def __getitem__(self, index):
        return self.ref()[index]

    @property
    def shape(self):
        return self.local.shape


class Given:
    def __init__(self, local, copies):
        self.local, self.copies, self.sent = local, copies, False

    def send(self):
        if not self.sent:
            for copy in self.copies:
                copy.start()
            self.sent = True

    def __setitem__(self, index, value):
        self.local[index] = value

    @property
    def shape(self):
        return self.local.shape


def call(body, takes, gives, scratch=(), flops=0, limit=40, later=()):
    takes = [t if isinstance(t, whole) else whole(t) for t in takes]
    arrays = [a for t in takes for a in t.arrays]
    pinned = [True] * len(later)
    for t in takes:
        pinned += [True] * (len(t.arrays) - t.loose) + [False] * t.loose
    outs = [o for g in gives for o in g.outs]
    n_later, n_in, n_out = len(later), len(arrays), len(outs)
    n_copies = sum(t.copies() for t in takes) + sum(g.copies() for g in gives)

    def kernel(*refs):
        refs = refs[n_later:]
        ins, res = list(refs[:n_in]), list(refs[n_in : n_in + n_out])
        local = list(refs[n_in + n_out : -1])
        sems = refs[-1]
        used = 0
        taken, given = [], []
        for t in takes:
            mine, ins = ins[: len(t.arrays)], ins[len(t.arrays) :]
            copies = []
            for a, b in t.plan(mine, local[0]):
                copies.append(pltpu.make_async_copy(a, b, sems.at[used]))
                used += 1
            for copy in copies:
                copy.start()
            taken.append(Taken(local.pop(0), copies))
        for g in gives:
            mine, res = res[: len(g.outs)], res[len(g.outs) :]
            copies = []
            place = taken[g.source].local if g.dims is None else local.pop(0)
            for a, b in g.plan(place, mine):
                copies.append(pltpu.make_async_copy(a, b, sems.at[used]))
                used += 1
            given.append(Given(place, copies))
        body(*taken, *given, *local)
        for t in taken:
            t.ref()
        for g in given:
            g.send()
        for g in given:
            for copy in g.copies:
                copy.wait()

    moved = sum(a.size * a.dtype.itemsize for a in arrays + outs)
    spec = pl.BlockSpec(memory_space=pltpu.HBM)
    loose = pl.BlockSpec(memory_space=pl.ANY)
    operands = [
        pltpu.with_memory_space_constraint(a, pltpu.HBM) if pin else a
        for a, pin in zip([*later, *arrays], pinned)
    ]
    values = pl.pallas_call(
        kernel,
        out_shape=[pltpu.HBM(o.shape, o.dtype) for o in outs],
        in_specs=[spec if pin else loose for pin in pinned],
        out_specs=[spec] * n_out,
        scratch_shapes=[pltpu.VMEM(t.dims, t.dtype) for t in takes]
        + [pltpu.VMEM(g.dims, g.dtype) for g in gives if g.dims is not None]
        + [pltpu.VMEM(dims, dtype) for dims, dtype in scratch]
        + [pltpu.SemaphoreType.DMA((n_copies,))],
        compiler_params=pltpu.CompilerParams(vmem_limit_bytes=limit * 2**20),
        cost_estimate=pl.CostEstimate(flops=flops, bytes_accessed=moved, transcendentals=0),
        name=body.__name__,
    )(*operands)
    return list(values)


def dot(a, b):
    return jnp.dot(a, b, preferred_element_type=F32)


def dot_nt(a, b):
    return lax.dot_general(a, b, (((1,), (1,)), ((), ())), preferred_element_type=F32)


def dot_tn(a, b):
    return lax.dot_general(a, b, (((0,), (0,)), ((), ())), preferred_element_type=F32)


def shift_col(x, step):
    rows, lanes = x.shape
    grouped = x.reshape(rows // SIDE, SIDE, lanes)
    rolled = pltpu.roll(grouped, step % SIDE, 1)
    col = lax.broadcasted_iota(jnp.int32, grouped.shape, 1)
    edge = 0 if step > 0 else SIDE - 1
    return jnp.where(col == edge, 0.0, rolled).reshape(rows, lanes)


def shift_row(x, step):
    part = x.shape[0] // SIDE
    blank = jnp.zeros((part, x.shape[1]), x.dtype)
    if step > 0:
        return jnp.concatenate([blank, x[:-part]], axis=0)
    return jnp.concatenate([x[part:], blank], axis=0)


def swap_orders(x, batch):
    pieces = [
        x[(b * SIDE + r) * SIDE : (b * SIDE + r + 1) * SIDE] for r in range(SIDE) for b in range(batch)
    ]
    return jnp.concatenate(pieces, axis=0)


def swap_back(x, batch):
    pieces = [
        x[(r * batch + b) * SIDE : (r * batch + b + 1) * SIDE] for b in range(batch) for r in range(SIDE)
    ]
    return jnp.concatenate(pieces, axis=0)


def col_sum(x):
    return jnp.sum(x, axis=0, keepdims=True)


def lane_sum(x):
    return jnp.sum(col_sum(x), axis=1, keepdims=True)


def rows_of(*rows):
    pad = SIDE - len(rows)
    tail = [jnp.zeros((pad, rows[0].shape[1]), F32)] if pad else []
    return jnp.concatenate(list(rows) + tail, axis=0)


def spread_rows(out, rows):
    out[...] = jnp.broadcast_to(rows[None], out.shape)


def mean_inverse(total, squares, count):
    center = total / count
    spread = squares / count - center * center
    return center, lax.rsqrt(spread + epsilon)


def slope(v):
    sigma = jax.nn.sigmoid(v)
    return sigma * (1.0 + v * (1.0 - sigma))


def add_up(pieces):
    total = pieces[0].astype(F32)
    for piece in pieces[1:]:
        total = total + piece.astype(F32)
    return total


def three_rows(values):
    high = values.astype(BF).astype(F32)
    rest = values - high
    middle = rest.astype(BF).astype(F32)
    low = rest - middle
    blank = jnp.zeros((TAIL - 3 * values.shape[0], values.shape[1]), F32)
    return jnp.concatenate([high, middle, low, blank], axis=0).astype(BF)


def one_row(parts, count):
    return parts[:count] + parts[count : 2 * count] + parts[2 * count : 3 * count]


def tail_sums(blocks, count):
    return one_row(jnp.sum(blocks[:, -TAIL:].astype(F32), axis=0), count)


def pixels_of(blocks):
    data = blocks[:, :-TAIL]
    return data.reshape(-1, data.shape[2]).astype(F32)


def expand_mask(inside):
    images, wide = inside.shape
    dims = (images, SIDE, wide)
    lane = lax.broadcasted_iota(jnp.int32, dims, 2)
    col = lax.broadcasted_iota(jnp.int32, dims, 1)
    picked = jnp.where(lane == col, jnp.broadcast_to(inside[:, None, :], dims), 0.0)
    return jnp.broadcast_to(jnp.sum(picked, axis=2, keepdims=True), dims).reshape(-1, wide)


def widen(mask, wide):
    return jnp.concatenate(
        [mask, jnp.zeros((mask.shape[0], wide - mask.shape[1]), mask.dtype)], axis=1
    )


def lane_row(x):
    return col_sum(x * x)


def pack_weights(w, p, mask, w_next, out, rows):
    depth, wide = p.shape
    w_ref, next_ref = w.ref(), w_next.ref()
    inside = widen(mask[...].astype(F32), wide)
    blank = jnp.zeros((TAIL - inside.shape[0], wide), F32)
    pieces = [w_ref[pl.ds(tap, depth, stride=9), :] for tap in range(9)] + [p[...], inside, blank]
    depth = w_next.shape[0] // 9
    pieces += [next_ref[pl.ds(tap, depth, stride=9), :] for tap in range(9)]
    out[...] = jnp.concatenate(pieces, axis=0).astype(BF)
    out.send()
    rows[...] = rows_of(lane_row(w[...]), lane_row(p[...]), lane_row(w_next[...]))


def pack_images(images, mask, even_out, odd_out, part_out, valid_out, scratch):
    count, pix, lanes = images.shape
    wide = valid_out.shape[1]
    half = count * pix // 2
    for k in range(lanes // wide):
        cut = slice(k * wide, (k + 1) * wide)
        scratch[k] = images[:, :, cut].astype(F32).reshape(count * pix, wide)
        for col in range(2):
            taken = scratch[k, pl.ds(col, half, stride=2), :].reshape(count, 2, SIDE, wide)
            odd = taken[:, 1].reshape(half // 2, wide).astype(BF)
            odd_out[col, :, cut] = odd
            part_out[col * (lanes // wide) + k] = odd
            even_out[col, :, cut] = taken[:, 0].reshape(half // 2, wide).astype(BF)
    part_out.send()
    inside = widen(mask[...].astype(F32), wide)
    part = inside.shape[0] * SIDE
    for row in range(SIDE):
        turned = pltpu.roll(inside, (wide - SIDE * row) % wide, 1)
        valid_out[row * part : (row + 1) * part] = expand_mask(turned)


def tap_major(w):
    return w.reshape(-1, 9, w.shape[1]).transpose(1, 0, 2)


def taps_of(w, depth, first=0):
    def taps(*which):
        starts = [first + t * depth for t in which]
        return jnp.concatenate(
            [w[:, a : a + depth].reshape(-1, w.shape[2]) for a in starts], axis=1
        )

    return taps


def halo_of(blocks):
    half = blocks.shape[0] // 2
    return [
        jnp.concatenate([blocks[col * half + k] for k in range(half)], axis=1) for col in range(2)
    ]


def make_conv_first(mask_rides):
    def conv_first(*refs):
        w, x0, x1, xh, n = refs[:5]
        zb_out, zp_out, pay, sums_out, valid_out = refs[-5:]
        taps = taps_of(w, (w.shape[1] - TAIL) // 10)
        wide = w.shape[2]
        y00 = dot(x0[0], taps(4, 9))
        y01 = dot(x0[1], taps(5, 3))
        y10 = dot(x1[0], taps(7))
        y11 = dot(x1[1], taps(8, 6))
        xh = halo_of(xh)
        yh0 = dot(xh[0], taps(1))
        yh1 = dot(xh[1], taps(2, 0))
        here = (y00[:, :wide] + y01[:, :wide]) + (y10 + y11[:, :wide]) + (yh0 + yh1[:, :wide])
        z = here + shift_col(y01[:, wide:] + y11[:, wide:] + yh1[:, wide:], 1)
        zp = y00[:, wide:]
        if mask_rides:
            inside = w[:, w.shape[1] - TAIL :].astype(F32)[:, :SIDE].reshape(-1, wide)
            turn = (wide - SIDE * lax.axis_index("dp")) % wide
            valid = expand_mask(pltpu.roll(inside, turn, 1))
        else:
            valid = refs[5][...]
        zb = z.astype(BF)
        vz, vzp = valid * z, valid * zp
        values = [col_sum(vz), col_sum(vz * z), col_sum(valid), n[0:1], n[1:2]]
        rows = three_rows(jnp.concatenate(values, axis=0))
        part = pay.shape[1] - TAIL
        pay[:, :part] = zb.reshape(SIDE, part, wide)
        pay[:, part:] = jnp.broadcast_to(rows[None], (SIDE, TAIL, wide))
        pay.send()
        zb_out[...] = zb
        zp_out[...] = zp
        sums_out[...] = rows_of(col_sum(vzp), col_sum(vzp * zp))
        valid_out[...] = valid

    return conv_first


def hand_on(w, *outs):
    w.ref()


def first_norm(z, rows):
    count = rows[2:3]
    center, inverse = mean_inverse(rows[0:1], rows[1:2], count)
    hat = (z - center) * inverse
    return hat, hat * rows[3:4] + rows[4:5], inverse


def conv_second(got, m, w, zp, sums, h_out, z2_out, pay, tot_out, own_out):
    blocks, wide = got.shape[0], got.shape[3]
    part = pay.shape[1] - TAIL
    pay[:, :part] = zp[...].astype(BF).reshape(SIDE, part, wide)
    valid = m[...]
    hidden = []
    for k in range(blocks):
        block = got[k]
        total = tail_sums(block, 5)
        own = one_row(got[k, 0, part:].astype(F32), 5)
        rows = rows_of(total[0:1], total[1:2], total[2:3], own[3:4], own[4:5])
        tot_out[k] = rows
        _, lin, _ = first_norm(pixels_of(block), rows)
        hidden.append((lin * jax.nn.sigmoid(lin) * valid).astype(BF))
        h_out[:, k * wide : (k + 1) * wide] = hidden[-1]
    hidden = jnp.concatenate(hidden, axis=1)
    depth = hidden.shape[1] // w.shape[0]
    taps = taps_of(w, depth)
    moved = []
    for col in range(3):
        y = dot(hidden, taps(col, 3 + col, 6 + col))
        moved.append(
            shift_row(y[:, :wide], 1) + y[:, wide : 2 * wide] + shift_row(y[:, 2 * wide :], -1)
        )
    z2 = moved[1] + shift_col(moved[0], 1) + shift_col(moved[2], -1)
    vz = valid * z2
    rows = jnp.concatenate([col_sum(vz), col_sum(vz * z2), sums[0:1], sums[1:2]], axis=0)
    pay[:, part:] = jnp.broadcast_to(three_rows(rows)[None], (SIDE, TAIL, wide))
    pay.send()
    z2_out[...] = z2
    own_out[...] = got[pl.ds(lax.axis_index("chan"), 1), :, :part].reshape(own_out.shape)


def block_output(z2, got, tot1, m, n, cot, out, e_out, pay, tot_out):
    count = tot1[2:3]
    total = tail_sums(got[...], 4)
    tot_out[...] = rows_of(total[0:1], total[1:2], total[2:3], total[3:4])
    center2, inverse2 = mean_inverse(total[0:1], total[1:2], count)
    center_p, inverse_p = mean_inverse(total[2:3], total[3:4], count)
    hat2 = (z2[...] - center2) * inverse2
    hat_p = (pixels_of(got[...]) - center_p) * inverse_p
    summed = hat2 * n[2:3] + n[3:4] + (hat_p * n[4:5] + n[5:6])
    sigma = jax.nn.sigmoid(summed)
    valid = m[...]
    batch, pix, wide = out.shape
    back = swap_orders(cot[...].astype(F32).reshape(batch * pix, wide), batch)
    e = back * valid * (sigma * (1.0 + summed * (1.0 - sigma)))
    part = pay.shape[1] - TAIL
    pay[:, :part] = e.astype(BF).reshape(SIDE, part, wide)
    rows = jnp.concatenate([col_sum(e), col_sum(e * hat2), col_sum(e * hat_p)], axis=0)
    pay[:, part:] = jnp.broadcast_to(three_rows(rows)[None], (SIDE, TAIL, wide))
    pay.send()
    e_out[...] = e
    out[...] = swap_back(summed * sigma * valid, batch).astype(BF).reshape(out.shape)


def grad_outputs(z2, e, got, tot2, tot1, n, m, m_rows, zp, g2_out, gp_out, tot_out):
    count = tot1[2:3]
    center2, inverse2 = mean_inverse(tot2[0:1], tot2[1:2], count)
    center_p, inverse_p = mean_inverse(tot2[2:3], tot2[3:4], count)
    back = tail_sums(got[...], 3)
    tot_out[...] = rows_of(back[0:1], back[1:2], back[2:3])
    hat2 = (z2[...] - center2) * inverse2
    g2 = n[2:3] * inverse2 * (e[...] - m[...] * ((back[0:1] + hat2 * back[1:2]) / count))
    g2_out[...] = g2.astype(BF)
    g2_out.send()
    hat_p = (zp[...] - center_p) * inverse_p
    loss = m_rows[...] * ((back[0:1] + hat_p * back[2:3]) / count)
    gp_out[...] = (n[4:5] * inverse_p * (pixels_of(got[...]) - loss)).astype(BF)


def grad_hidden(w, g2, z, tot1, m, pay):
    blocks, _, wide = g2.shape
    count, part = w.shape[1], w.shape[2] // 9
    depth = count * part
    moved = []
    for col in range(3):
        y = 0.0
        for k in range(blocks):
            starts = [(3 * row + col) * part for row in range(3)]
            taps = [w[k, :, a : a + part].reshape(depth, wide) for a in starts]
            y = y + dot_nt(g2[k], jnp.concatenate(taps, axis=0))
        moved.append(
            shift_row(y[:, :depth], -1) + y[:, depth : 2 * depth] + shift_row(y[:, 2 * depth :], 1)
        )
    gh = moved[1] + shift_col(moved[0], -1) + shift_col(moved[2], 1)
    part = pay.shape[1] - TAIL
    pay[:, :part] = gh.astype(BF).reshape(SIDE, part, depth)
    hat, lin, _ = first_norm(z[...].astype(F32), tot1[...])
    b = gh * (slope(lin) * m[...])
    rows = three_rows(jnp.concatenate([col_sum(b), col_sum(b * hat)], axis=0))
    pay[:, part:] = jnp.broadcast_to(rows[None], (SIDE, TAIL, depth))


def make_grad_second(on_ring):
    def grad_second(h, g2, x, gp, g_out):
        places = list(range(g_out.shape[0]))
        if on_ring:
            last, turn = len(RING) - 1, turn_round()
            places = [RING.index(k) for k in places]
            places = [p + turn * (last - 2 * p) for p in places]
        grad_second_in(places, h, g2, x, gp, g_out)

    return grad_second


def grad_second_in(places, h, g2, x, gp, g_out):
    groups, rows, wide = g_out.shape
    share = h.shape[1] // groups
    h, g2 = h[...], g2[...].astype(F32)
    moved = [shift_col(g2, step).astype(BF) if step else g2.astype(BF) for step in (-1, 0, 1)]

    def put(rows, g):
        g = g.astype(BF).reshape(groups, -1, wide)
        for k, place in enumerate(places):
            g_out[place, rows] = g[k]

    for tap in range(9):
        step = tap // 3 - 1
        g = shift_row(moved[tap % 3], step) if step else moved[tap % 3]
        put(slice(tap * share, (tap + 1) * share), dot_tn(h, g))
    put(slice(9 * share, rows), dot_tn(x[...], gp[...]))


def grad_first(got, zb, tot1, n, m, x0, x1, xh, gp, g_out, blocks_out, tot_out):
    wide = got.shape[2]
    back, gh = tail_sums(got[...], 2), pixels_of(got[...])
    tot_out[...] = rows_of(back[0:1], back[1:2])
    count, valid = tot1[2:3], m[...]
    hat, lin, inverse = first_norm(zb[...].astype(F32), tot1[...])
    b = gh * (slope(lin) * valid)
    g = n[0:1] * inverse * (b - valid * ((back[0:1] + hat * back[1:2]) / count))
    here = g.astype(BF)
    g_out[0] = here
    g_out[1] = gp[...]
    g_out.send()
    both = jnp.concatenate([here, shift_col(g, -1).astype(BF)], axis=1)
    groups = blocks_out.shape[0]
    share = x0.shape[2] // groups

    def put(tap, grad):
        rows = grad.astype(BF).reshape(groups, share, wide)
        blocks_out[:, tap * share : (tap + 1) * share] = rows

    for x, plain, (right, left) in ((x0, 4, (5, 3)), (x1, 7, (8, 6)), (halo_of(xh), 1, (2, 0))):
        put(plain, dot_tn(x[0], here))
        pair = dot_tn(x[1], both)
        put(right, pair[:, :wide])
        put(left, pair[:, wide:])


def grad_images(g, w, out, next_out):
    blocks, count = w.shape[0], w.shape[1]
    depth = (w.shape[2] - TAIL) // 10
    half, wide = count * depth, w.shape[3]

    def taps(k, *which):
        return jnp.concatenate(
            [w[k, :, t * depth : (t + 1) * depth].reshape(half, wide) for t in which], axis=0
        )

    plain, moved, proj = 0.0, 0.0, 0.0
    for k in range(blocks):
        plain = plain + dot_nt(g[k, 0], taps(k, 4, 5, 7, 8, 1, 2))
        moved = moved + dot_nt(g[k, 0], taps(k, 3, 3, 6, 6, 0, 0))
        proj = proj + dot_nt(g[k, 1], taps(k, 9, 9))
    lane = lax.broadcasted_iota(jnp.int32, moved.shape, 1) % (2 * half)
    total = plain + jnp.where(lane >= half, shift_col(moved, -1), 0.0)
    next_out[...] = total[:, 4 * half :].astype(BF)
    next_out.send()
    lane = lax.broadcasted_iota(jnp.int32, proj.shape, 1)
    out[0] = total[:, : 2 * half] + jnp.where(lane < half, proj, 0.0)
    out[1] = total[:, 2 * half : 4 * half]


def finish_images(own, come, out, scratch):
    images, pix, half = out.shape
    wide = own.shape[2]
    odd = own[1] + come[...].astype(F32)
    total = [part.reshape(images, 1, SIDE, wide) for part in (own[0], odd)]
    rows = images * pix // 2
    total = jnp.concatenate(total, axis=1).reshape(rows, wide)
    scratch[pl.ds(0, rows, stride=2), :] = total
    scratch[pl.ds(1, rows, stride=2), :] = pltpu.roll(total, half, 1)
    out[...] = scratch[...][:, :half].astype(BF).reshape(out.shape)


def put_rows(out, total):
    depth = out.shape[0] // 9
    for tap in range(9):
        out.local[pl.ds(tap, depth, stride=9), :] = total[tap * depth : (tap + 1) * depth]


def reduce_all(second, x, sw, t3, t4, n, g1_out, g2_out, gp_out, pay):
    second = second[...].astype(F32)
    cut = g2_out.shape[0]
    conv, proj = second[:cut], second[cut:]
    parts = [lane_row(conv), lane_row(proj)]
    first = add_up([x[k] for k in range(x.shape[0])])
    rows = [sw[0:1], lane_row(first), sw[2:3], parts[0], sw[1:2], parts[1]]
    nw, gn = n[...], norm_grad(t3, t4)
    blank = jnp.zeros((2, nw.shape[1]), F32)
    cols = [
        jnp.sum(jnp.concatenate(rows + [blank], axis=0), axis=1, keepdims=True),
        jnp.sum(jnp.concatenate([nw * nw, blank], axis=0), axis=1, keepdims=True),
        jnp.sum(jnp.concatenate([gn * gn, blank], axis=0), axis=1, keepdims=True),
    ]
    lane = lax.broadcasted_iota(jnp.int32, pay.shape[1:], 1)
    block = jnp.zeros(pay.shape[1:], F32)
    for place, col in enumerate(cols):
        block = jnp.where(lane == place, col, block)
    spread_rows(pay, block)
    pay.send()
    gp_out[...] = proj
    put_rows(g2_out, conv)
    g2_out.send()
    put_rows(g1_out, first)


def norm_grad(t3, t4):
    return jnp.concatenate([t4[1:2], t4[0:1], t3[1:2], t3[0:1], t3[2:3], t3[0:1]], axis=0)


def step_of(w, g, m, a, weight_sq, grad_sq):
    weight_len = jnp.sqrt(weight_sq)
    trust = trust_coef * weight_len / (jnp.sqrt(grad_sq) + weight_decay * weight_len + tiny_term)
    step = trust * (g + weight_decay * w)
    m_new = momentum * m + step
    w_new = w - learn_rate * (step + momentum * m_new)
    return w_new, m_new, avg_decay * a + (1.0 - avg_decay) * w_new


def make_update(dp_count):
    def update(*refs):
        r6, t3, t4 = refs[:3]
        ins, outs = refs[3:18], refs[18:]
        total = jnp.sum(r6[...], axis=0)
        for place in range(3):
            w, g, m, a = (ref[...] for ref in ins[4 * place : 4 * place + 4])
            weight_sq = total[2 * place : 2 * place + 1, 0:1]
            grad_sq = total[2 * place + 1 : 2 * place + 2, 0:1]
            for ref, value in zip(outs[3 * place :], step_of(w, g, m, a, weight_sq, grad_sq)):
                ref[...] = value
                ref.send()
        w, m, a = (ref[...] for ref in ins[12:15])
        weight_sq, grad_sq = total[0:6, 1:2] / dp_count, total[0:6, 2:3] / dp_count
        g = norm_grad(t3, t4)
        for ref, value in zip(outs[9:], step_of(w, g, m, a, weight_sq, grad_sq)):
            ref[...] = value

    return update


def exchange(blocks, axes):
    groups = [list(range(lax.axis_size(axes)))]
    return lax.all_to_all(blocks, axes, 0, 0, axis_index_groups=groups)


def rings():
    count = lax.axis_size("chan")
    return [[(d ^ (c % 2)) * count + c for d in RING] for c in range(count)]


def turn_round():
    return lax.axis_index("chan") % 2


def swap(array, axis, bits):
    return lax.ppermute(array, axis, [(i, i ^ bits) for i in range(lax.axis_size(axis))])


def away(axis, k):
    return lambda: lax.axis_index(axis) ^ k


def plain_parts(values):
    high = lax.reduce_precision(values, 8, 7)
    middle = lax.reduce_precision(values - high, 8, 7)
    low = values - high - middle
    blank = jnp.zeros((TAIL - 3 * values.shape[0], values.shape[1]), F32)
    return jnp.concatenate([high, middle, low, blank], axis=0).astype(BF)


def in_groups(taps, groups):
    return taps.reshape(taps.shape[0], groups, -1, taps.shape[2]).transpose(1, 0, 2, 3)


def regroup(blocks, taps, groups):
    blocks = blocks.reshape(blocks.shape[0], taps, -1, blocks.shape[2]).transpose(1, 0, 2, 3)
    blocks = in_groups(blocks.reshape(taps, -1, blocks.shape[3]), groups)
    return blocks.reshape(groups, -1, blocks.shape[3])


def as_messages(data, values):
    tail = jnp.zeros((data.shape[0], TAIL, data.shape[2]), BF).at[0].set(plain_parts(values))
    return jnp.concatenate([data.astype(BF), tail], axis=1)


def plain_forward(pay):
    part = pay.shape[1] - TAIL
    rows = one_row(pay[0, part:].astype(F32), 5)
    sums = lax.psum(rows[:3], "dp")
    own = as_messages(pay[:, :part], jnp.concatenate([sums, rows[3:]], axis=0))
    return lax.all_gather(own, "chan")


def plain_sums(pay, count):
    part = pay.shape[1] - TAIL
    return as_messages(
        pay[:, :part], lax.psum(one_row(pay[0, part:].astype(F32), count), "dp")
    )


def per_device(
    images, mask, cotangent, w_first, w_second, w_proj, norm_params, mom_first, mom_second,
    mom_proj, mom_norm, avg_first, avg_second, avg_proj, avg_norm,
):
    everyone = ("dp", "chan")
    dp_count, ch_count = lax.axis_size("dp"), lax.axis_size("chan")
    n_all = dp_count * ch_count
    batch = mask.shape[0]
    pix_here, d_in = images.shape[1], images.shape[2]
    wide = w_first.shape[1]
    d_out = wide * ch_count
    part = batch * SIDE
    pix = SIDE * part
    first_here, second_here = d_in // dp_count, d_out // dp_count
    eight = dp_count == SIDE and pix_here == 4 * SIDE
    groups = SIDE
    square_rows = result((SIDE, wide))
    pixel_pair = (2, pix, d_in)

    message = result((SIDE, part + TAIL, wide), BF)
    all_ch = [away("chan", k) for k in range(ch_count)]

    def slot_dp(k):
        return lax.axis_index("dp") ^ k

    def slot_ch(k):
        return lax.axis_index("chan") ^ k

    first_rows, second_rows = 10 * d_in // groups + TAIL, 9 * d_out // groups
    if eight:
        even, odd, send, valid = call(
            pack_images,
            [images, mask],
            [
                result(pixel_pair, BF),
                result(pixel_pair, BF),
                split([away("chan", 0)], (ch_count, pix, wide), BF),
                result((pix, wide)),
            ],
            scratch=[((d_in // wide, images.shape[0] * pix_here, wide), F32)],
        )
        come = lax.ppermute(send, "dp", [(i, i + 1) for i in range(dp_count - 1)])
        own, squares = call(
            pack_weights,
            [w_first, w_proj, mask, w_second],
            [result((first_rows + second_rows, wide), BF), square_rows],
        )
        gathered = lax.all_gather(own, everyone, axis_index_groups=rings())
        order, masks = [lambda d=d: d ^ turn_round() for d in RING], []
        far = swap(come, "chan", 2)
        halo = stack([come, swap(come, "chan", 1), far, swap(far, "chan", 1)], slot_ch)
    else:
        inside = mask.reshape(batch, SIDE, SIDE).transpose(1, 0, 2).reshape(pix, 1).astype(F32)
        valid = jnp.broadcast_to(inside, (pix, wide))
        masks = [valid]
        own = jnp.concatenate([tap_major(w_first), w_proj[None]], axis=0).astype(BF)
        own = in_groups(lax.all_gather(own, "dp", axis=1, tiled=True), groups)
        own = jnp.pad(own.reshape(groups, -1, wide), ((0, 0), (0, TAIL), (0, 0)))
        next = lax.all_gather(tap_major(w_second).astype(BF), "dp", axis=1, tiled=True)
        next = in_groups(next, groups).reshape(groups, -1, wide)
        gathered = jnp.concatenate([own, next], axis=1)
        order = [lambda g=g: g for g in range(groups)]
        squares = jnp.zeros((SIDE, wide), F32).at[0].set(jnp.sum(w_first * w_first, axis=0))
        squares = squares.at[1].set(jnp.sum(w_proj * w_proj, axis=0))
        squares = squares.at[2].set(jnp.sum(w_second * w_second, axis=0))
        own = images.reshape(dp_count, batch, pix_here, d_in)
        own = exchange(own, "dp").transpose(1, 0, 2, 3)
        own = own.reshape(batch, SIDE, 2, SIDE, 2, d_in).transpose(2, 4, 1, 0, 3, 5)
        even, odd = own.reshape(2, 2, pix, d_in)
        halo = jnp.pad(odd, ((0, 0), (part, 0), (0, 0)))[:, :pix]
        halo = halo.reshape(2, pix, 2, wide).transpose(0, 2, 1, 3).reshape(ch_count, pix, wide)

    macs = pix * 9 * wide * d_in
    per_block = groups // ch_count

    block_slots = [lambda k=k: (lax.axis_index("chan") ^ k) * per_block for k in range(ch_count)]
    z_rows, z_proj, pay, sums_proj, valid_rows = call(
        make_conv_first(eight),
        [spread(gathered, order, 0, first_rows), even, odd, halo, norm_params] + masks,
        [
            result((pix, wide), BF),
            result((pix, wide)),
            message,
            square_rows,
            result((pix, wide)),
        ],
        flops=2 * macs,
    )
    if eight:
        got1_mine = exchange(pay, "dp")
        far = swap(got1_mine, "chan", 2)
        got1 = [got1_mine, swap(got1_mine, "chan", 1), far, swap(far, "chan", 1)]
        got1 = stack(got1, slot_ch, ch_count)
    else:
        got1 = plain_forward(pay)

    hidden, z_second, pay, total1, z_own = call(
        conv_second,
        [got1, valid, spread(gathered, order, first_rows, second_rows), z_proj, sums_proj],
        [
            result((pix, d_out), BF),
            result((pix, wide)),
            message,
            result((ch_count, SIDE, wide)),
            result((pix, wide), BF),
        ],
        flops=4 * macs,
    )
    turned = call(
        hand_on,
        [spread(gathered, order, 0, first_rows + second_rows)],
        [
            parts_of(0, block_slots, per_block, 0, first_rows, gathered),
            parts_of(0, block_slots, per_block, first_rows, second_rows, gathered),
        ],
        later=[z_second],
    )
    turned_first, turned = turned[:ch_count], turned[ch_count:]
    turned = turned[:1] + [swap(block, "chan", k) for k, block in enumerate(turned) if k]
    total1_own = pick(total1, away("chan", 0))
    got2 = exchange(pay, "dp") if eight else plain_sums(pay, 4)
    output, e, pay, total2 = call(
        block_output,
        [z_second, fresh(got2), total1_own, valid, norm_params, cotangent],
        [result((batch, SIDE * SIDE, wide), BF), result((pix, wide)), message, square_rows],
    )
    got3 = exchange(pay, "dp") if eight else plain_sums(pay, 3)

    g_second_out, g_proj_out, total3 = call(
        grad_outputs,
        [z_second, e, fresh(got3), total2, total1_own, norm_params, valid, valid_rows, z_proj],
        [result((pix, wide), BF), result((pix, wide), BF), square_rows],
        later=turned[1:],
    )
    rows_second = 9 * (d_out // groups) + d_in // groups
    takes = [hidden, g_second_out, pick(even, lambda: 0), g_proj_out]
    (grads,) = call(
        make_grad_second(eight),
        takes,
        [result((groups, rows_second, wide), BF)],
        flops=4 * macs,
    )
    far = swap(g_second_out, "chan", 2)
    far, grads = lax.optimization_barrier((far, grads))
    g_all = [g_second_out, swap(g_second_out, "chan", 1), far, swap(far, "chan", 1)]
    if eight:
        grads = lax.psum_scatter(
            grads.reshape(groups * rows_second, wide),
            everyone,
            scatter_dimension=0,
            axis_index_groups=rings(),
            tiled=True,
        )
        grads_second = grads
    else:
        cut = 9 * (d_out // groups)
        grads = [regroup(grads[:, :cut], 9, dp_count), regroup(grads[:, cut:], 1, dp_count)]
        grads = jnp.concatenate(grads, axis=1)
        grads_second = jnp.sum(exchange(grads, "dp").astype(F32), axis=0)

    (pay,) = call(
        grad_hidden,
        [
            stack(turned, slot_ch),
            stack(g_all, slot_ch, 3),
            z_own,
            total1_own,
            valid,
        ],
        [message],
        flops=4 * macs,
    )
    pay, *turned_first = lax.optimization_barrier((pay, *turned_first))
    turned_first = turned_first[:1] + [
        swap(block, "chan", k) for k, block in enumerate(turned_first) if k
    ]
    got4 = exchange(pay, "dp") if eight else plain_sums(pay, 2)

    g_first_out, grads, total4 = call(
        grad_first,
        [fresh(got4), z_rows, total1_own, norm_params, valid_rows, even, odd, halo, g_proj_out],
        [
            result((2, pix, wide), BF),
            result((groups, 9 * (d_in // groups), wide), BF),
            square_rows,
        ],
        flops=2 * macs,
    )
    if not eight:
        grads = regroup(grads, 9, dp_count)
    got_first = exchange(grads, "dp")

    far = swap(g_first_out, "chan", 2)
    g_all = [g_first_out, swap(g_first_out, "chan", 1), far, swap(far, "chan", 1)]
    got_first, *g_all = lax.optimization_barrier((got_first, *g_all))
    reduced_first, reduced_second, reduced_proj, pay = call(
        reduce_all,
        [grads_second, fresh(got_first), squares, total3, total4, norm_params],
        [
            result(w_first.shape),
            result(w_second.shape),
            result(w_proj.shape),
            result((n_all, SIDE, wide)),
        ],
    )
    got6 = exchange(pay, everyone)

    own, above = call(
        grad_images,
        [stack(g_all, slot_ch, 3), stack(turned_first, slot_ch, 3)],
        [result((2, pix, wide)), result((pix, wide), BF)],
        flops=2 * macs,
        later=[pay],
    )
    conv = (
        (w_first, reduced_first, mom_first, avg_first),
        (w_second, reduced_second, mom_second, avg_second),
        (w_proj, reduced_proj, mom_proj, avg_proj),
    )
    results = call(
        make_update(dp_count),
        [fresh(got6), total3, total4, *(array for group in conv for array in group)]
        + [norm_params, mom_norm, avg_norm],
        [result(group[0].shape) for group in conv for _ in range(3)]
        + [result(norm_params.shape)] * 3,
    )
    half = wide // 2
    if eight:
        come = lax.ppermute(above, "dp", [(i + 1, i) for i in range(dp_count - 1)])
        (grad_pixels,) = call(
            finish_images,
            [own, fresh(come)],
            [result((images.shape[0], pix_here, half), BF)],
            scratch=[((images.shape[0] * pix_here, wide), F32)],
            later=results[:1],
        )
    else:
        cols = pix_here // 2
        below = jnp.pad(above, ((0, part), (0, 0)))[part:].astype(F32)
        total = jnp.stack([own[0], own[1] + below]).astype(BF)
        total = total.reshape(2, SIDE, batch, SIDE // cols, cols, wide)
        total = total.transpose(1, 0, 3, 2, 4, 5).reshape(dp_count, batch, cols, wide)
        grad_pixels = exchange(total, "dp").reshape(dp_count * batch, pix_here, half)

    return (output, grad_pixels, *results)


def solution(mesh):
    rows, cols, batch = P("dp", "chan"), P(None, "chan"), P("dp", None, "chan")
    weights = (rows, rows, rows, cols)
    in_specs = (P(None, "dp", None), P("dp", None), batch) + weights * 3
    out_specs = (batch, P(None, "dp", "chan")) + (rows,) * 9 + (cols,) * 3
    return jax.shard_map(
        per_device, mesh=mesh, in_specs=in_specs, out_specs=out_specs, check_vma=False
    )
```

```python
import jax
import jax.numpy as jnp
from jax import lax
from jax.experimental import pallas as pl
from jax.experimental.pallas import tpu as pltpu
from jax.sharding import PartitionSpec as P

BF = jnp.bfloat16
F32 = jnp.float32

epsilon = 1e-05
learn_rate = 0.4
trust_coef = 0.5
momentum = 0.5
avg_decay = 0.6
weight_decay = 5e-05
tiny_term = 1e-06

SIDE = 8
TAIL = 16
RING = [0, 2, 4, 6, 7, 5, 3, 1]


class whole:
    loose = 0
    direct = False

    def __init__(self, array):
        self.arrays, self.dims, self.dtype = [array], array.shape, array.dtype

    def copies(self):
        return len(self.arrays)

    def plan(self, refs, local):
        return [(refs[0], local)]


class fresh(whole):
    loose = 1
    direct = True

    def copies(self):
        return 0

    def plan(self, refs, local):
        return []


class stack(whole):
    def __init__(self, arrays, slot, loose=0):
        self.arrays, self.dtype, self.loose = list(arrays), arrays[0].dtype, loose
        self.dims, self.slot = (len(arrays),) + arrays[0].shape, slot

    def plan(self, refs, local):
        return [(ref, local.at[self.slot(k)]) for k, ref in enumerate(refs)]


class pick(whole):
    def __init__(self, array, index):
        self.arrays, self.dtype, self.index = [array], array.dtype, index
        self.dims = array.shape[1:]

    def plan(self, refs, local):
        return [(refs[0].at[self.index()], local)]


class spread(whole):
    def __init__(self, array, order, first, rows):
        self.arrays, self.dtype, self.order = [array], array.dtype, order
        self.first, self.rows = first, rows
        self.dims = (array.shape[0], rows) + array.shape[2:]

    def copies(self):
        return self.dims[0]

    def plan(self, refs, local):
        cut = pl.ds(self.first, self.rows)
        return [(refs[0].at[k, cut], local.at[place()]) for k, place in enumerate(self.order)]


class stack_rows(stack):
    def __init__(self, arrays, slot, first, rows, loose=0):
        super().__init__(arrays, slot, loose)
        self.cut = pl.ds(first, rows)
        self.dims = self.dims[:2] + (rows,) + self.dims[3:]

    def plan(self, refs, local):
        return [(ref.at[:, self.cut], local.at[self.slot(k)]) for k, ref in enumerate(refs)]


class quarter(whole):
    def __init__(self, images, groups, count):
        self.arrays, self.dtype = [images], images.dtype
        self.per, self.count = images.shape[0] // groups, count
        self.dims = (groups, count) + images.shape[1:]

    def copies(self):
        return self.dims[0]

    def plan(self, refs, local):
        mine = lax.axis_index("chan") * self.count
        return [
            (refs[0].at[pl.ds(g * self.per + mine, self.count)], local.at[g])
            for g in range(self.dims[0])
        ]


class even_phase(stack):
    def __init__(self, arrays, slot):
        super().__init__(arrays, slot)
        self.lanes = arrays[0].shape[3] // 2
        self.dims = (len(arrays), arrays[0].shape[0], arrays[0].shape[2], self.lanes)

    def plan(self, refs, local):
        lanes = pl.ds(0, self.lanes)
        return [(ref.at[:, 0, :, lanes], local.at[self.slot(k)]) for k, ref in enumerate(refs)]


class result:
    pinned = True

    def __init__(self, dims, dtype=F32, pinned=True):
        self.dims, self.dtype, self.pinned = tuple(dims), dtype, pinned
        self.outs = [jax.ShapeDtypeStruct(self.dims, dtype)]

    def copies(self):
        return len(self.outs)

    def plan(self, local, refs):
        return [(local, refs[0])]


class split(result):
    def __init__(self, slots, dims, dtype=F32, part=None):
        self.dims, self.dtype, self.slots = tuple(dims), dtype, slots
        self.outs = [jax.ShapeDtypeStruct(self.dims[1:], dtype) for _ in slots]

    def plan(self, local, refs):
        return [(local.at[slot()], ref) for slot, ref in zip(self.slots, refs)]


class parts_of(result):
    dims = None

    def __init__(self, source, slots, count, first, rows, array):
        self.source, self.slots, self.count, self.cut = source, slots, count, pl.ds(first, rows)
        dims = (count, rows) + array.shape[2:]
        self.outs = [jax.ShapeDtypeStruct(dims, array.dtype) for _ in slots]

    def plan(self, local, refs):
        return [
            (local.at[pl.ds(slot(), self.count), self.cut], ref)
            for slot, ref in zip(self.slots, refs)
        ]


class Taken:
    def __init__(self, local, copies):
        self.local, self.copies, self.waited = local, copies, False

    def ref(self):
        if not self.waited:
            for copy in self.copies:
                copy.wait()
            self.waited = True
        return self.local

    def __getitem__(self, index):
        return self.ref()[index]

    @property
    def shape(self):
        return self.local.shape


class Given:
    def __init__(self, local, copies):
        self.local, self.copies, self.sent = local, copies, False

    def send(self):
        if not self.sent:
            for copy in self.copies:
                copy.start()
            self.sent = True

    def __setitem__(self, index, value):
        self.local[index] = value

    @property
    def shape(self):
        return self.local.shape


def call(body, takes, gives, scratch=(), flops=0, limit=40, later=()):
    takes = [t if isinstance(t, whole) else whole(t) for t in takes]
    arrays = [a for t in takes for a in t.arrays]
    spec = pl.BlockSpec(memory_space=pltpu.HBM)
    loose, vmem = pl.BlockSpec(memory_space=pl.ANY), pl.BlockSpec(memory_space=pltpu.VMEM)
    pinned = [False] * len(later)
    in_specs = [loose] * len(later)
    for t in takes:
        pinned += [True] * (len(t.arrays) - t.loose) + [False] * t.loose
        in_specs += [spec] * (len(t.arrays) - t.loose) + [vmem if t.direct else loose] * t.loose
    outs = [o for g in gives for o in g.outs]
    n_later, n_in, n_out = len(later), len(arrays), len(outs)
    n_copies = sum(t.copies() for t in takes) + sum(g.copies() for g in gives if g.pinned)

    def kernel(*refs):
        refs = refs[n_later:]
        ins, res = list(refs[:n_in]), list(refs[n_in : n_in + n_out])
        local = list(refs[n_in + n_out : -1])
        sems = refs[-1]
        used = 0
        taken, given = [], []
        for t in takes:
            mine, ins = ins[: len(t.arrays)], ins[len(t.arrays) :]
            place = mine[0] if t.direct else local.pop(0)
            copies = []
            for a, b in t.plan(mine, place):
                copies.append(pltpu.make_async_copy(a, b, sems.at[used]))
                used += 1
            for copy in copies:
                copy.start()
            taken.append(Taken(place, copies))
        for g in gives:
            mine, res = res[: len(g.outs)], res[len(g.outs) :]
            if g.dims is None:
                place = taken[g.source].local
            else:
                place = local.pop(0) if g.pinned else mine[0]
            copies = []
            for a, b in g.plan(place, mine) if g.pinned else ():
                copies.append(pltpu.make_async_copy(a, b, sems.at[used]))
                used += 1
            given.append(Given(place, copies))
        body(*taken, *given, *local)
        for t in taken:
            t.ref()
        for g in given:
            g.send()
        for g in given:
            for copy in g.copies:
                copy.wait()

    moved = sum(a.size * a.dtype.itemsize for a in arrays + outs)
    operands = [
        pltpu.with_memory_space_constraint(a, pltpu.HBM) if pin else a
        for a, pin in zip([*later, *arrays], pinned)
    ]
    values = pl.pallas_call(
        kernel,
        out_shape=[pltpu.HBM(o.shape, o.dtype) if g.pinned else o for g in gives for o in g.outs],
        in_specs=in_specs,
        out_specs=[spec if g.pinned else vmem for g in gives for _ in g.outs],
        scratch_shapes=[pltpu.VMEM(t.dims, t.dtype) for t in takes if not t.direct]
        + [pltpu.VMEM(g.dims, g.dtype) for g in gives if g.dims is not None and g.pinned]
        + [pltpu.VMEM(dims, dtype) for dims, dtype in scratch]
        + [pltpu.SemaphoreType.DMA((n_copies,))],
        compiler_params=pltpu.CompilerParams(vmem_limit_bytes=limit * 2**20),
        cost_estimate=pl.CostEstimate(flops=flops, bytes_accessed=moved, transcendentals=0),
        name=body.__name__,
    )(*operands)
    return list(values)


def dot(a, b):
    return jnp.dot(a, b, preferred_element_type=F32)


def dot_nt(a, b):
    return lax.dot_general(a, b, (((1,), (1,)), ((), ())), preferred_element_type=F32)


def dot_tn(a, b):
    return lax.dot_general(a, b, (((0,), (0,)), ((), ())), preferred_element_type=F32)


def shift_col(x, step):
    rows, lanes = x.shape
    grouped = x.reshape(rows // SIDE, SIDE, lanes)
    rolled = pltpu.roll(grouped, step % SIDE, 1)
    col = lax.broadcasted_iota(jnp.int32, grouped.shape, 1)
    edge = 0 if step > 0 else SIDE - 1
    return jnp.where(col == edge, 0.0, rolled).reshape(rows, lanes)


def shift_row(x, step):
    part = x.shape[0] // SIDE
    blank = jnp.zeros((part, x.shape[1]), x.dtype)
    if step > 0:
        return jnp.concatenate([blank, x[:-part]], axis=0)
    return jnp.concatenate([x[part:], blank], axis=0)


def swap_orders(x, batch):
    pieces = [
        x[(b * SIDE + r) * SIDE : (b * SIDE + r + 1) * SIDE] for r in range(SIDE) for b in range(batch)
    ]
    return jnp.concatenate(pieces, axis=0)


def swap_back(x, batch):
    pieces = [
        x[(r * batch + b) * SIDE : (r * batch + b + 1) * SIDE] for b in range(batch) for r in range(SIDE)
    ]
    return jnp.concatenate(pieces, axis=0)


def col_sum(x):
    return jnp.sum(x, axis=0, keepdims=True)


def lane_sum(x):
    return jnp.sum(col_sum(x), axis=1, keepdims=True)


def rows_of(*rows):
    pad = SIDE - len(rows)
    tail = [jnp.zeros((pad, rows[0].shape[1]), F32)] if pad else []
    return jnp.concatenate(list(rows) + tail, axis=0)


def spread_rows(out, rows):
    out[...] = jnp.broadcast_to(rows[None], out.shape)


def mean_inverse(total, squares, count):
    center = total / count
    spread = squares / count - center * center
    return center, lax.rsqrt(spread + epsilon)


def slope(v):
    sigma = jax.nn.sigmoid(v)
    return sigma * (1.0 + v * (1.0 - sigma))


def three_rows(values):
    high = values.astype(BF).astype(F32)
    rest = values - high
    middle = rest.astype(BF).astype(F32)
    low = rest - middle
    blank = jnp.zeros((TAIL - 3 * values.shape[0], values.shape[1]), F32)
    return jnp.concatenate([high, middle, low, blank], axis=0).astype(BF)


def one_row(parts, count):
    parts = parts.astype(F32)
    return parts[:count] + parts[count : 2 * count] + parts[2 * count : 3 * count]


def add_up(pieces):
    total = pieces[0].astype(F32)
    for piece in pieces[1:]:
        total = total + piece.astype(F32)
    return total


def expand_mask(inside):
    images, wide = inside.shape
    dims = (images, SIDE, wide)
    lane = lax.broadcasted_iota(jnp.int32, dims, 2)
    col = lax.broadcasted_iota(jnp.int32, dims, 1)
    picked = jnp.where(lane == col, jnp.broadcast_to(inside[:, None, :], dims), 0.0)
    return jnp.broadcast_to(jnp.sum(picked, axis=2, keepdims=True), dims).reshape(-1, wide)


def widen(mask, wide):
    return jnp.concatenate(
        [mask, jnp.zeros((mask.shape[0], wide - mask.shape[1]), mask.dtype)], axis=1
    )


def lane_row(x):
    return col_sum(x * x)


def pack_weights(w, p, w_next, out, rows):
    depth = p.shape[0]
    w_ref, next_ref = w.ref(), w_next.ref()
    pieces = [w_ref[pl.ds(tap, depth, stride=9), :] for tap in range(9)] + [p[...]]
    depth = w_next.shape[0] // 9
    pieces += [next_ref[pl.ds(tap, depth, stride=9), :] for tap in range(9)]
    out[...] = jnp.concatenate(pieces, axis=0).astype(BF)
    out.send()
    rows[...] = rows_of(lane_row(w[...]), lane_row(p[...]), lane_row(w_next[...]))


def pack_images(images, mask, out, valid_out, scratch):
    groups, count, pix, lanes = images.shape
    wide = valid_out.shape[1]
    half = groups * count * pix // 2
    for k in range(lanes // wide):
        cut = slice(k * wide, (k + 1) * wide)
        scratch[k] = images[:, :, :, cut].astype(F32).reshape(2 * half, wide)
        for col in range(2):
            taken = scratch[k, pl.ds(col, half, stride=2), :].reshape(groups, count, 2, SIDE, wide)
            for row in range(2):
                rows = jnp.concatenate([taken[:, i, row] for i in range(count)], axis=1)
                start = col * lanes + k * wide
                out[:, row, :, start : start + wide] = rows.astype(BF)
    out.send()
    inside = widen(mask[...].astype(F32), wide)
    part = inside.shape[0] * SIDE
    for row in range(SIDE):
        turned = pltpu.roll(inside, (wide - SIDE * row) % wide, 1)
        valid_out[row * part : (row + 1) * part] = expand_mask(turned)


def tap_major(w):
    return w.reshape(-1, 9, w.shape[1]).transpose(1, 0, 2)


def taps_of(w, depth, first=0):
    def taps(*which):
        starts = [first + t * depth for t in which]
        return jnp.concatenate(
            [w[:, a : a + depth].reshape(-1, w.shape[2]) for a in starts], axis=1
        )

    return taps


def phase_of(x, row, col):
    lanes = x.shape[4] // 2
    cut = slice(col * lanes, (col + 1) * lanes)
    pieces = [x[k, r, row, :, cut] for r in range(x.shape[1]) for k in range(x.shape[0])]
    return jnp.concatenate(pieces, axis=0)


def conv_first(w, x, m, n, zb_out, zp_out, pay):
    taps = taps_of(w, w.shape[1] // 10)
    wide = w.shape[2]
    y00 = dot(phase_of(x, 0, 0), taps(4, 9))
    y01 = dot(phase_of(x, 0, 1), taps(5, 3))
    y10 = dot(phase_of(x, 1, 0), taps(7, 1))
    y11 = dot(phase_of(x, 1, 1), taps(8, 6, 2, 0))
    here = y00[:, :wide] + y01[:, :wide] + y10[:, :wide] + y11[:, :wide]
    left = y01[:, wide:] + y11[:, wide : 2 * wide]
    above = y10[:, wide:] + y11[:, 2 * wide : 3 * wide]
    corner = y11[:, 3 * wide :]
    z = here + shift_row(above, 1) + shift_col(left + shift_row(corner, 1), 1)
    zb_out[...] = z.astype(BF)
    zb_out.send()
    zp = y00[:, wide:]
    valid = m[...]
    vz, vzp = valid * z, valid * zp
    sums = [col_sum(vz), col_sum(vz * z), col_sum(valid), n[0:1], n[1:2]]
    spread_rows(pay, rows_of(*sums, col_sum(vzp), col_sum(vzp * zp)))
    pay.send()
    zp_out[...] = zp


def hand_on(w, *outs):
    w.ref()


def first_norm(z, rows):
    count = rows[2:3]
    center, inverse = mean_inverse(rows[0:1], rows[1:2], count)
    hat = (z - center) * inverse
    return hat, hat * rows[3:4] + rows[4:5], inverse


def conv_second(z, got, m, w, zp, cot, h_out, z2_out, pay, tot_out, m_out, zp_out, cot_out, own_out):
    blocks, wide = z.shape[0], z.shape[2]
    valid = m[...]
    hidden = []
    for k in range(blocks):
        total = jnp.sum(got[:, k], axis=0)
        rows = jnp.concatenate([total[0:3], got[0, k, 3:5], total[5:8]], axis=0)
        tot_out[k] = rows
        _, lin, _ = first_norm(z[k].astype(F32), rows)
        hidden.append((lin * jax.nn.sigmoid(lin) * valid).astype(BF))
        h_out[:, k * wide : (k + 1) * wide] = hidden[-1]
    h_out.send()
    hidden = jnp.concatenate(hidden, axis=1)
    taps = taps_of(w, hidden.shape[1] // w.shape[0])
    moved = []
    for col in range(3):
        y = dot(hidden, taps(col, 3 + col, 6 + col))
        moved.append(
            shift_row(y[:, :wide], 1) + y[:, wide : 2 * wide] + shift_row(y[:, 2 * wide :], -1)
        )
    z2 = moved[1] + shift_col(moved[0], 1) + shift_col(moved[2], -1)
    vz = valid * z2
    spread_rows(pay, rows_of(col_sum(vz), col_sum(vz * z2)))
    pay.send()
    z2_out[...] = z2
    batch, pix, wide = cot.shape
    m_out[...] = valid
    zp_out[...] = zp[...]
    cot_out[...] = swap_orders(cot[...].astype(F32).reshape(batch * pix, wide), batch)
    own_out[...] = tot_out.local[pl.ds(lax.axis_index("chan"), 1)][0]


def block_output(z2, zp, got, tot1, m, n, cot, out, e_out, hat2_out, hat_p_out, rows_out, pay):
    total, count = jnp.sum(got[...], axis=0), tot1[2:3]
    center2, inverse2 = mean_inverse(total[0:1], total[1:2], count)
    center_p, inverse_p = mean_inverse(tot1[5:6], tot1[6:7], count)
    hat2, hat_p = (z2[...] - center2) * inverse2, (zp[...] - center_p) * inverse_p
    hat2_out[...] = hat2
    hat_p_out[...] = hat_p
    rows_out[...] = rows_of(n[2:3] * inverse2, n[4:5] * inverse_p, count)
    summed = hat2 * n[2:3] + n[3:4] + (hat_p * n[4:5] + n[5:6])
    sigma = jax.nn.sigmoid(summed)
    valid = m[...]
    batch, pix, wide = out.shape
    e = cot[...] * valid * (sigma * (1.0 + summed * (1.0 - sigma)))
    spread_rows(pay, rows_of(col_sum(e), col_sum(e * hat2), col_sum(e * hat_p)))
    pay.send()
    e_out[...] = e
    out[...] = swap_back(summed * sigma * valid, batch).astype(BF).reshape(out.shape)


def grad_outputs(e, hat2, hat_p, rows, got, m, g2_out, gp_out, tot_out):
    back, count = jnp.sum(got[...], axis=0), rows[2:3]
    tot_out[...] = back
    valid, e = m[...], e[...]
    loss = valid * ((back[0:1] + hat2[...] * back[1:2]) / count)
    g2_out[...] = (rows[0:1] * (e - loss)).astype(BF)
    g2_out.send()
    loss = valid * ((back[0:1] + hat_p[...] * back[2:3]) / count)
    gp_out[...] = (rows[1:2] * (e - loss)).astype(BF)


def grad_hidden(w, g2, z, gp, tot1, m, b_out, msg, pay):
    blocks, _, wide = g2.shape
    count, part = w.shape[1], w.shape[2] // 9
    depth = count * part
    moved = []
    for col in range(3):
        y = 0.0
        for k in range(blocks):
            starts = [(3 * row + col) * part for row in range(3)]
            taps = [w[k, :, a : a + part].reshape(depth, wide) for a in starts]
            y = y + dot_nt(g2[k], jnp.concatenate(taps, axis=0))
        moved.append(
            shift_row(y[:, :depth], -1) + y[:, depth : 2 * depth] + shift_row(y[:, 2 * depth :], 1)
        )
    gh = moved[1] + shift_col(moved[0], -1) + shift_col(moved[2], 1)
    hat, lin, _ = first_norm(z[...].astype(F32), tot1[...])
    valid = m[...]
    b = gh * (slope(lin) * valid)
    shift, scaled = col_sum(b), col_sum(b * hat)
    spread_rows(pay, rows_of(shift, scaled))
    pay.send()
    here = col_sum(valid)
    shift, scaled = shift / here, scaled / here
    pix = b.shape[0]
    msg[:pix] = (b - valid * (shift + hat * scaled)).astype(BF)
    msg[pix : 2 * pix] = gp[...]
    msg[2 * pix :] = three_rows(jnp.concatenate([shift, scaled], axis=0))
    msg.send()
    b_out[...] = b


def make_grad_second(on_ring):
    def grad_second(h, g2, x, gp, g_out):
        groups, rows, wide = g_out.shape
        places = list(range(groups))
        if on_ring:
            last, turn = len(RING) - 1, turn_round()
            places = [RING.index(k) for k in places]
            places = [p + turn * (last - 2 * p) for p in places]
        share = h.shape[1] // groups
        h, g2 = h[...], g2[...].astype(F32)
        moved = [shift_col(g2, step).astype(BF) if step else g2.astype(BF) for step in (-1, 0, 1)]

        def put(rows, g):
            g = g.astype(BF).reshape(groups, -1, wide)
            for k, place in enumerate(places):
                g_out[place, rows] = g[k]

        for tap in range(9):
            step = tap // 3 - 1
            g = shift_row(moved[tap % 3], step) if step else moved[tap % 3]
            put(slice(tap * share, (tap + 1) * share), dot_tn(h, g))
        pieces = [x[k, r] for r in range(SIDE) for k in range(x.shape[0])]
        put(slice(9 * share, rows), dot_tn(jnp.concatenate(pieces, axis=0), gp[...]))

    return grad_second


def grad_first(b, z, got, tot1, n, m, x, blocks_out, tot_out):
    own = got[:, pl.ds(lax.axis_index("chan"), 1)]
    back, count = jnp.sum(own, axis=0)[0], tot1[2:3]
    tot_out[...] = back
    hat, _, inverse = first_norm(z[...].astype(F32), tot1[...])
    g = n[0:1] * inverse * (b[...] - m[...] * ((back[0:1] + hat * back[1:2]) / count))
    here, left = g.astype(BF), shift_col(g, -1).astype(BF)
    wide = here.shape[1]
    groups = blocks_out.shape[0]
    share = x.shape[4] // 2 // groups

    def put(tap, grad):
        rows = grad.astype(BF).reshape(groups, share, wide)
        blocks_out[:, tap * share : (tap + 1) * share] = rows

    above, corner = shift_row(here, -1), shift_row(left, -1)
    for row, col, pairs in (
        (0, 0, ((4, here),)),
        (0, 1, ((5, here), (3, left))),
        (1, 0, ((7, here), (1, above))),
        (1, 1, ((8, here), (6, left), (2, above), (0, corner))),
    ):
        both = jnp.concatenate([grad for _, grad in pairs], axis=1)
        both = dot_tn(phase_of(x, row, col), both)
        for place, (tap, _) in enumerate(pairs):
            put(tap, both[:, place * wide : (place + 1) * wide])


def grad_images(msg, z, got, tot1, m, w, out):
    blocks, count = w.shape[0], w.shape[1]
    depth = w.shape[2] // 10
    half, wide = count * depth, w.shape[3]

    def taps(k, *which):
        return jnp.concatenate(
            [w[k, :, t * depth : (t + 1) * depth].reshape(half, wide) for t in which], axis=0
        )

    plain, moved, proj = 0.0, 0.0, 0.0
    valid = m[...]
    pix = valid.shape[0]
    for k in range(blocks):
        rows, back = tot1[k], jnp.sum(got[:, k], axis=0)
        hat, _, inverse = first_norm(z[k].astype(F32), rows)
        fit = back[0:2] / rows[2:3] - one_row(msg[k, 2 * pix :], 2)
        loss = valid * (fit[0:1] + hat * fit[1:2])
        g = (rows[3:4] * inverse * (msg[k, :pix].astype(F32) - loss)).astype(BF)
        plain = plain + dot_nt(g, taps(k, 4, 5, 7, 8, 1, 2))
        moved = moved + dot_nt(g, taps(k, 3, 3, 6, 6, 0, 0))
        proj = proj + dot_nt(msg[k, pix : 2 * pix], taps(k, 9, 9))
    lane = lax.broadcasted_iota(jnp.int32, moved.shape, 1) % (2 * half)
    total = plain + jnp.where(lane >= half, shift_col(moved, -1), 0.0)
    lane = lax.broadcasted_iota(jnp.int32, proj.shape, 1)
    even = total[:, : 2 * half] + jnp.where(lane < half, proj, 0.0)
    odd = total[:, 2 * half : 4 * half] + shift_row(total[:, 4 * half :], -1)
    for row, value in enumerate((even, odd)):
        out[:, row] = value.astype(BF).reshape(out.shape[0], -1, 2 * half)


def finish_images(x, out, scratch):
    images, pix, half = out.shape
    groups, _, part, wide = x.shape
    count = part // SIDE
    value = x[...].astype(F32).reshape(groups, 2, count, 1, SIDE, wide)
    value = jnp.concatenate([value[:, 0], value[:, 1]], axis=2)
    rows = images * pix // 2
    value = value.reshape(rows, wide)
    scratch[pl.ds(0, rows, stride=2), :] = value
    scratch[pl.ds(1, rows, stride=2), :] = pltpu.roll(value, half, 1)
    out[...] = scratch[...][:, :half].astype(BF).reshape(out.shape)


def put_rows(out, total):
    depth = out.shape[0] // 9
    for tap in range(9):
        out.local[pl.ds(tap, depth, stride=9), :] = total[tap * depth : (tap + 1) * depth]


def reduce_all(second, x, sw, t3, t4, n, g1_out, g2_out, gp_out, pay):
    second = second[...].astype(F32)
    cut = g2_out.shape[0]
    conv, proj = second[:cut], second[cut:]
    parts = [lane_row(conv), lane_row(proj)]
    first = add_up([x[k] for k in range(x.shape[0])])
    rows = [sw[0:1], lane_row(first), sw[2:3], parts[0], sw[1:2], parts[1]]
    nw, gn = n[...], norm_grad(t3, t4)
    blank = jnp.zeros((2, nw.shape[1]), F32)
    cols = [
        jnp.sum(jnp.concatenate(rows + [blank], axis=0), axis=1, keepdims=True),
        jnp.sum(jnp.concatenate([nw * nw, blank], axis=0), axis=1, keepdims=True),
        jnp.sum(jnp.concatenate([gn * gn, blank], axis=0), axis=1, keepdims=True),
    ]
    lane = lax.broadcasted_iota(jnp.int32, pay.shape[1:], 1)
    block = jnp.zeros(pay.shape[1:], F32)
    for place, col in enumerate(cols):
        block = jnp.where(lane == place, col, block)
    spread_rows(pay, block)
    pay.send()
    gp_out[...] = proj
    put_rows(g2_out, conv)
    g2_out.send()
    put_rows(g1_out, first)


def norm_grad(t3, t4):
    return jnp.concatenate([t4[1:2], t4[0:1], t3[1:2], t3[0:1], t3[2:3], t3[0:1]], axis=0)


def step_of(w, g, m, a, weight_sq, grad_sq):
    weight_len = jnp.sqrt(weight_sq)
    trust = trust_coef * weight_len / (jnp.sqrt(grad_sq) + weight_decay * weight_len + tiny_term)
    step = trust * (g + weight_decay * w)
    m_new = momentum * m + step
    w_new = w - learn_rate * (step + momentum * m_new)
    return w_new, m_new, avg_decay * a + (1.0 - avg_decay) * w_new


def make_update(dp_count):
    def update(*refs):
        r6, t3, t4 = refs[:3]
        ins, outs = refs[3:18], refs[18:]
        total = jnp.sum(r6[...], axis=0)
        for place in range(3):
            w, g, m, a = (ref[...] for ref in ins[4 * place : 4 * place + 4])
            weight_sq = total[2 * place : 2 * place + 1, 0:1]
            grad_sq = total[2 * place + 1 : 2 * place + 2, 0:1]
            for ref, value in zip(outs[3 * place :], step_of(w, g, m, a, weight_sq, grad_sq)):
                ref[...] = value
                ref.send()
        w, m, a = (ref[...] for ref in ins[12:15])
        weight_sq, grad_sq = total[0:6, 1:2] / dp_count, total[0:6, 2:3] / dp_count
        g = norm_grad(t3, t4)
        for ref, value in zip(outs[9:], step_of(w, g, m, a, weight_sq, grad_sq)):
            ref[...] = value

    return update


def exchange(blocks, axes):
    return lax.all_to_all(blocks, axes, 0, 0)


def rings():
    count = lax.axis_size("chan")
    return [[(d ^ (c % 2)) * count + c for d in RING] for c in range(count)]


def turn_round():
    return lax.axis_index("chan") % 2


def swap(array, axis, bits):
    return lax.ppermute(array, axis, [(i, i ^ bits) for i in range(lax.axis_size(axis))])


def away(axis, k):
    return lambda: lax.axis_index(axis) ^ k


def in_groups(taps, groups):
    return taps.reshape(taps.shape[0], groups, -1, taps.shape[2]).transpose(1, 0, 2, 3)


def regroup(blocks, taps, groups):
    blocks = blocks.reshape(blocks.shape[0], taps, -1, blocks.shape[2]).transpose(1, 0, 2, 3)
    blocks = in_groups(blocks.reshape(taps, -1, blocks.shape[3]), groups)
    return blocks.reshape(groups, -1, blocks.shape[3])


def per_device(
    images, mask, cotangent, w_first, w_second, w_proj, norm_params, mom_first, mom_second,
    mom_proj, mom_norm, avg_first, avg_second, avg_proj, avg_norm,
):
    everyone = ("dp", "chan")
    dp_count, ch_count = lax.axis_size("dp"), lax.axis_size("chan")
    n_all = dp_count * ch_count
    batch = mask.shape[0]
    pix_here, d_in = images.shape[1], images.shape[2]
    wide = w_first.shape[1]
    d_out = wide * ch_count
    part = batch * SIDE
    pix = SIDE * part
    share = batch // ch_count
    eight = dp_count == SIDE and pix_here == 4 * SIDE
    groups = SIDE
    first_rows, second_rows = 10 * d_in // groups, 9 * d_out // groups
    square_rows = result((SIDE, wide))
    sums = result((dp_count, SIDE, wide), pinned=False)
    passing, few = (result((n, wide), pinned=False) for n in (pix, SIDE))

    def slot_dp(k):
        return lax.axis_index("dp") ^ k

    def slot_ch(k):
        return lax.axis_index("chan") ^ k

    def share_out(own):
        far = swap(own, "chan", 2)
        return [own, swap(own, "chan", 1), far, swap(far, "chan", 1)]

    if eight:
        own, squares = call(
            pack_weights,
            [w_first, w_proj, w_second],
            [result((first_rows + second_rows, wide), BF), square_rows],
        )
        gathered = lax.all_gather(own, everyone, axis_index_groups=rings())
        order = [lambda d=d: d ^ turn_round() for d in RING]
        mine, valid = call(
            pack_images,
            [quarter(images, dp_count, share), mask],
            [result((dp_count, 2, share * SIDE, 2 * d_in), BF), result((pix, wide))],
            scratch=[((d_in // wide, dp_count * share * pix_here, wide), F32)],
            later=[own],
        )
        pixels, slot = share_out(exchange(mine, "dp")), slot_ch
    else:
        valid = mask.reshape(batch, SIDE, SIDE).transpose(1, 0, 2).reshape(pix, 1).astype(F32)
        valid = jnp.broadcast_to(valid, (pix, wide))
        own = jnp.concatenate([tap_major(w_first), w_proj[None]], axis=0).astype(BF)
        own = lax.all_gather(own, "dp", axis=1, tiled=True)
        next = lax.all_gather(tap_major(w_second).astype(BF), "dp", axis=1, tiled=True)
        gathered = [in_groups(taps, groups).reshape(groups, -1, wide) for taps in (own, next)]
        gathered = jnp.concatenate(gathered, axis=1)
        order = [lambda g=g: g for g in range(groups)]
        squares = [jnp.sum(w * w, axis=0) for w in (w_first, w_proj, w_second)]
        squares = jnp.zeros((SIDE, wide), F32).at[:3].set(jnp.stack(squares))
        mine = images.reshape(dp_count, ch_count, share, pix_here, d_in)
        mine = lax.dynamic_index_in_dim(mine, lax.axis_index("chan"), 1, keepdims=False)
        pixels = lax.all_gather(exchange(mine, "dp"), "chan")
        cols = pix_here // 2
        pixels = pixels.reshape(ch_count, SIDE, 2, SIDE // cols, share, cols, 2 * d_in)
        pixels = pixels.transpose(0, 1, 2, 4, 3, 5, 6)
        pixels = pixels.reshape(ch_count, SIDE, 2, share * SIDE, 2 * d_in)
        pixels, slot = [pixels[k] for k in range(ch_count)], lambda k: k

    macs = pix * 9 * wide * d_in
    per_block = groups // ch_count
    block_slots = [lambda k=k: (lax.axis_index("chan") ^ k) * per_block for k in range(ch_count)]
    z_own, z_proj, pay = call(
        conv_first,
        [spread(gathered, order, 0, first_rows), stack(pixels, slot), valid, norm_params],
        [result((pix, wide), BF), result((pix, wide)), result((n_all, SIDE, wide))],
        flops=2 * macs,
    )
    turned = call(
        hand_on,
        [spread(gathered, order, 0, first_rows + second_rows)],
        [parts_of(0, block_slots, per_block, 0, first_rows + second_rows, gathered)],
        later=[z_own],
    )
    got1 = exchange(pay, everyone).reshape(dp_count, ch_count, SIDE, wide)
    far = swap(z_own, "chan", 2)
    far, got1, *turned = lax.optimization_barrier((far, got1, *turned))
    z_all = [z_own, swap(z_own, "chan", 1), far, swap(far, "chan", 1)]

    hidden, z_second, pay, total1, *near = call(
        conv_second,
        [
            stack(z_all, slot_ch, 3),
            fresh(got1),
            valid,
            spread(gathered, order, first_rows, second_rows),
            z_proj,
            cotangent,
        ],
        [
            result((pix, d_out), BF, pinned=False),
            passing,
            sums,
            result((ch_count, SIDE, wide)),
            passing,
            passing,
            passing,
            few,
        ],
        flops=4 * macs,
    )
    turned = turned[:1] + [swap(block, "chan", k) for k, block in enumerate(turned) if k]
    total1_own = pick(total1, away("chan", 0))
    got2 = exchange(pay, "dp")
    near_valid, near_proj, near_cot, near_total = (fresh(array) for array in near)
    output, e, hat_second, hat_proj, near_rows, pay = call(
        block_output,
        [fresh(z_second), near_proj, fresh(got2), near_total, near_valid, norm_params, near_cot],
        [result((batch, SIDE * SIDE, wide), BF), passing, passing, passing, few, sums],
    )
    got3 = exchange(pay, "dp")

    g_second_out, g_proj_out, total3 = call(
        grad_outputs,
        [fresh(e), fresh(hat_second), fresh(hat_proj), fresh(near_rows), fresh(got3), near_valid],
        [result((pix, wide), BF), result((pix, wide), BF), square_rows],
        later=turned[1:],
    )
    rows = second_rows + d_in // groups
    (grads,) = call(
        make_grad_second(eight),
        [fresh(hidden), g_second_out, even_phase(pixels, slot), g_proj_out],
        [result((groups, rows, wide), BF)],
        flops=4 * macs,
    )
    far = swap(g_second_out, "chan", 2)
    far, grads = lax.optimization_barrier((far, grads))
    g_all = [g_second_out, swap(g_second_out, "chan", 1), far, swap(far, "chan", 1)]
    if eight:
        grads_second = lax.psum_scatter(
            grads.reshape(groups * rows, wide),
            everyone,
            scatter_dimension=0,
            axis_index_groups=rings(),
            tiled=True,
        )
    else:
        grads = [
            regroup(grads[:, :second_rows], 9, dp_count),
            regroup(grads[:, second_rows:], 1, dp_count),
        ]
        grads = jnp.concatenate(grads, axis=1)
        grads_second = jnp.sum(exchange(grads, "dp").astype(F32), axis=0)

    back, msg, pay = call(
        grad_hidden,
        [stack_rows(turned, slot_ch, first_rows, second_rows, 3), stack(g_all, slot_ch, 3)]
        + [z_own, g_proj_out, total1_own, valid],
        [passing, result((2 * pix + TAIL, wide), BF), result((n_all, SIDE, wide), pinned=False)],
        flops=4 * macs,
    )
    got4 = exchange(pay, everyone).reshape(dp_count, ch_count, SIDE, wide)
    far = swap(msg, "chan", 2)
    far, got4 = lax.optimization_barrier((far, got4))
    messages = [msg, swap(msg, "chan", 1), far, swap(far, "chan", 1)]

    grads, total4 = call(
        grad_first,
        [fresh(back), z_own, fresh(got4), total1_own, norm_params, valid, stack(pixels, slot)],
        [result((groups, 9 * (d_in // groups), wide), BF), square_rows],
        flops=2 * macs,
    )
    if not eight:
        grads = regroup(grads, 9, dp_count)
    got_first = exchange(grads, "dp")

    half = wide // 2
    takes = [
        stack(messages, slot_ch, 3),
        stack(z_all, slot_ch, 3),
        fresh(got4),
        total1,
        valid,
        stack_rows(turned, slot_ch, 0, first_rows, 3),
    ]
    dims = (SIDE, 2, part, wide)
    if eight:
        rows = call(
            grad_images,
            takes,
            [split([away("dp", k) for k in range(SIDE)], dims, BF)],
            flops=2 * macs,
        )
        rows = rows[:1] + [swap(row, "dp", k) for k, row in enumerate(rows) if k]
    else:
        (rows,) = call(grad_images, takes, [result(dims, BF)], flops=2 * macs)
        cols = pix_here // 2
        rows = rows.reshape(SIDE, 2, batch, SIDE // cols, cols, wide)
        rows = rows.transpose(0, 1, 3, 2, 4, 5).reshape(dp_count, batch, cols, wide)
        rows = [exchange(rows, "dp")]
    reduced_first, reduced_second, reduced_proj, pay = call(
        reduce_all,
        [grads_second, fresh(got_first), squares, total3, total4, norm_params],
        [
            result(w_first.shape),
            result(w_second.shape),
            result(w_proj.shape),
            result((n_all, SIDE, wide)),
        ],
    )
    pay, *rows = lax.optimization_barrier((pay, *rows))
    got6 = exchange(pay, everyone)

    conv = (
        (w_first, reduced_first, mom_first, avg_first),
        (w_second, reduced_second, mom_second, avg_second),
        (w_proj, reduced_proj, mom_proj, avg_proj),
    )
    results = call(
        make_update(dp_count),
        [fresh(got6), total3, total4, *(array for group in conv for array in group)]
        + [norm_params, mom_norm, avg_norm],
        [result(group[0].shape) for group in conv for _ in range(3)]
        + [result(norm_params.shape)] * 3,
    )
    if eight:
        (grad_pixels,) = call(
            finish_images,
            [stack(rows, slot_dp, 7)],
            [result((images.shape[0], pix_here, half), BF)],
            scratch=[((images.shape[0] * pix_here, wide), F32)],
        )
    else:
        grad_pixels = rows[0].reshape(dp_count * batch, pix_here, half)
    return (output, grad_pixels, *results)


def solution(mesh):
    rows, cols, batch = P("dp", "chan"), P(None, "chan"), P("dp", None, "chan")
    weights = (rows, rows, rows, cols)
    in_specs = (P(None, "dp", None), P("dp", None), batch) + weights * 3
    out_specs = (batch, P(None, "dp", "chan")) + (rows,) * 9 + (cols,) * 3
    return jax.shard_map(
        per_device, mesh=mesh, in_specs=in_specs, out_specs=out_specs, check_vma=False
    )
```

```python
import jax
import jax.numpy as jnp
from jax import lax
from jax.experimental import pallas as pl
from jax.experimental.pallas import tpu as pltpu
from jax.sharding import PartitionSpec as P

BF = jnp.bfloat16
F32 = jnp.float32

epsilon = 1e-05
learn_rate = 0.4
trust_coef = 0.5
momentum = 0.5
avg_decay = 0.6
weight_decay = 5e-05
tiny_term = 1e-06

SIDE = 8
TAIL = 16
RING = [0, 2, 4, 6, 7, 5, 3, 1]


class whole:
    loose = 0
    direct = False

    def __init__(self, array):
        self.arrays, self.dims, self.dtype = [array], array.shape, array.dtype

    def copies(self):
        return len(self.arrays)

    def plan(self, refs, local):
        return [(refs[0], local)]


class fresh(whole):
    loose = 1
    direct = True

    def copies(self):
        return 0

    def plan(self, refs, local):
        return []


class stack(whole):
    def __init__(self, arrays, slot, loose=0):
        self.arrays, self.dtype, self.loose = list(arrays), arrays[0].dtype, loose
        self.dims, self.slot = (len(arrays),) + arrays[0].shape, slot

    def plan(self, refs, local):
        return [(ref, local.at[self.slot(k)]) for k, ref in enumerate(refs)]


class pick(whole):
    def __init__(self, array, index):
        self.arrays, self.dtype, self.index = [array], array.dtype, index
        self.dims = array.shape[1:]

    def plan(self, refs, local):
        return [(refs[0].at[self.index()], local)]


class spread(whole):
    def __init__(self, array, order, first, rows):
        self.arrays, self.dtype, self.order = [array], array.dtype, order
        self.first, self.rows = first, rows
        self.dims = (array.shape[0], rows) + array.shape[2:]

    def copies(self):
        return self.dims[0]

    def plan(self, refs, local):
        cut = pl.ds(self.first, self.rows)
        return [(refs[0].at[k, cut], local.at[place()]) for k, place in enumerate(self.order)]


class stack_rows(stack):
    def __init__(self, arrays, slot, first, rows, loose=0):
        super().__init__(arrays, slot, loose)
        self.cut = pl.ds(first, rows)
        self.dims = self.dims[:2] + (rows,) + self.dims[3:]

    def plan(self, refs, local):
        return [(ref.at[:, self.cut], local.at[self.slot(k)]) for k, ref in enumerate(refs)]


class quarter(whole):
    def __init__(self, images, groups, count):
        self.arrays, self.dtype = [images], images.dtype
        self.per, self.count = images.shape[0] // groups, count
        self.dims = (groups, count) + images.shape[1:]

    def copies(self):
        return self.dims[0]

    def plan(self, refs, local):
        mine = lax.axis_index("chan") * self.count
        return [
            (refs[0].at[pl.ds(g * self.per + mine, self.count)], local.at[g])
            for g in range(self.dims[0])
        ]


class even_phase(stack):
    def __init__(self, arrays, slot):
        super().__init__(arrays, slot)
        self.lanes = arrays[0].shape[3] // 2
        self.dims = (len(arrays), arrays[0].shape[0], arrays[0].shape[2], self.lanes)

    def plan(self, refs, local):
        lanes = pl.ds(0, self.lanes)
        return [(ref.at[:, 0, :, lanes], local.at[self.slot(k)]) for k, ref in enumerate(refs)]


class result:
    pinned = True

    def __init__(self, dims, dtype=F32, pinned=True):
        self.dims, self.dtype, self.pinned = tuple(dims), dtype, pinned
        self.outs = [jax.ShapeDtypeStruct(self.dims, dtype)]

    def copies(self):
        return len(self.outs)

    def plan(self, local, refs):
        return [(local, refs[0])]


class split(result):
    def __init__(self, slots, dims, dtype=F32, part=None):
        self.dims, self.dtype, self.slots = tuple(dims), dtype, slots
        self.outs = [jax.ShapeDtypeStruct(self.dims[1:], dtype) for _ in slots]

    def plan(self, local, refs):
        return [(local.at[slot()], ref) for slot, ref in zip(self.slots, refs)]


class parts_of(result):
    dims = None

    def __init__(self, source, slots, count, first, rows, array):
        self.source, self.slots, self.count, self.cut = source, slots, count, pl.ds(first, rows)
        dims = (count, rows) + array.shape[2:]
        self.outs = [jax.ShapeDtypeStruct(dims, array.dtype) for _ in slots]

    def plan(self, local, refs):
        return [
            (local.at[pl.ds(slot(), self.count), self.cut], ref)
            for slot, ref in zip(self.slots, refs)
        ]


class Taken:
    def __init__(self, local, copies):
        self.local, self.copies, self.waited = local, copies, False

    def ref(self):
        if not self.waited:
            for copy in self.copies:
                copy.wait()
            self.waited = True
        return self.local

    def __getitem__(self, index):
        return self.ref()[index]

    @property
    def shape(self):
        return self.local.shape


class Given:
    def __init__(self, local, copies):
        self.local, self.copies, self.sent = local, copies, False

    def send(self):
        if not self.sent:
            for copy in self.copies:
                copy.start()
            self.sent = True

    def __setitem__(self, index, value):
        self.local[index] = value

    @property
    def shape(self):
        return self.local.shape


def call(body, takes, gives, scratch=(), flops=0, limit=40, later=()):
    takes = [t if isinstance(t, whole) else whole(t) for t in takes]
    arrays = [a for t in takes for a in t.arrays]
    spec = pl.BlockSpec(memory_space=pltpu.HBM)
    loose, vmem = pl.BlockSpec(memory_space=pl.ANY), pl.BlockSpec(memory_space=pltpu.VMEM)
    pinned = [False] * len(later)
    in_specs = [loose] * len(later)
    for t in takes:
        pinned += [True] * (len(t.arrays) - t.loose) + [False] * t.loose
        in_specs += [spec] * (len(t.arrays) - t.loose) + [vmem if t.direct else loose] * t.loose
    outs = [o for g in gives for o in g.outs]
    n_later, n_in, n_out = len(later), len(arrays), len(outs)
    n_copies = sum(t.copies() for t in takes) + sum(g.copies() for g in gives if g.pinned)

    def kernel(*refs):
        refs = refs[n_later:]
        ins, res = list(refs[:n_in]), list(refs[n_in : n_in + n_out])
        local = list(refs[n_in + n_out : -1])
        sems = refs[-1]
        used = 0
        taken, given = [], []
        for t in takes:
            mine, ins = ins[: len(t.arrays)], ins[len(t.arrays) :]
            place = mine[0] if t.direct else local.pop(0)
            copies = []
            for a, b in t.plan(mine, place):
                copies.append(pltpu.make_async_copy(a, b, sems.at[used]))
                used += 1
            for copy in copies:
                copy.start()
            taken.append(Taken(place, copies))
        for g in gives:
            mine, res = res[: len(g.outs)], res[len(g.outs) :]
            if g.dims is None:
                place = taken[g.source].local
            else:
                place = local.pop(0) if g.pinned else mine[0]
            copies = []
            for a, b in g.plan(place, mine) if g.pinned else ():
                copies.append(pltpu.make_async_copy(a, b, sems.at[used]))
                used += 1
            given.append(Given(place, copies))
        body(*taken, *given, *local)
        for t in taken:
            t.ref()
        for g in given:
            g.send()
        for g in given:
            for copy in g.copies:
                copy.wait()

    moved = sum(a.size * a.dtype.itemsize for a in arrays + outs)
    operands = [
        pltpu.with_memory_space_constraint(a, pltpu.HBM) if pin else a
        for a, pin in zip([*later, *arrays], pinned)
    ]
    values = pl.pallas_call(
        kernel,
        out_shape=[pltpu.HBM(o.shape, o.dtype) if g.pinned else o for g in gives for o in g.outs],
        in_specs=in_specs,
        out_specs=[spec if g.pinned else vmem for g in gives for _ in g.outs],
        scratch_shapes=[pltpu.VMEM(t.dims, t.dtype) for t in takes if not t.direct]
        + [pltpu.VMEM(g.dims, g.dtype) for g in gives if g.dims is not None and g.pinned]
        + [pltpu.VMEM(dims, dtype) for dims, dtype in scratch]
        + [pltpu.SemaphoreType.DMA((n_copies,))],
        compiler_params=pltpu.CompilerParams(vmem_limit_bytes=limit * 2**20),
        cost_estimate=pl.CostEstimate(flops=flops, bytes_accessed=moved, transcendentals=0),
        name=body.__name__,
    )(*operands)
    return list(values)


def dot(a, b):
    return jnp.dot(a, b, preferred_element_type=F32)


def dot_nt(a, b):
    return lax.dot_general(a, b, (((1,), (1,)), ((), ())), preferred_element_type=F32)


def dot_tn(a, b):
    return lax.dot_general(a, b, (((0,), (0,)), ((), ())), preferred_element_type=F32)


def shift_col(x, step):
    rows, lanes = x.shape
    grouped = x.reshape(rows // SIDE, SIDE, lanes)
    rolled = pltpu.roll(grouped, step % SIDE, 1)
    col = lax.broadcasted_iota(jnp.int32, grouped.shape, 1)
    edge = 0 if step > 0 else SIDE - 1
    return jnp.where(col == edge, 0.0, rolled).reshape(rows, lanes)


def shift_row(x, step):
    part = x.shape[0] // SIDE
    blank = jnp.zeros((part, x.shape[1]), x.dtype)
    if step > 0:
        return jnp.concatenate([blank, x[:-part]], axis=0)
    return jnp.concatenate([x[part:], blank], axis=0)


def swap_orders(x, batch):
    pieces = [
        x[(b * SIDE + r) * SIDE : (b * SIDE + r + 1) * SIDE] for r in range(SIDE) for b in range(batch)
    ]
    return jnp.concatenate(pieces, axis=0)


def swap_back(x, batch):
    pieces = [
        x[(r * batch + b) * SIDE : (r * batch + b + 1) * SIDE] for b in range(batch) for r in range(SIDE)
    ]
    return jnp.concatenate(pieces, axis=0)


def col_sum(x):
    return jnp.sum(x, axis=0, keepdims=True)


def lane_sum(x):
    return jnp.sum(col_sum(x), axis=1, keepdims=True)


def rows_of(*rows):
    pad = SIDE - sum(row.shape[0] for row in rows)
    tail = [jnp.zeros((pad, rows[0].shape[1]), F32)] if pad else []
    return jnp.concatenate(list(rows) + tail, axis=0)


def spread_rows(out, rows):
    out[...] = jnp.broadcast_to(rows[None, : out.shape[1]], out.shape)


def mean_inverse(total, squares, count):
    center = total / count
    spread = squares / count - center * center
    return center, lax.rsqrt(spread + epsilon)


def slope(v):
    sigma = jax.nn.sigmoid(v)
    return sigma * (1.0 + v * (1.0 - sigma))


def three_rows(values):
    high = values.astype(BF).astype(F32)
    rest = values - high
    middle = rest.astype(BF).astype(F32)
    low = rest - middle
    blank = jnp.zeros((TAIL - 3 * values.shape[0], values.shape[1]), F32)
    return jnp.concatenate([high, middle, low, blank], axis=0).astype(BF)


def one_row(parts, count):
    parts = parts.astype(F32)
    return parts[:count] + parts[count : 2 * count] + parts[2 * count : 3 * count]


def add_up(pieces):
    total = pieces[0].astype(F32)
    for piece in pieces[1:]:
        total = total + piece.astype(F32)
    return total


def expand_mask(inside):
    images, wide = inside.shape
    dims = (images, SIDE, wide)
    lane = lax.broadcasted_iota(jnp.int32, dims, 2)
    col = lax.broadcasted_iota(jnp.int32, dims, 1)
    picked = jnp.where(lane == col, jnp.broadcast_to(inside[:, None, :], dims), 0.0)
    return jnp.broadcast_to(jnp.sum(picked, axis=2, keepdims=True), dims).reshape(-1, wide)


def widen(mask, wide):
    return jnp.concatenate(
        [mask, jnp.zeros((mask.shape[0], wide - mask.shape[1]), mask.dtype)], axis=1
    )


def lane_row(x):
    return col_sum(x * x)


def pack_weights(w, p, w_next, out, rows):
    depth = p.shape[0]
    w_ref, next_ref = w.ref(), w_next.ref()
    pieces = [w_ref[pl.ds(tap, depth, stride=9), :] for tap in range(9)] + [p[...]]
    depth = w_next.shape[0] // 9
    pieces += [next_ref[pl.ds(tap, depth, stride=9), :] for tap in range(9)]
    out[...] = jnp.concatenate(pieces, axis=0).astype(BF)
    out.send()
    rows[...] = rows_of(lane_row(w[...]), lane_row(p[...]), lane_row(w_next[...]))


def pack_images(images, mask, out, valid_out, scratch):
    groups, count, pix, lanes = images.shape
    wide = valid_out.shape[1]
    half = groups * count * pix // 2
    for k in range(lanes // wide):
        cut = slice(k * wide, (k + 1) * wide)
        scratch[k] = images[:, :, :, cut].astype(F32).reshape(2 * half, wide)
        for col in range(2):
            taken = scratch[k, pl.ds(col, half, stride=2), :].reshape(groups, count, 2, SIDE, wide)
            for row in range(2):
                rows = jnp.concatenate([taken[:, i, row] for i in range(count)], axis=1)
                start = col * lanes + k * wide
                out[:, row, :, start : start + wide] = rows.astype(BF)
    out.send()
    inside = widen(mask[...].astype(F32), wide)
    part = inside.shape[0] * SIDE
    for row in range(SIDE):
        turned = pltpu.roll(inside, (wide - SIDE * row) % wide, 1)
        valid_out[row * part : (row + 1) * part] = expand_mask(turned)


def tap_major(w):
    return w.reshape(-1, 9, w.shape[1]).transpose(1, 0, 2)


def taps_of(w, depth, first=0):
    def taps(*which):
        starts = [first + t * depth for t in which]
        return jnp.concatenate(
            [w[:, a : a + depth].reshape(-1, w.shape[2]) for a in starts], axis=1
        )

    return taps


def phase_of(x, row, col):
    lanes = x.shape[4] // 2
    cut = slice(col * lanes, (col + 1) * lanes)
    pieces = [x[k, r, row, :, cut] for r in range(x.shape[1]) for k in range(x.shape[0])]
    return jnp.concatenate(pieces, axis=0)


def conv_first(w, x, m, n, zb_out, zp_out, sums_out, pay):
    taps = taps_of(w, w.shape[1] // 10)
    wide = w.shape[2]
    y00 = dot(phase_of(x, 0, 0), taps(4, 9))
    y01 = dot(phase_of(x, 0, 1), taps(5, 3))
    y10 = dot(phase_of(x, 1, 0), taps(7, 1))
    y11 = dot(phase_of(x, 1, 1), taps(8, 6, 2, 0))
    here = y00[:, :wide] + y01[:, :wide] + y10[:, :wide] + y11[:, :wide]
    left = y01[:, wide:] + y11[:, wide : 2 * wide]
    above = y10[:, wide:] + y11[:, 2 * wide : 3 * wide]
    corner = y11[:, 3 * wide :]
    z = here + shift_row(above, 1) + shift_col(left + shift_row(corner, 1), 1)
    pix = z.shape[0]
    zb_out[:pix] = z.astype(BF)
    zb_out[pix:] = three_rows(n[0:2])
    zb_out.send()
    zp = y00[:, wide:]
    valid = m[...]
    vz, vzp = valid * z, valid * zp
    spread_rows(pay, rows_of(col_sum(vz), col_sum(vz * z), col_sum(valid)))
    pay.send()
    sums_out[...] = rows_of(col_sum(vzp), col_sum(vzp * zp))
    zp_out[...] = zp


def hand_on(w, *outs):
    w.ref()


def first_norm(z, rows):
    count = rows[2:3]
    center, inverse = mean_inverse(rows[0:1], rows[1:2], count)
    hat = (z - center) * inverse
    return hat, hat * rows[3:4] + rows[4:5], inverse


def conv_second(z, got, m, w, zp, sums, cot, h_out, z2_out, pay, tot_out, m_out, zp_out, cot_out, own_out):
    blocks, wide = z.shape[0], z.shape[2]
    valid = m[...]
    pix = valid.shape[0]
    hidden = []
    for k in range(blocks):
        rows = rows_of(jnp.sum(got[:, k], axis=0)[0:3], one_row(z[k, pix:], 2))
        tot_out[k] = rows
        _, lin, _ = first_norm(z[k, :pix].astype(F32), rows)
        hidden.append((lin * jax.nn.sigmoid(lin) * valid).astype(BF))
        h_out[:, k * wide : (k + 1) * wide] = hidden[-1]
    h_out.send()
    hidden = jnp.concatenate(hidden, axis=1)
    taps = taps_of(w, hidden.shape[1] // w.shape[0])
    moved = []
    for col in range(3):
        y = dot(hidden, taps(col, 3 + col, 6 + col))
        moved.append(
            shift_row(y[:, :wide], 1) + y[:, wide : 2 * wide] + shift_row(y[:, 2 * wide :], -1)
        )
    z2 = moved[1] + shift_col(moved[0], 1) + shift_col(moved[2], -1)
    vz = valid * z2
    spread_rows(pay, rows_of(col_sum(vz), col_sum(vz * z2), sums[0:2]))
    pay.send()
    z2_out[...] = z2
    batch, pix, wide = cot.shape
    m_out[...] = valid
    zp_out[...] = zp[...]
    cot_out[...] = swap_orders(cot[...].astype(F32).reshape(batch * pix, wide), batch)
    own_out[...] = tot_out.local[pl.ds(lax.axis_index("chan"), 1)][0]


def block_output(z2, zp, got, tot1, m, n, cot, out, e_out, hat2_out, hat_p_out, rows_out, pay):
    total, count = jnp.sum(got[...], axis=0), tot1[2:3]
    center2, inverse2 = mean_inverse(total[0:1], total[1:2], count)
    center_p, inverse_p = mean_inverse(total[2:3], total[3:4], count)
    hat2, hat_p = (z2[...] - center2) * inverse2, (zp[...] - center_p) * inverse_p
    hat2_out[...] = hat2
    hat_p_out[...] = hat_p
    rows_out[...] = rows_of(n[2:3] * inverse2, n[4:5] * inverse_p, count)
    summed = hat2 * n[2:3] + n[3:4] + (hat_p * n[4:5] + n[5:6])
    sigma = jax.nn.sigmoid(summed)
    valid = m[...]
    batch, pix, wide = out.shape
    e = cot[...] * valid * (sigma * (1.0 + summed * (1.0 - sigma)))
    spread_rows(pay, rows_of(col_sum(e), col_sum(e * hat2), col_sum(e * hat_p)))
    pay.send()
    e_out[...] = e
    out[...] = swap_back(summed * sigma * valid, batch).astype(BF).reshape(out.shape)


def grad_outputs(e, hat2, hat_p, rows, got, m, g2_out, gp_out, tot_out):
    back, count = jnp.sum(got[...], axis=0), rows[2:3]
    tot_out[...] = rows_of(back)
    valid, e = m[...], e[...]
    loss = valid * ((back[0:1] + hat2[...] * back[1:2]) / count)
    g2_out[...] = (rows[0:1] * (e - loss)).astype(BF)
    g2_out.send()
    loss = valid * ((back[0:1] + hat_p[...] * back[2:3]) / count)
    gp_out[...] = (rows[1:2] * (e - loss)).astype(BF)


def grad_hidden(w, g2, z, gp, tot1, m, b_out, msg, pay):
    blocks, _, wide = g2.shape
    count, part = w.shape[1], w.shape[2] // 9
    depth = count * part
    moved = []
    grads = jnp.concatenate([g2[k] for k in range(blocks)], axis=1)
    for col in range(3):
        starts = [(3 * row + col) * part for row in range(3)]
        taps = [
            jnp.concatenate([w[k, :, a : a + part].reshape(depth, wide) for k in range(blocks)], axis=1)
            for a in starts
        ]
        y = dot_nt(grads, jnp.concatenate(taps, axis=0))
        moved.append(
            shift_row(y[:, :depth], -1) + y[:, depth : 2 * depth] + shift_row(y[:, 2 * depth :], 1)
        )
    gh = moved[1] + shift_col(moved[0], -1) + shift_col(moved[2], 1)
    valid = m[...]
    hat, lin, _ = first_norm(z[: valid.shape[0]].astype(F32), tot1[...])
    b = gh * (slope(lin) * valid)
    shift, scaled = col_sum(b), col_sum(b * hat)
    spread_rows(pay, rows_of(shift, scaled))
    pay.send()
    here = col_sum(valid)
    shift, scaled = shift / here, scaled / here
    pix = b.shape[0]
    msg[:pix] = (b - valid * (shift + hat * scaled)).astype(BF)
    msg[pix : 2 * pix] = gp[...]
    msg[2 * pix :] = three_rows(jnp.concatenate([shift, scaled], axis=0))
    msg.send()
    b_out[...] = b


def make_grad_second(on_ring):
    def grad_second(h, g2, x, gp, g_out):
        groups, rows, wide = g_out.shape
        places = list(range(groups))
        if on_ring:
            last, turn = len(RING) - 1, turn_round()
            places = [RING.index(k) for k in places]
            places = [p + turn * (last - 2 * p) for p in places]
        share = h.shape[1] // groups
        h, g2 = h[...], g2[...].astype(F32)
        moved = [shift_col(g2, step).astype(BF) if step else g2.astype(BF) for step in (-1, 0, 1)]

        def put(rows, g):
            g = g.astype(BF).reshape(groups, -1, wide)
            for k, place in enumerate(places):
                g_out[place, rows] = g[k]

        spread_out = []
        for tap in range(9):
            step = tap // 3 - 1
            spread_out.append(shift_row(moved[tap % 3], step) if step else moved[tap % 3])
        spread_out = dot_tn(h, jnp.concatenate(spread_out, axis=1))
        for tap in range(9):
            g = spread_out[:, tap * wide : (tap + 1) * wide]
            put(slice(tap * share, (tap + 1) * share), g)
        pieces = [x[k, r] for r in range(SIDE) for k in range(x.shape[0])]
        put(slice(9 * share, rows), dot_tn(jnp.concatenate(pieces, axis=0), gp[...]))

    return grad_second


def grad_first(b, z, got, tot1, n, m, x, blocks_out, tot_out):
    own = got[:, pl.ds(lax.axis_index("chan"), 1)]
    back, count = jnp.sum(own, axis=0)[0], tot1[2:3]
    tot_out[...] = rows_of(back)
    hat, _, inverse = first_norm(z[: m.shape[0]].astype(F32), tot1[...])
    g = n[0:1] * inverse * (b[...] - m[...] * ((back[0:1] + hat * back[1:2]) / count))
    here, left = g.astype(BF), shift_col(g, -1).astype(BF)
    wide = here.shape[1]
    groups = blocks_out.shape[0]
    share = x.shape[4] // 2 // groups

    def put(tap, grad):
        rows = grad.astype(BF).reshape(groups, share, wide)
        blocks_out[:, tap * share : (tap + 1) * share] = rows

    above, corner = shift_row(here, -1), shift_row(left, -1)
    for row, col, pairs in (
        (0, 0, ((4, here),)),
        (0, 1, ((5, here), (3, left))),
        (1, 0, ((7, here), (1, above))),
        (1, 1, ((8, here), (6, left), (2, above), (0, corner))),
    ):
        both = jnp.concatenate([grad for _, grad in pairs], axis=1)
        both = dot_tn(phase_of(x, row, col), both)
        for place, (tap, _) in enumerate(pairs):
            put(tap, both[:, place * wide : (place + 1) * wide])


def grad_images(msg, z, got, tot1, m, w, out):
    blocks, count = w.shape[0], w.shape[1]
    depth = w.shape[2] // 10
    half, wide = count * depth, w.shape[3]

    def taps(*which):
        blocks_of = [
            [w[k, :, t * depth : (t + 1) * depth].reshape(half, wide) for k in range(blocks)]
            for t in which
        ]
        return jnp.concatenate([jnp.concatenate(row, axis=1) for row in blocks_of], axis=0)

    grads = []
    valid = m[...]
    pix = valid.shape[0]
    for k in range(blocks):
        rows, back = tot1[k], jnp.sum(got[:, k], axis=0)
        hat, _, inverse = first_norm(z[k, :pix].astype(F32), rows)
        fit = back[0:2] / rows[2:3] - one_row(msg[k, 2 * pix :], 2)
        loss = valid * (fit[0:1] + hat * fit[1:2])
        grads.append((rows[3:4] * inverse * (msg[k, :pix].astype(F32) - loss)).astype(BF))
    grads = jnp.concatenate(grads, axis=1)
    plain, moved = dot_nt(grads, taps(4, 5, 7, 8, 1, 2)), dot_nt(grads, taps(3, 3, 6, 6, 0, 0))
    proj = jnp.concatenate([msg[k, pix : 2 * pix] for k in range(blocks)], axis=1)
    proj = dot_nt(proj, taps(9, 9))
    lane = lax.broadcasted_iota(jnp.int32, moved.shape, 1) % (2 * half)
    total = plain + jnp.where(lane >= half, shift_col(moved, -1), 0.0)
    lane = lax.broadcasted_iota(jnp.int32, proj.shape, 1)
    even = total[:, : 2 * half] + jnp.where(lane < half, proj, 0.0)
    odd = total[:, 2 * half : 4 * half] + shift_row(total[:, 4 * half :], -1)
    for row, value in enumerate((even, odd)):
        out[:, row] = value.astype(BF).reshape(out.shape[0], -1, 2 * half)


def finish_images(x, out, scratch):
    images, pix, half = out.shape
    groups, _, part, wide = x.shape
    count = part // SIDE
    value = x[...].astype(F32).reshape(groups, 2, count, 1, SIDE, wide)
    value = jnp.concatenate([value[:, 0], value[:, 1]], axis=2)
    rows = images * pix // 2
    value = value.reshape(rows, wide)
    scratch[pl.ds(0, rows, stride=2), :] = value
    scratch[pl.ds(1, rows, stride=2), :] = pltpu.roll(value, half, 1)
    out[...] = scratch[...][:, :half].astype(BF).reshape(out.shape)


def put_rows(out, total):
    depth = out.shape[0] // 9
    for tap in range(9):
        out.local[pl.ds(tap, depth, stride=9), :] = total[tap * depth : (tap + 1) * depth]


def reduce_all(second, x, sw, t3, t4, n, g1_out, g2_out, gp_out, pay):
    second = second[...].astype(F32)
    cut = g2_out.shape[0]
    conv, proj = second[:cut], second[cut:]
    parts = [lane_row(conv), lane_row(proj)]
    first = add_up([x[k] for k in range(x.shape[0])])
    rows = [sw[0:1], lane_row(first), sw[2:3], parts[0], sw[1:2], parts[1]]
    nw, gn = n[...], norm_grad(t3, t4)
    blank = jnp.zeros((2, nw.shape[1]), F32)
    cols = [
        jnp.sum(jnp.concatenate(rows + [blank], axis=0), axis=1, keepdims=True),
        jnp.sum(jnp.concatenate([nw * nw, blank], axis=0), axis=1, keepdims=True),
        jnp.sum(jnp.concatenate([gn * gn, blank], axis=0), axis=1, keepdims=True),
    ]
    dims = (SIDE, pay.shape[2])
    lane, row = (lax.broadcasted_iota(jnp.int32, dims, axis) for axis in (1, 0))
    block = jnp.zeros(dims, F32)
    for place, col in enumerate(cols):
        block = jnp.where(lane == SIDE * place + row, col, block)
    spread_rows(pay, col_sum(block))
    pay.send()
    gp_out[...] = proj
    put_rows(g2_out, conv)
    g2_out.send()
    put_rows(g1_out, first)


def norm_grad(t3, t4):
    return jnp.concatenate([t4[1:2], t4[0:1], t3[1:2], t3[0:1], t3[2:3], t3[0:1]], axis=0)


def step_of(w, g, m, a, weight_sq, grad_sq):
    weight_len = jnp.sqrt(weight_sq)
    trust = trust_coef * weight_len / (jnp.sqrt(grad_sq) + weight_decay * weight_len + tiny_term)
    step = trust * (g + weight_decay * w)
    m_new = momentum * m + step
    w_new = w - learn_rate * (step + momentum * m_new)
    return w_new, m_new, avg_decay * a + (1.0 - avg_decay) * w_new


def make_update(dp_count):
    def update(*refs):
        r6, t3, t4 = refs[:3]
        ins, outs = refs[3:18], refs[18:]
        total = jnp.broadcast_to(jnp.sum(r6[...], axis=0), (SIDE, r6.shape[2]))
        lane, row = (lax.broadcasted_iota(jnp.int32, total.shape, axis) for axis in (1, 0))
        total = [
            jnp.sum(jnp.where(lane == SIDE * k + row, total, 0.0), axis=1, keepdims=True)
            for k in range(3)
        ]
        for place in range(3):
            w, g, m, a = (ref[...] for ref in ins[4 * place : 4 * place + 4])
            weight_sq = total[0][2 * place : 2 * place + 1]
            grad_sq = total[0][2 * place + 1 : 2 * place + 2]
            for ref, value in zip(outs[3 * place :], step_of(w, g, m, a, weight_sq, grad_sq)):
                ref[...] = value
                ref.send()
        w, m, a = (ref[...] for ref in ins[12:15])
        weight_sq, grad_sq = total[1][0:6] / dp_count, total[2][0:6] / dp_count
        g = norm_grad(t3, t4)
        for ref, value in zip(outs[9:], step_of(w, g, m, a, weight_sq, grad_sq)):
            ref[...] = value

    return update


def exchange(blocks, axes):
    return lax.all_to_all(blocks, axes, 0, 0)


def rings():
    count = lax.axis_size("chan")
    return [[(d ^ (c % 2)) * count + c for d in RING] for c in range(count)]


def turn_round():
    return lax.axis_index("chan") % 2


def swap(array, axis, bits):
    return lax.ppermute(array, axis, [(i, i ^ bits) for i in range(lax.axis_size(axis))])


def away(axis, k):
    return lambda: lax.axis_index(axis) ^ k


def in_groups(taps, groups):
    return taps.reshape(taps.shape[0], groups, -1, taps.shape[2]).transpose(1, 0, 2, 3)


def regroup(blocks, taps, groups):
    blocks = blocks.reshape(blocks.shape[0], taps, -1, blocks.shape[2]).transpose(1, 0, 2, 3)
    blocks = in_groups(blocks.reshape(taps, -1, blocks.shape[3]), groups)
    return blocks.reshape(groups, -1, blocks.shape[3])


def per_device(
    images, mask, cotangent, w_first, w_second, w_proj, norm_params, mom_first, mom_second,
    mom_proj, mom_norm, avg_first, avg_second, avg_proj, avg_norm,
):
    everyone = ("dp", "chan")
    dp_count, ch_count = lax.axis_size("dp"), lax.axis_size("chan")
    n_all = dp_count * ch_count
    batch = mask.shape[0]
    pix_here, d_in = images.shape[1], images.shape[2]
    wide = w_first.shape[1]
    d_out = wide * ch_count
    part = batch * SIDE
    pix = SIDE * part
    share = batch // ch_count
    eight = dp_count == SIDE and pix_here == 4 * SIDE
    groups = SIDE
    first_rows, second_rows = 10 * d_in // groups, 9 * d_out // groups
    square_rows = result((SIDE, wide))
    four = result((dp_count, 4, wide), pinned=False)
    passing, few = (result((n, wide), pinned=False) for n in (pix, SIDE))

    def slot_dp(k):
        return lax.axis_index("dp") ^ k

    def slot_ch(k):
        return lax.axis_index("chan") ^ k

    def share_out(own):
        far = swap(own, "chan", 2)
        return [own, swap(own, "chan", 1), far, swap(far, "chan", 1)]

    if eight:
        own, squares = call(
            pack_weights,
            [w_first, w_proj, w_second],
            [result((first_rows + second_rows, wide), BF), square_rows],
        )
        gathered = lax.all_gather(own, everyone, axis_index_groups=rings())
        order = [lambda d=d: d ^ turn_round() for d in RING]
        mine, valid = call(
            pack_images,
            [quarter(images, dp_count, share), mask],
            [result((dp_count, 2, share * SIDE, 2 * d_in), BF), result((pix, wide))],
            scratch=[((d_in // wide, dp_count * share * pix_here, wide), F32)],
            later=[own],
        )
        pixels, slot = share_out(exchange(mine, "dp")), slot_ch
    else:
        valid = mask.reshape(batch, SIDE, SIDE).transpose(1, 0, 2).reshape(pix, 1).astype(F32)
        valid = jnp.broadcast_to(valid, (pix, wide))
        own = jnp.concatenate([tap_major(w_first), w_proj[None]], axis=0).astype(BF)
        own = lax.all_gather(own, "dp", axis=1, tiled=True)
        next = lax.all_gather(tap_major(w_second).astype(BF), "dp", axis=1, tiled=True)
        gathered = [in_groups(taps, groups).reshape(groups, -1, wide) for taps in (own, next)]
        gathered = jnp.concatenate(gathered, axis=1)
        order = [lambda g=g: g for g in range(groups)]
        squares = [jnp.sum(w * w, axis=0) for w in (w_first, w_proj, w_second)]
        squares = jnp.zeros((SIDE, wide), F32).at[:3].set(jnp.stack(squares))
        mine = images.reshape(dp_count, ch_count, share, pix_here, d_in)
        mine = lax.dynamic_index_in_dim(mine, lax.axis_index("chan"), 1, keepdims=False)
        pixels = lax.all_gather(exchange(mine, "dp"), "chan")
        cols = pix_here // 2
        pixels = pixels.reshape(ch_count, SIDE, 2, SIDE // cols, share, cols, 2 * d_in)
        pixels = pixels.transpose(0, 1, 2, 4, 3, 5, 6)
        pixels = pixels.reshape(ch_count, SIDE, 2, share * SIDE, 2 * d_in)
        pixels, slot = [pixels[k] for k in range(ch_count)], lambda k: k

    macs = pix * 9 * wide * d_in
    per_block = groups // ch_count
    block_slots = [lambda k=k: (lax.axis_index("chan") ^ k) * per_block for k in range(ch_count)]
    z_own, z_proj, sums_proj, pay = call(
        conv_first,
        [spread(gathered, order, 0, first_rows), stack(pixels, slot), valid, norm_params],
        [
            result((pix + TAIL, wide), BF),
            result((pix, wide)),
            square_rows,
            result((n_all, 4, wide)),
        ],
        flops=2 * macs,
    )
    turned = call(
        hand_on,
        [spread(gathered, order, 0, first_rows + second_rows)],
        [parts_of(0, block_slots, per_block, 0, first_rows + second_rows, gathered)],
        later=[z_own],
    )
    got1 = exchange(pay, everyone).reshape(dp_count, ch_count, 4, wide)
    far = swap(z_own, "chan", 2)
    far, got1, *turned = lax.optimization_barrier((far, got1, *turned))
    z_all = [z_own, swap(z_own, "chan", 1), far, swap(far, "chan", 1)]

    hidden, z_second, pay, total1, *near = call(
        conv_second,
        [
            stack(z_all, slot_ch, 3),
            fresh(got1),
            valid,
            spread(gathered, order, first_rows, second_rows),
            z_proj,
            sums_proj,
            cotangent,
        ],
        [
            result((pix, d_out), BF, pinned=False),
            passing,
            four,
            result((ch_count, SIDE, wide)),
            passing,
            passing,
            passing,
            few,
        ],
        flops=4 * macs,
    )
    turned = turned[:1] + [swap(block, "chan", k) for k, block in enumerate(turned) if k]
    total1_own = pick(total1, away("chan", 0))
    got2 = exchange(pay, "dp")
    near_valid, near_proj, near_cot, near_total = (fresh(array) for array in near)
    output, e, hat_second, hat_proj, near_rows, pay = call(
        block_output,
        [fresh(z_second), near_proj, fresh(got2), near_total, near_valid, norm_params, near_cot],
        [result((batch, SIDE * SIDE, wide), BF), passing, passing, passing, few, four],
    )
    got3 = exchange(pay, "dp")

    g_second_out, g_proj_out, total3 = call(
        grad_outputs,
        [fresh(e), fresh(hat_second), fresh(hat_proj), fresh(near_rows), fresh(got3), near_valid],
        [result((pix, wide), BF), result((pix, wide), BF), square_rows],
        later=turned[1:],
    )
    rows = second_rows + d_in // groups
    (grads,) = call(
        make_grad_second(eight),
        [fresh(hidden), g_second_out, even_phase(pixels, slot), g_proj_out],
        [result((groups, rows, wide), BF)],
        flops=4 * macs,
    )
    far = swap(g_second_out, "chan", 2)
    far, grads = lax.optimization_barrier((far, grads))
    g_all = [g_second_out, swap(g_second_out, "chan", 1), far, swap(far, "chan", 1)]
    if eight:
        grads_second = lax.psum_scatter(
            grads.reshape(groups * rows, wide),
            everyone,
            scatter_dimension=0,
            axis_index_groups=rings(),
            tiled=True,
        )
    else:
        grads = [
            regroup(grads[:, :second_rows], 9, dp_count),
            regroup(grads[:, second_rows:], 1, dp_count),
        ]
        grads = jnp.concatenate(grads, axis=1)
        grads_second = jnp.sum(exchange(grads, "dp").astype(F32), axis=0)

    back, msg, pay = call(
        grad_hidden,
        [stack_rows(turned, slot_ch, first_rows, second_rows, 3), stack(g_all, slot_ch, 3)]
        + [z_own, g_proj_out, total1_own, valid],
        [passing, result((2 * pix + TAIL, wide), BF), result((n_all, 2, wide), pinned=False)],
        flops=4 * macs,
    )
    got4 = exchange(pay, everyone).reshape(dp_count, ch_count, 2, wide)
    far = swap(msg, "chan", 2)
    far, got4 = lax.optimization_barrier((far, got4))
    messages = [msg, swap(msg, "chan", 1), far, swap(far, "chan", 1)]

    grads, total4 = call(
        grad_first,
        [fresh(back), z_own, fresh(got4), total1_own, norm_params, valid, stack(pixels, slot)],
        [result((groups, 9 * (d_in // groups), wide), BF), square_rows],
        flops=2 * macs,
    )
    if not eight:
        grads = regroup(grads, 9, dp_count)
    got_first = exchange(grads, "dp")

    half = wide // 2
    takes = [
        stack(messages, slot_ch, 3),
        stack(z_all, slot_ch, 3),
        fresh(got4),
        total1,
        valid,
        stack_rows(turned, slot_ch, 0, first_rows, 3),
    ]
    dims = (SIDE, 2, part, wide)
    if eight:
        rows = call(
            grad_images,
            takes,
            [split([away("dp", k) for k in range(SIDE)], dims, BF)],
            flops=2 * macs,
        )
        rows = rows[:1] + [swap(row, "dp", k) for k, row in enumerate(rows) if k]
    else:
        (rows,) = call(grad_images, takes, [result(dims, BF)], flops=2 * macs)
        cols = pix_here // 2
        rows = rows.reshape(SIDE, 2, batch, SIDE // cols, cols, wide)
        rows = rows.transpose(0, 1, 3, 2, 4, 5).reshape(dp_count, batch, cols, wide)
        rows = [exchange(rows, "dp")]
    reduced_first, reduced_second, reduced_proj, pay = call(
        reduce_all,
        [grads_second, fresh(got_first), squares, total3, total4, norm_params],
        [
            result(w_first.shape),
            result(w_second.shape),
            result(w_proj.shape),
            result((n_all, 1, wide)),
        ],
    )
    pay, *rows = lax.optimization_barrier((pay, *rows))
    got6 = exchange(pay, everyone)

    conv = (
        (w_first, reduced_first, mom_first, avg_first),
        (w_second, reduced_second, mom_second, avg_second),
        (w_proj, reduced_proj, mom_proj, avg_proj),
    )
    results = call(
        make_update(dp_count),
        [fresh(got6), total3, total4, *(array for group in conv for array in group)]
        + [norm_params, mom_norm, avg_norm],
        [result(group[0].shape) for group in conv for _ in range(3)]
        + [result(norm_params.shape)] * 3,
    )
    if eight:
        (grad_pixels,) = call(
            finish_images,
            [stack(rows, slot_dp, 7)],
            [result((images.shape[0], pix_here, half), BF)],
            scratch=[((images.shape[0] * pix_here, wide), F32)],
        )
    else:
        grad_pixels = rows[0].reshape(dp_count * batch, pix_here, half)
    return (output, grad_pixels, *results)


def solution(mesh):
    rows, cols, batch = P("dp", "chan"), P(None, "chan"), P("dp", None, "chan")
    weights = (rows, rows, rows, cols)
    in_specs = (P(None, "dp", None), P("dp", None), batch) + weights * 3
    out_specs = (batch, P(None, "dp", "chan")) + (rows,) * 9 + (cols,) * 3
    return jax.shard_map(
        per_device, mesh=mesh, in_specs=in_specs, out_specs=out_specs, check_vma=False
    )
```

```python
import jax
import jax.numpy as jnp
from jax import lax
from jax.experimental import pallas as pl
from jax.experimental.pallas import tpu as pltpu
from jax.sharding import PartitionSpec as P

BF = jnp.bfloat16
F32 = jnp.float32

epsilon = 1e-05
learn_rate = 0.4
trust_coef = 0.5
momentum = 0.5
avg_decay = 0.6
weight_decay = 5e-05
tiny_term = 1e-06

SIDE = 8
TAIL = 16
RING = [0, 2, 4, 6, 7, 5, 3, 1]


class whole:
    loose = 0
    direct = False

    def __init__(self, array):
        self.arrays, self.dims, self.dtype = [array], array.shape, array.dtype

    def copies(self):
        return len(self.arrays)

    def plan(self, refs, local):
        return [(refs[0], local)]


class fresh(whole):
    loose = 1
    direct = True

    def copies(self):
        return 0

    def plan(self, refs, local):
        return []


class stack(whole):
    def __init__(self, arrays, slot, loose=0):
        self.arrays, self.dtype, self.loose = list(arrays), arrays[0].dtype, loose
        self.dims, self.slot = (len(arrays),) + arrays[0].shape, slot

    def plan(self, refs, local):
        return [(ref, local.at[self.slot(k)]) for k, ref in enumerate(refs)]


class pick(whole):
    def __init__(self, array, index):
        self.arrays, self.dtype, self.index = [array], array.dtype, index
        self.dims = array.shape[1:]

    def plan(self, refs, local):
        return [(refs[0].at[self.index()], local)]


class spread(whole):
    def __init__(self, array, order, first, rows):
        self.arrays, self.dtype, self.order = [array], array.dtype, order
        self.first, self.rows = first, rows
        self.dims = (array.shape[0], rows) + array.shape[2:]

    def copies(self):
        return self.dims[0]

    def plan(self, refs, local):
        cut = pl.ds(self.first, self.rows)
        return [(refs[0].at[k, cut], local.at[place()]) for k, place in enumerate(self.order)]


class stack_rows(stack):
    def __init__(self, arrays, slot, first, rows, loose=0):
        super().__init__(arrays, slot, loose)
        self.cut = pl.ds(first, rows)
        self.dims = self.dims[:2] + (rows,) + self.dims[3:]

    def plan(self, refs, local):
        return [(ref.at[:, self.cut], local.at[self.slot(k)]) for k, ref in enumerate(refs)]


class quarter(whole):
    def __init__(self, images, groups, count):
        self.arrays, self.dtype = [images], images.dtype
        self.per, self.count = images.shape[0] // groups, count
        self.dims = (groups, count) + images.shape[1:]

    def copies(self):
        return self.dims[0]

    def plan(self, refs, local):
        mine = lax.axis_index("chan") * self.count
        return [
            (refs[0].at[pl.ds(g * self.per + mine, self.count)], local.at[g])
            for g in range(self.dims[0])
        ]


class even_phase(stack):
    def __init__(self, arrays, slot):
        super().__init__(arrays, slot)
        self.lanes = arrays[0].shape[3] // 2
        self.dims = (len(arrays), arrays[0].shape[0], arrays[0].shape[2], self.lanes)

    def plan(self, refs, local):
        lanes = pl.ds(0, self.lanes)
        return [(ref.at[:, 0, :, lanes], local.at[self.slot(k)]) for k, ref in enumerate(refs)]


class result:
    pinned = True

    def __init__(self, dims, dtype=F32, pinned=True):
        self.dims, self.dtype, self.pinned = tuple(dims), dtype, pinned
        self.outs = [jax.ShapeDtypeStruct(self.dims, dtype)]

    def copies(self):
        return len(self.outs)

    def plan(self, local, refs):
        return [(local, refs[0])]


class split(result):
    def __init__(self, slots, dims, dtype=F32, part=None):
        self.dims, self.dtype, self.slots = tuple(dims), dtype, slots
        self.outs = [jax.ShapeDtypeStruct(self.dims[1:], dtype) for _ in slots]

    def plan(self, local, refs):
        return [(local.at[slot()], ref) for slot, ref in zip(self.slots, refs)]


class parts_of(result):
    dims = None

    def __init__(self, source, slots, count, first, rows, array):
        self.source, self.slots, self.count, self.cut = source, slots, count, pl.ds(first, rows)
        dims = (count, rows) + array.shape[2:]
        self.outs = [jax.ShapeDtypeStruct(dims, array.dtype) for _ in slots]

    def plan(self, local, refs):
        return [
            (local.at[pl.ds(slot(), self.count), self.cut], ref)
            for slot, ref in zip(self.slots, refs)
        ]


class Taken:
    def __init__(self, local, copies):
        self.local, self.copies, self.waited = local, copies, False

    def ref(self):
        if not self.waited:
            for copy in self.copies:
                copy.wait()
            self.waited = True
        return self.local

    def __getitem__(self, index):
        return self.ref()[index]

    @property
    def shape(self):
        return self.local.shape


class Given:
    def __init__(self, local, copies):
        self.local, self.copies, self.sent = local, copies, False

    def send(self):
        if not self.sent:
            for copy in self.copies:
                copy.start()
            self.sent = True

    def __setitem__(self, index, value):
        self.local[index] = value

    @property
    def shape(self):
        return self.local.shape


def call(body, takes, gives, scratch=(), flops=0, limit=40, later=()):
    takes = [t if isinstance(t, whole) else whole(t) for t in takes]
    arrays = [a for t in takes for a in t.arrays]
    spec = pl.BlockSpec(memory_space=pltpu.HBM)
    loose, vmem = pl.BlockSpec(memory_space=pl.ANY), pl.BlockSpec(memory_space=pltpu.VMEM)
    pinned = [False] * len(later)
    in_specs = [loose] * len(later)
    for t in takes:
        pinned += [True] * (len(t.arrays) - t.loose) + [False] * t.loose
        in_specs += [spec] * (len(t.arrays) - t.loose) + [vmem if t.direct else loose] * t.loose
    outs = [o for g in gives for o in g.outs]
    n_later, n_in, n_out = len(later), len(arrays), len(outs)
    n_copies = sum(t.copies() for t in takes) + sum(g.copies() for g in gives if g.pinned)

    def kernel(*refs):
        refs = refs[n_later:]
        ins, res = list(refs[:n_in]), list(refs[n_in : n_in + n_out])
        local = list(refs[n_in + n_out : -1])
        sems = refs[-1]
        used = 0
        taken, given = [], []
        for t in takes:
            mine, ins = ins[: len(t.arrays)], ins[len(t.arrays) :]
            place = mine[0] if t.direct else local.pop(0)
            copies = []
            for a, b in t.plan(mine, place):
                copies.append(pltpu.make_async_copy(a, b, sems.at[used]))
                used += 1
            for copy in copies:
                copy.start()
            taken.append(Taken(place, copies))
        for g in gives:
            mine, res = res[: len(g.outs)], res[len(g.outs) :]
            if g.dims is None:
                place = taken[g.source].local
            else:
                place = local.pop(0) if g.pinned else mine[0]
            copies = []
            for a, b in g.plan(place, mine) if g.pinned else ():
                copies.append(pltpu.make_async_copy(a, b, sems.at[used]))
                used += 1
            given.append(Given(place, copies))
        body(*taken, *given, *local)
        for t in taken:
            t.ref()
        for g in given:
            g.send()
        for g in given:
            for copy in g.copies:
                copy.wait()

    moved = sum(a.size * a.dtype.itemsize for a in arrays + outs)
    operands = [
        pltpu.with_memory_space_constraint(a, pltpu.HBM) if pin else a
        for a, pin in zip([*later, *arrays], pinned)
    ]
    values = pl.pallas_call(
        kernel,
        out_shape=[pltpu.HBM(o.shape, o.dtype) if g.pinned else o for g in gives for o in g.outs],
        in_specs=in_specs,
        out_specs=[spec if g.pinned else vmem for g in gives for _ in g.outs],
        scratch_shapes=[pltpu.VMEM(t.dims, t.dtype) for t in takes if not t.direct]
        + [pltpu.VMEM(g.dims, g.dtype) for g in gives if g.dims is not None and g.pinned]
        + [pltpu.VMEM(dims, dtype) for dims, dtype in scratch]
        + [pltpu.SemaphoreType.DMA((n_copies,))],
        compiler_params=pltpu.CompilerParams(vmem_limit_bytes=limit * 2**20),
        cost_estimate=pl.CostEstimate(flops=flops, bytes_accessed=moved, transcendentals=0),
        name=body.__name__,
    )(*operands)
    return list(values)


def dot(a, b):
    return jnp.dot(a, b, preferred_element_type=F32)


def dot_nt(a, b):
    return lax.dot_general(a, b, (((1,), (1,)), ((), ())), preferred_element_type=F32)


def dot_tn(a, b):
    return lax.dot_general(a, b, (((0,), (0,)), ((), ())), preferred_element_type=F32)


def shift_col(x, step):
    rows, lanes = x.shape
    grouped = x.reshape(rows // SIDE, SIDE, lanes)
    rolled = pltpu.roll(grouped, step % SIDE, 1)
    col = lax.broadcasted_iota(jnp.int32, grouped.shape, 1)
    edge = 0 if step > 0 else SIDE - 1
    return jnp.where(col == edge, 0.0, rolled).reshape(rows, lanes)


def shift_row(x, step):
    part = x.shape[0] // SIDE
    blank = jnp.zeros((part, x.shape[1]), x.dtype)
    if step > 0:
        return jnp.concatenate([blank, x[:-part]], axis=0)
    return jnp.concatenate([x[part:], blank], axis=0)


def swap_orders(x, batch):
    pieces = [
        x[(b * SIDE + r) * SIDE : (b * SIDE + r + 1) * SIDE] for r in range(SIDE) for b in range(batch)
    ]
    return jnp.concatenate(pieces, axis=0)


def swap_back(x, batch):
    pieces = [
        x[(r * batch + b) * SIDE : (r * batch + b + 1) * SIDE] for b in range(batch) for r in range(SIDE)
    ]
    return jnp.concatenate(pieces, axis=0)


def col_sum(x):
    return jnp.sum(x, axis=0, keepdims=True)


def lane_sum(x):
    return jnp.sum(col_sum(x), axis=1, keepdims=True)


def rows_of(*rows):
    pad = SIDE - sum(row.shape[0] for row in rows)
    tail = [jnp.zeros((pad, rows[0].shape[1]), F32)] if pad else []
    return jnp.concatenate(list(rows) + tail, axis=0)


def spread_rows(out, rows):
    out[...] = jnp.broadcast_to(rows[None, : out.shape[1]], out.shape)


def mean_inverse(total, squares, count):
    center = total / count
    spread = squares / count - center * center
    return center, lax.rsqrt(spread + epsilon)


def slope(v):
    sigma = jax.nn.sigmoid(v)
    return sigma * (1.0 + v * (1.0 - sigma))


def three_rows(values):
    high = values.astype(BF).astype(F32)
    rest = values - high
    middle = rest.astype(BF).astype(F32)
    low = rest - middle
    blank = jnp.zeros((TAIL - 3 * values.shape[0], values.shape[1]), F32)
    return jnp.concatenate([high, middle, low, blank], axis=0).astype(BF)


def one_row(parts, count):
    parts = parts.astype(F32)
    return parts[:count] + parts[count : 2 * count] + parts[2 * count : 3 * count]


def add_up(pieces):
    total = pieces[0].astype(F32)
    for piece in pieces[1:]:
        total = total + piece.astype(F32)
    return total


def expand_mask(inside):
    images, wide = inside.shape
    dims = (images, SIDE, wide)
    lane = lax.broadcasted_iota(jnp.int32, dims, 2)
    col = lax.broadcasted_iota(jnp.int32, dims, 1)
    picked = jnp.where(lane == col, jnp.broadcast_to(inside[:, None, :], dims), 0.0)
    return jnp.broadcast_to(jnp.sum(picked, axis=2, keepdims=True), dims).reshape(-1, wide)


def widen(mask, wide):
    return jnp.concatenate(
        [mask, jnp.zeros((mask.shape[0], wide - mask.shape[1]), mask.dtype)], axis=1
    )


def lane_row(x):
    return col_sum(x * x)


def pack_weights(w, p, w_next, out, rows):
    depth = p.shape[0]
    w_ref, next_ref = w.ref(), w_next.ref()
    pieces = [w_ref[pl.ds(tap, depth, stride=9), :] for tap in range(9)] + [p[...]]
    depth = w_next.shape[0] // 9
    pieces += [next_ref[pl.ds(tap, depth, stride=9), :] for tap in range(9)]
    out[...] = jnp.concatenate(pieces, axis=0).astype(BF)
    out.send()
    rows[...] = rows_of(lane_row(w[...]), lane_row(p[...]), lane_row(w_next[...]))


def pack_images(images, mask, out, valid_out, scratch):
    groups, count, pix, lanes = images.shape
    wide = valid_out.shape[1]
    half = groups * count * pix // 2
    for k in range(lanes // wide):
        cut = slice(k * wide, (k + 1) * wide)
        scratch[k] = images[:, :, :, cut].astype(F32).reshape(2 * half, wide)
        for col in range(2):
            taken = scratch[k, pl.ds(col, half, stride=2), :].reshape(groups, count, 2, SIDE, wide)
            for row in range(2):
                rows = jnp.concatenate([taken[:, i, row] for i in range(count)], axis=1)
                start = col * lanes + k * wide
                out[:, row, :, start : start + wide] = rows.astype(BF)
    out.send()
    inside = widen(mask[...].astype(F32), wide)
    part = inside.shape[0] * SIDE
    for row in range(SIDE):
        turned = pltpu.roll(inside, (wide - SIDE * row) % wide, 1)
        valid_out[row * part : (row + 1) * part] = expand_mask(turned)


def tap_major(w):
    return w.reshape(-1, 9, w.shape[1]).transpose(1, 0, 2)


def taps_of(w, depth, first=0):
    def taps(*which):
        starts = [first + t * depth for t in which]
        return jnp.concatenate(
            [w[:, a : a + depth].reshape(-1, w.shape[2]) for a in starts], axis=1
        )

    return taps


def phase_of(x, row, col):
    lanes = x.shape[4] // 2
    cut = slice(col * lanes, (col + 1) * lanes)
    pieces = [x[k, r, row, :, cut] for r in range(x.shape[1]) for k in range(x.shape[0])]
    return jnp.concatenate(pieces, axis=0)


def conv_first(w, x, m, n, zb_out, zp_out, sums_out, pay):
    taps = taps_of(w, w.shape[1] // 10)
    wide = w.shape[2]
    y00 = dot(phase_of(x, 0, 0), taps(4, 9))
    y01 = dot(phase_of(x, 0, 1), taps(5, 3))
    y10 = dot(phase_of(x, 1, 0), taps(7, 1))
    y11 = dot(phase_of(x, 1, 1), taps(8, 6, 2, 0))
    here = y00[:, :wide] + y01[:, :wide] + y10[:, :wide] + y11[:, :wide]
    left = y01[:, wide:] + y11[:, wide : 2 * wide]
    above = y10[:, wide:] + y11[:, 2 * wide : 3 * wide]
    corner = y11[:, 3 * wide :]
    z = here + shift_row(above, 1) + shift_col(left + shift_row(corner, 1), 1)
    pix = z.shape[0]
    zb_out[:pix] = z.astype(BF)
    zb_out[pix:] = three_rows(n[0:2])
    zb_out.send()
    zp = y00[:, wide:]
    valid = m[...]
    vz, vzp = valid * z, valid * zp
    spread_rows(pay, rows_of(col_sum(vz), col_sum(vz * z), col_sum(valid)))
    pay.send()
    sums_out[...] = rows_of(col_sum(vzp), col_sum(vzp * zp))
    zp_out[...] = zp


def hand_on(w, *outs):
    w.ref()


def first_norm(z, rows):
    count = rows[2:3]
    center, inverse = mean_inverse(rows[0:1], rows[1:2], count)
    hat = (z - center) * inverse
    return hat, hat * rows[3:4] + rows[4:5], inverse


def conv_second(z, got, m, w, zp, sums, cot, h_out, z2_out, pay, tot_out, m_out, zp_out, cot_out, own_out):
    blocks, wide = z.shape[0], z.shape[2]
    valid = m[...]
    pix = valid.shape[0]
    hidden = []
    for k in range(blocks):
        rows = rows_of(jnp.sum(got[:, k], axis=0)[0:3], one_row(z[k, pix:], 2))
        tot_out[k] = rows
        _, lin, _ = first_norm(z[k, :pix].astype(F32), rows)
        hidden.append((lin * jax.nn.sigmoid(lin) * valid).astype(BF))
        h_out[:, k * wide : (k + 1) * wide] = hidden[-1]
    h_out.send()
    hidden = jnp.concatenate(hidden, axis=1)
    taps = taps_of(w, hidden.shape[1] // w.shape[0])
    moved = []
    for col in range(3):
        y = dot(hidden, taps(col, 3 + col, 6 + col))
        moved.append(
            shift_row(y[:, :wide], 1) + y[:, wide : 2 * wide] + shift_row(y[:, 2 * wide :], -1)
        )
    z2 = moved[1] + shift_col(moved[0], 1) + shift_col(moved[2], -1)
    vz = valid * z2
    spread_rows(pay, rows_of(col_sum(vz), col_sum(vz * z2), sums[0:2]))
    pay.send()
    z2_out[...] = z2
    batch, pix, wide = cot.shape
    m_out[...] = valid
    zp_out[...] = zp[...]
    cot_out[...] = swap_orders(cot[...].astype(F32).reshape(batch * pix, wide), batch)
    own_out[...] = tot_out.local[pl.ds(lax.axis_index("chan"), 1)][0]


def block_output(z2, zp, got, tot1, m, n, cot, out, e_out, hat2_out, hat_p_out, rows_out, pay):
    total, count = jnp.sum(got[...], axis=0), tot1[2:3]
    center2, inverse2 = mean_inverse(total[0:1], total[1:2], count)
    center_p, inverse_p = mean_inverse(total[2:3], total[3:4], count)
    hat2, hat_p = (z2[...] - center2) * inverse2, (zp[...] - center_p) * inverse_p
    hat2_out[...] = hat2
    hat_p_out[...] = hat_p
    rows_out[...] = rows_of(n[2:3] * inverse2, n[4:5] * inverse_p, count)
    summed = hat2 * n[2:3] + n[3:4] + (hat_p * n[4:5] + n[5:6])
    sigma = jax.nn.sigmoid(summed)
    valid = m[...]
    batch, pix, wide = out.shape
    e = cot[...] * valid * (sigma * (1.0 + summed * (1.0 - sigma)))
    spread_rows(pay, rows_of(col_sum(e), col_sum(e * hat2), col_sum(e * hat_p)))
    pay.send()
    e_out[...] = e
    out[...] = swap_back(summed * sigma * valid, batch).astype(BF).reshape(out.shape)


def grad_outputs(e, hat2, hat_p, rows, got, m, g2_out, gp_out, tot_out):
    back, count = jnp.sum(got[...], axis=0), rows[2:3]
    tot_out[...] = rows_of(back)
    valid, e = m[...], e[...]
    loss = valid * ((back[0:1] + hat2[...] * back[1:2]) / count)
    g2_out[...] = (rows[0:1] * (e - loss)).astype(BF)
    g2_out.send()
    loss = valid * ((back[0:1] + hat_p[...] * back[2:3]) / count)
    gp_out[...] = (rows[1:2] * (e - loss)).astype(BF)


def grad_hidden(w, g2, z, gp, tot1, m, b_out, msg, pay):
    blocks, _, wide = g2.shape
    count, part = w.shape[1], w.shape[2] // 9
    depth = count * part
    moved = []
    grads = jnp.concatenate([g2[k] for k in range(blocks)], axis=1)
    for col in range(3):
        starts = [(3 * row + col) * part for row in range(3)]
        taps = [
            jnp.concatenate([w[k, :, a : a + part].reshape(depth, wide) for k in range(blocks)], axis=1)
            for a in starts
        ]
        y = dot_nt(grads, jnp.concatenate(taps, axis=0))
        moved.append(
            shift_row(y[:, :depth], -1) + y[:, depth : 2 * depth] + shift_row(y[:, 2 * depth :], 1)
        )
    gh = moved[1] + shift_col(moved[0], -1) + shift_col(moved[2], 1)
    valid = m[...]
    hat, lin, _ = first_norm(z[: valid.shape[0]].astype(F32), tot1[...])
    b = gh * (slope(lin) * valid)
    shift, scaled = col_sum(b), col_sum(b * hat)
    spread_rows(pay, rows_of(shift, scaled))
    pay.send()
    here = col_sum(valid)
    shift, scaled = shift / here, scaled / here
    pix = b.shape[0]
    msg[:pix] = (b - valid * (shift + hat * scaled)).astype(BF)
    msg[pix : 2 * pix] = gp[...]
    msg[2 * pix :] = three_rows(jnp.concatenate([shift, scaled], axis=0))
    msg.send()
    b_out[...] = b


def make_grad_second(on_ring):
    def grad_second(h, g2, x, gp, g_out):
        groups, rows, wide = g_out.shape
        places = list(range(groups))
        if on_ring:
            last, turn = len(RING) - 1, turn_round()
            places = [RING.index(k) for k in places]
            places = [p + turn * (last - 2 * p) for p in places]
        share = h.shape[1] // groups
        h, g2 = h[...], g2[...].astype(F32)
        moved = [shift_col(g2, step).astype(BF) if step else g2.astype(BF) for step in (-1, 0, 1)]

        def put(rows, g):
            g = g.astype(BF).reshape(groups, -1, wide)
            for k, place in enumerate(places):
                g_out[place, rows] = g[k]

        spread_out = []
        for tap in range(9):
            step = tap // 3 - 1
            spread_out.append(shift_row(moved[tap % 3], step) if step else moved[tap % 3])
        spread_out = dot_tn(h, jnp.concatenate(spread_out, axis=1))
        for tap in range(9):
            g = spread_out[:, tap * wide : (tap + 1) * wide]
            put(slice(tap * share, (tap + 1) * share), g)
        pieces = [x[k, r] for r in range(SIDE) for k in range(x.shape[0])]
        put(slice(9 * share, rows), dot_tn(jnp.concatenate(pieces, axis=0), gp[...]))

    return grad_second


def grad_first(b, z, got, tot1, n, m, x, blocks_out, tot_out):
    own = got[:, pl.ds(lax.axis_index("chan"), 1)]
    back, count = jnp.sum(own, axis=0)[0], tot1[2:3]
    tot_out[...] = rows_of(back)
    hat, _, inverse = first_norm(z[: m.shape[0]].astype(F32), tot1[...])
    g = n[0:1] * inverse * (b[...] - m[...] * ((back[0:1] + hat * back[1:2]) / count))
    here, left = g.astype(BF), shift_col(g, -1).astype(BF)
    wide = here.shape[1]
    groups = blocks_out.shape[0]
    share = x.shape[4] // 2 // groups

    def put(tap, grad):
        rows = grad.astype(BF).reshape(groups, share, wide)
        blocks_out[:, tap * share : (tap + 1) * share] = rows

    above, corner = shift_row(here, -1), shift_row(left, -1)
    for row, col, pairs in (
        (0, 0, ((4, here),)),
        (0, 1, ((5, here), (3, left))),
        (1, 0, ((7, here), (1, above))),
        (1, 1, ((8, here), (6, left), (2, above), (0, corner))),
    ):
        both = jnp.concatenate([grad for _, grad in pairs], axis=1)
        both = dot_tn(phase_of(x, row, col), both)
        for place, (tap, _) in enumerate(pairs):
            put(tap, both[:, place * wide : (place + 1) * wide])


def grad_images(msg, z, got, tot1, m, w, out):
    blocks, count = w.shape[0], w.shape[1]
    depth = w.shape[2] // 10
    half, wide = count * depth, w.shape[3]

    def taps(*which):
        blocks_of = [
            [w[k, :, t * depth : (t + 1) * depth].reshape(half, wide) for k in range(blocks)]
            for t in which
        ]
        return jnp.concatenate([jnp.concatenate(row, axis=1) for row in blocks_of], axis=0)

    grads = []
    valid = m[...]
    pix = valid.shape[0]
    for k in range(blocks):
        rows, back = tot1[k], jnp.sum(got[:, k], axis=0)
        hat, _, inverse = first_norm(z[k, :pix].astype(F32), rows)
        fit = back[0:2] / rows[2:3] - one_row(msg[k, 2 * pix :], 2)
        loss = valid * (fit[0:1] + hat * fit[1:2])
        grads.append((rows[3:4] * inverse * (msg[k, :pix].astype(F32) - loss)).astype(BF))
    grads = jnp.concatenate(grads, axis=1)
    plain, moved = dot_nt(grads, taps(4, 5, 7, 8, 1, 2)), dot_nt(grads, taps(3, 3, 6, 6, 0, 0))
    proj = jnp.concatenate([msg[k, pix : 2 * pix] for k in range(blocks)], axis=1)
    proj = dot_nt(proj, taps(9, 9))
    lane = lax.broadcasted_iota(jnp.int32, moved.shape, 1) % (2 * half)
    total = plain + jnp.where(lane >= half, shift_col(moved, -1), 0.0)
    lane = lax.broadcasted_iota(jnp.int32, proj.shape, 1)
    even = total[:, : 2 * half] + jnp.where(lane < half, proj, 0.0)
    odd = total[:, 2 * half : 4 * half] + shift_row(total[:, 4 * half :], -1)
    for row, value in enumerate((even, odd)):
        out[:, row] = value.astype(BF).reshape(out.shape[0], -1, 2 * half)


def finish_images(x, out, scratch):
    images, pix, half = out.shape
    groups, _, part, wide = x.shape
    count = part // SIDE
    value = x[...].astype(F32).reshape(groups, 2, count, 1, SIDE, wide)
    value = jnp.concatenate([value[:, 0], value[:, 1]], axis=2)
    rows = images * pix // 2
    value = value.reshape(rows, wide)
    scratch[pl.ds(0, rows, stride=2), :] = value
    scratch[pl.ds(1, rows, stride=2), :] = pltpu.roll(value, half, 1)
    out[...] = scratch[...][:, :half].astype(BF).reshape(out.shape)


def put_rows(out, total):
    depth = out.shape[0] // 9
    for tap in range(9):
        out.local[pl.ds(tap, depth, stride=9), :] = total[tap * depth : (tap + 1) * depth]


def reduce_all(second, x, sw, t3, t4, n, g1_out, g2_out, gp_out, pay):
    second = second[...].astype(F32)
    cut = g2_out.shape[0]
    conv, proj = second[:cut], second[cut:]
    parts = [lane_row(conv), lane_row(proj)]
    first = add_up([x[k] for k in range(x.shape[0])])
    rows = [sw[0:1], lane_row(first), sw[2:3], parts[0], sw[1:2], parts[1]]
    nw, gn = n[...], norm_grad(t3, t4)
    blank = jnp.zeros((2, nw.shape[1]), F32)
    cols = [
        jnp.sum(jnp.concatenate(rows + [blank], axis=0), axis=1, keepdims=True),
        jnp.sum(jnp.concatenate([nw * nw, blank], axis=0), axis=1, keepdims=True),
        jnp.sum(jnp.concatenate([gn * gn, blank], axis=0), axis=1, keepdims=True),
    ]
    dims = (SIDE, pay.shape[2])
    lane, row = (lax.broadcasted_iota(jnp.int32, dims, axis) for axis in (1, 0))
    block = jnp.zeros(dims, F32)
    for place, col in enumerate(cols):
        block = jnp.where(lane == SIDE * place + row, col, block)
    spread_rows(pay, col_sum(block))
    pay.send()
    gp_out[...] = proj
    put_rows(g2_out, conv)
    g2_out.send()
    put_rows(g1_out, first)


def norm_grad(t3, t4):
    return jnp.concatenate([t4[1:2], t4[0:1], t3[1:2], t3[0:1], t3[2:3], t3[0:1]], axis=0)


def step_of(w, g, m, a, weight_sq, grad_sq):
    weight_len = jnp.sqrt(weight_sq)
    trust = trust_coef * weight_len / (jnp.sqrt(grad_sq) + weight_decay * weight_len + tiny_term)
    step = trust * (g + weight_decay * w)
    m_new = momentum * m + step
    w_new = w - learn_rate * (step + momentum * m_new)
    return w_new, m_new, avg_decay * a + (1.0 - avg_decay) * w_new


def make_update(dp_count):
    def update(*refs):
        r6, t3, t4 = refs[:3]
        ins, outs = refs[3:18], refs[18:]
        total = jnp.broadcast_to(jnp.sum(r6[...], axis=0), (SIDE, r6.shape[2]))
        lane, row = (lax.broadcasted_iota(jnp.int32, total.shape, axis) for axis in (1, 0))
        total = [
            jnp.sum(jnp.where(lane == SIDE * k + row, total, 0.0), axis=1, keepdims=True)
            for k in range(3)
        ]
        for place in range(3):
            w, g, m, a = (ref[...] for ref in ins[4 * place : 4 * place + 4])
            weight_sq = total[0][2 * place : 2 * place + 1]
            grad_sq = total[0][2 * place + 1 : 2 * place + 2]
            for ref, value in zip(outs[3 * place :], step_of(w, g, m, a, weight_sq, grad_sq)):
                ref[...] = value
                ref.send()
        w, m, a = (ref[...] for ref in ins[12:15])
        weight_sq, grad_sq = total[1][0:6] / dp_count, total[2][0:6] / dp_count
        g = norm_grad(t3, t4)
        for ref, value in zip(outs[9:], step_of(w, g, m, a, weight_sq, grad_sq)):
            ref[...] = value

    return update


def exchange(blocks, axes):
    return lax.all_to_all(blocks, axes, 0, 0)


def rings():
    count = lax.axis_size("chan")
    return [[(d ^ (c % 2)) * count + c for d in RING] for c in range(count)]


def turn_round():
    return lax.axis_index("chan") % 2


def swap(array, axis, bits):
    return lax.ppermute(array, axis, [(i, i ^ bits) for i in range(lax.axis_size(axis))])


def away(axis, k):
    return lambda: lax.axis_index(axis) ^ k


def in_groups(taps, groups):
    return taps.reshape(taps.shape[0], groups, -1, taps.shape[2]).transpose(1, 0, 2, 3)


def regroup(blocks, taps, groups):
    blocks = blocks.reshape(blocks.shape[0], taps, -1, blocks.shape[2]).transpose(1, 0, 2, 3)
    blocks = in_groups(blocks.reshape(taps, -1, blocks.shape[3]), groups)
    return blocks.reshape(groups, -1, blocks.shape[3])


def per_device(
    images, mask, cotangent, w_first, w_second, w_proj, norm_params, mom_first, mom_second,
    mom_proj, mom_norm, avg_first, avg_second, avg_proj, avg_norm,
):
    everyone = ("dp", "chan")
    dp_count, ch_count = lax.axis_size("dp"), lax.axis_size("chan")
    n_all = dp_count * ch_count
    batch = mask.shape[0]
    pix_here, d_in = images.shape[1], images.shape[2]
    wide = w_first.shape[1]
    d_out = wide * ch_count
    part = batch * SIDE
    pix = SIDE * part
    share = batch // ch_count
    eight = dp_count == SIDE and pix_here == 4 * SIDE
    groups = SIDE
    first_rows, second_rows = 10 * d_in // groups, 9 * d_out // groups
    square_rows = result((SIDE, wide))
    four = result((dp_count, 4, wide), pinned=False)
    passing, few = (result((n, wide), pinned=False) for n in (pix, SIDE))

    def slot_dp(k):
        return lax.axis_index("dp") ^ k

    def slot_ch(k):
        return lax.axis_index("chan") ^ k

    def share_out(own):
        far = swap(own, "chan", 2)
        return [own, swap(own, "chan", 1), far, swap(far, "chan", 1)]

    if eight:
        own, squares = call(
            pack_weights,
            [w_first, w_proj, w_second],
            [result((first_rows + second_rows, wide), BF), square_rows],
        )
        gathered = lax.all_gather(own, everyone, axis_index_groups=rings())
        order = [lambda d=d: d ^ turn_round() for d in RING]
        mine, valid = call(
            pack_images,
            [quarter(images, dp_count, share), mask],
            [result((dp_count, 2, share * SIDE, 2 * d_in), BF), result((pix, wide))],
            scratch=[((d_in // wide, dp_count * share * pix_here, wide), F32)],
            later=[own],
        )
        pixels, slot = share_out(exchange(mine, "dp")), slot_ch
    else:
        valid = mask.reshape(batch, SIDE, SIDE).transpose(1, 0, 2).reshape(pix, 1).astype(F32)
        valid = jnp.broadcast_to(valid, (pix, wide))
        own = jnp.concatenate([tap_major(w_first), w_proj[None]], axis=0).astype(BF)
        own = lax.all_gather(own, "dp", axis=1, tiled=True)
        next = lax.all_gather(tap_major(w_second).astype(BF), "dp", axis=1, tiled=True)
        gathered = [in_groups(taps, groups).reshape(groups, -1, wide) for taps in (own, next)]
        gathered = jnp.concatenate(gathered, axis=1)
        order = [lambda g=g: g for g in range(groups)]
        squares = [jnp.sum(w * w, axis=0) for w in (w_first, w_proj, w_second)]
        squares = jnp.zeros((SIDE, wide), F32).at[:3].set(jnp.stack(squares))
        mine = images.reshape(dp_count, ch_count, share, pix_here, d_in)
        mine = lax.dynamic_index_in_dim(mine, lax.axis_index("chan"), 1, keepdims=False)
        pixels = lax.all_gather(exchange(mine, "dp"), "chan")
        cols = pix_here // 2
        pixels = pixels.reshape(ch_count, SIDE, 2, SIDE // cols, share, cols, 2 * d_in)
        pixels = pixels.transpose(0, 1, 2, 4, 3, 5, 6)
        pixels = pixels.reshape(ch_count, SIDE, 2, share * SIDE, 2 * d_in)
        pixels, slot = [pixels[k] for k in range(ch_count)], lambda k: k

    macs = pix * 9 * wide * d_in
    per_block = groups // ch_count
    block_slots = [lambda k=k: (lax.axis_index("chan") ^ k) * per_block for k in range(ch_count)]
    z_own, z_proj, sums_proj, pay = call(
        conv_first,
        [spread(gathered, order, 0, first_rows), stack(pixels, slot), valid, norm_params],
        [
            result((pix + TAIL, wide), BF),
            result((pix, wide)),
            square_rows,
            result((n_all, 4, wide)),
        ],
        flops=2 * macs,
    )
    turned = call(
        hand_on,
        [spread(gathered, order, 0, first_rows + second_rows)],
        [parts_of(0, block_slots, per_block, 0, first_rows + second_rows, gathered)],
        later=[z_own],
    )
    got1 = exchange(pay, everyone).reshape(dp_count, ch_count, 4, wide)
    z_all = [swap(z_own, "chan", k) for k in range(1, ch_count)]
    got1, *both = lax.optimization_barrier((got1, *z_all, *turned))
    z_all, turned = [z_own, *both[: ch_count - 1]], both[ch_count - 1 :]

    hidden, z_second, pay, total1, *near = call(
        conv_second,
        [
            stack(z_all, slot_ch, 3),
            fresh(got1),
            valid,
            spread(gathered, order, first_rows, second_rows),
            z_proj,
            sums_proj,
            cotangent,
        ],
        [
            result((pix, d_out), BF, pinned=False),
            passing,
            four,
            result((ch_count, SIDE, wide)),
            passing,
            passing,
            passing,
            few,
        ],
        flops=4 * macs,
    )
    turned = turned[:1] + [swap(block, "chan", k) for k, block in enumerate(turned) if k]
    total1_own = pick(total1, away("chan", 0))
    got2 = exchange(pay, "dp")
    near_valid, near_proj, near_cot, near_total = (fresh(array) for array in near)
    output, e, hat_second, hat_proj, near_rows, pay = call(
        block_output,
        [fresh(z_second), near_proj, fresh(got2), near_total, near_valid, norm_params, near_cot],
        [result((batch, SIDE * SIDE, wide), BF), passing, passing, passing, few, four],
    )
    got3 = exchange(pay, "dp")

    g_second_out, g_proj_out, total3 = call(
        grad_outputs,
        [fresh(e), fresh(hat_second), fresh(hat_proj), fresh(near_rows), fresh(got3), near_valid],
        [result((pix, wide), BF), result((pix, wide), BF), square_rows],
        later=turned[1:],
    )
    rows = second_rows + d_in // groups
    (grads,) = call(
        make_grad_second(eight),
        [fresh(hidden), g_second_out, even_phase(pixels, slot), g_proj_out],
        [result((groups, rows, wide), BF)],
        flops=4 * macs,
    )
    far = swap(g_second_out, "chan", 2)
    far, grads = lax.optimization_barrier((far, grads))
    g_all = [g_second_out, swap(g_second_out, "chan", 1), far, swap(far, "chan", 1)]
    if eight:
        grads_second = lax.psum_scatter(
            grads.reshape(groups * rows, wide),
            everyone,
            scatter_dimension=0,
            axis_index_groups=rings(),
            tiled=True,
        )
    else:
        grads = [
            regroup(grads[:, :second_rows], 9, dp_count),
            regroup(grads[:, second_rows:], 1, dp_count),
        ]
        grads = jnp.concatenate(grads, axis=1)
        grads_second = jnp.sum(exchange(grads, "dp").astype(F32), axis=0)

    back, msg, pay = call(
        grad_hidden,
        [stack_rows(turned, slot_ch, first_rows, second_rows, 3), stack(g_all, slot_ch, 3)]
        + [z_own, g_proj_out, total1_own, valid],
        [passing, result((2 * pix + TAIL, wide), BF), result((n_all, 2, wide), pinned=False)],
        flops=4 * macs,
    )
    got4 = exchange(pay, everyone).reshape(dp_count, ch_count, 2, wide)
    far = swap(msg, "chan", 2)
    far, got4 = lax.optimization_barrier((far, got4))
    messages = [msg, swap(msg, "chan", 1), far, swap(far, "chan", 1)]

    grads, total4 = call(
        grad_first,
        [fresh(back), z_own, fresh(got4), total1_own, norm_params, valid, stack(pixels, slot)],
        [result((groups, 9 * (d_in // groups), wide), BF), square_rows],
        flops=2 * macs,
    )
    if not eight:
        grads = regroup(grads, 9, dp_count)
    got_first = exchange(grads, "dp")

    half = wide // 2
    takes = [
        stack(messages, slot_ch, 3),
        stack(z_all, slot_ch, 3),
        fresh(got4),
        total1,
        valid,
        stack_rows(turned, slot_ch, 0, first_rows, 3),
    ]
    dims = (SIDE, 2, part, wide)
    if eight:
        rows = call(
            grad_images,
            takes,
            [split([away("dp", k) for k in range(SIDE)], dims, BF)],
            flops=2 * macs,
        )
        rows = rows[:1] + [swap(row, "dp", k) for k, row in enumerate(rows) if k]
    else:
        (rows,) = call(grad_images, takes, [result(dims, BF)], flops=2 * macs)
        cols = pix_here // 2
        rows = rows.reshape(SIDE, 2, batch, SIDE // cols, cols, wide)
        rows = rows.transpose(0, 1, 3, 2, 4, 5).reshape(dp_count, batch, cols, wide)
        rows = [exchange(rows, "dp")]
    reduced_first, reduced_second, reduced_proj, pay = call(
        reduce_all,
        [grads_second, fresh(got_first), squares, total3, total4, norm_params],
        [
            result(w_first.shape),
            result(w_second.shape),
            result(w_proj.shape),
            result((n_all, 1, wide)),
        ],
    )
    pay, *rows = lax.optimization_barrier((pay, *rows))
    got6 = exchange(pay, everyone)

    conv = (
        (w_first, reduced_first, mom_first, avg_first),
        (w_second, reduced_second, mom_second, avg_second),
        (w_proj, reduced_proj, mom_proj, avg_proj),
    )
    results = call(
        make_update(dp_count),
        [fresh(got6), total3, total4, *(array for group in conv for array in group)]
        + [norm_params, mom_norm, avg_norm],
        [result(group[0].shape) for group in conv for _ in range(3)]
        + [result(norm_params.shape)] * 3,
    )
    if eight:
        (grad_pixels,) = call(
            finish_images,
            [stack(rows, slot_dp, 7)],
            [result((images.shape[0], pix_here, half), BF)],
            scratch=[((images.shape[0] * pix_here, wide), F32)],
        )
    else:
        grad_pixels = rows[0].reshape(dp_count * batch, pix_here, half)
    return (output, grad_pixels, *results)


def solution(mesh):
    rows, cols, batch = P("dp", "chan"), P(None, "chan"), P("dp", None, "chan")
    weights = (rows, rows, rows, cols)
    in_specs = (P(None, "dp", None), P("dp", None), batch) + weights * 3
    out_specs = (batch, P(None, "dp", "chan")) + (rows,) * 9 + (cols,) * 3
    return jax.shard_map(
        per_device, mesh=mesh, in_specs=in_specs, out_specs=out_specs, check_vma=False
    )
```

```python
import jax
import jax.numpy as jnp
from jax import lax
from jax.experimental import pallas as pl
from jax.experimental.pallas import tpu as pltpu
from jax.sharding import PartitionSpec as P

BF = jnp.bfloat16
F32 = jnp.float32

epsilon = 1e-05
learn_rate = 0.4
trust_coef = 0.5
momentum = 0.5
avg_decay = 0.6
weight_decay = 5e-05
tiny_term = 1e-06

SIDE = 8
TAIL = 16
RING = [0, 2, 4, 6, 7, 5, 3, 1]


class whole:
    loose = 0
    direct = False

    def __init__(self, array):
        self.arrays, self.dims, self.dtype = [array], array.shape, array.dtype

    def copies(self):
        return len(self.arrays)

    def plan(self, refs, local):
        return [(refs[0], local)]


class fresh(whole):
    loose = 1
    direct = True

    def copies(self):
        return 0

    def plan(self, refs, local):
        return []


class stack(whole):
    def __init__(self, arrays, slot, loose=0):
        self.arrays, self.dtype, self.loose = list(arrays), arrays[0].dtype, loose
        self.dims, self.slot = (len(arrays),) + arrays[0].shape, slot

    def plan(self, refs, local):
        return [(ref, local.at[self.slot(k)]) for k, ref in enumerate(refs)]


class pick(whole):
    def __init__(self, array, index):
        self.arrays, self.dtype, self.index = [array], array.dtype, index
        self.dims = array.shape[1:]

    def plan(self, refs, local):
        return [(refs[0].at[self.index()], local)]


class spread(whole):
    def __init__(self, array, order, first, rows):
        self.arrays, self.dtype, self.order = [array], array.dtype, order
        self.first, self.rows = first, rows
        self.dims = (array.shape[0], rows) + array.shape[2:]

    def copies(self):
        return self.dims[0]

    def plan(self, refs, local):
        cut = pl.ds(self.first, self.rows)
        return [(refs[0].at[k, cut], local.at[place()]) for k, place in enumerate(self.order)]


class stack_rows(stack):
    def __init__(self, arrays, slot, first, rows, loose=0):
        super().__init__(arrays, slot, loose)
        self.cut = pl.ds(first, rows)
        self.dims = self.dims[:2] + (rows,) + self.dims[3:]

    def plan(self, refs, local):
        return [(ref.at[:, self.cut], local.at[self.slot(k)]) for k, ref in enumerate(refs)]


class quarter(whole):
    def __init__(self, images, groups, count):
        self.arrays, self.dtype = [images], images.dtype
        self.per, self.count = images.shape[0] // groups, count
        self.dims = (groups, count) + images.shape[1:]

    def copies(self):
        return self.dims[0]

    def plan(self, refs, local):
        mine = lax.axis_index("chan") * self.count
        return [
            (refs[0].at[pl.ds(g * self.per + mine, self.count)], local.at[g])
            for g in range(self.dims[0])
        ]


class even_phase(stack):
    def __init__(self, arrays, slot):
        super().__init__(arrays, slot)
        self.lanes = arrays[0].shape[3] // 2
        self.dims = (len(arrays), arrays[0].shape[0], arrays[0].shape[2], self.lanes)

    def plan(self, refs, local):
        lanes = pl.ds(0, self.lanes)
        return [(ref.at[:, 0, :, lanes], local.at[self.slot(k)]) for k, ref in enumerate(refs)]


class result:
    pinned = True

    def __init__(self, dims, dtype=F32, pinned=True):
        self.dims, self.dtype, self.pinned = tuple(dims), dtype, pinned
        self.outs = [jax.ShapeDtypeStruct(self.dims, dtype)]

    def copies(self):
        return len(self.outs)

    def plan(self, local, refs):
        return [(local, refs[0])]


class split(result):
    def __init__(self, slots, dims, dtype=F32, part=None):
        self.dims, self.dtype, self.slots = tuple(dims), dtype, slots
        self.outs = [jax.ShapeDtypeStruct(self.dims[1:], dtype) for _ in slots]

    def plan(self, local, refs):
        return [(local.at[slot()], ref) for slot, ref in zip(self.slots, refs)]


class parts_of(result):
    dims = None

    def __init__(self, source, slots, count, first, rows, array):
        self.source, self.slots, self.count, self.cut = source, slots, count, pl.ds(first, rows)
        dims = (count, rows) + array.shape[2:]
        self.outs = [jax.ShapeDtypeStruct(dims, array.dtype) for _ in slots]

    def plan(self, local, refs):
        return [
            (local.at[pl.ds(slot(), self.count), self.cut], ref)
            for slot, ref in zip(self.slots, refs)
        ]


class Taken:
    def __init__(self, local, copies):
        self.local, self.copies, self.waited = local, copies, False

    def ref(self):
        if not self.waited:
            for copy in self.copies:
                copy.wait()
            self.waited = True
        return self.local

    def __getitem__(self, index):
        return self.ref()[index]

    @property
    def shape(self):
        return self.local.shape


class Given:
    def __init__(self, local, copies):
        self.local, self.copies, self.sent = local, copies, False

    def send(self):
        if not self.sent:
            for copy in self.copies:
                copy.start()
            self.sent = True

    def __setitem__(self, index, value):
        self.local[index] = value

    @property
    def shape(self):
        return self.local.shape


def call(body, takes, gives, scratch=(), flops=0, limit=40, later=()):
    takes = [t if isinstance(t, whole) else whole(t) for t in takes]
    arrays = [a for t in takes for a in t.arrays]
    spec = pl.BlockSpec(memory_space=pltpu.HBM)
    loose, vmem = pl.BlockSpec(memory_space=pl.ANY), pl.BlockSpec(memory_space=pltpu.VMEM)
    pinned = [False] * len(later)
    in_specs = [loose] * len(later)
    for t in takes:
        pinned += [True] * (len(t.arrays) - t.loose) + [False] * t.loose
        in_specs += [spec] * (len(t.arrays) - t.loose) + [vmem if t.direct else loose] * t.loose
    outs = [o for g in gives for o in g.outs]
    n_later, n_in, n_out = len(later), len(arrays), len(outs)
    n_copies = sum(t.copies() for t in takes) + sum(g.copies() for g in gives if g.pinned)

    def kernel(*refs):
        refs = refs[n_later:]
        ins, res = list(refs[:n_in]), list(refs[n_in : n_in + n_out])
        local = list(refs[n_in + n_out : -1])
        sems = refs[-1]
        used = 0
        taken, given = [], []
        for t in takes:
            mine, ins = ins[: len(t.arrays)], ins[len(t.arrays) :]
            place = mine[0] if t.direct else local.pop(0)
            copies = []
            for a, b in t.plan(mine, place):
                copies.append(pltpu.make_async_copy(a, b, sems.at[used]))
                used += 1
            for copy in copies:
                copy.start()
            taken.append(Taken(place, copies))
        for g in gives:
            mine, res = res[: len(g.outs)], res[len(g.outs) :]
            if g.dims is None:
                place = taken[g.source].local
            else:
                place = local.pop(0) if g.pinned else mine[0]
            copies = []
            for a, b in g.plan(place, mine) if g.pinned else ():
                copies.append(pltpu.make_async_copy(a, b, sems.at[used]))
                used += 1
            given.append(Given(place, copies))
        body(*taken, *given, *local)
        for t in taken:
            t.ref()
        for g in given:
            g.send()
        for g in given:
            for copy in g.copies:
                copy.wait()

    moved = sum(a.size * a.dtype.itemsize for a in arrays + outs)
    operands = [
        pltpu.with_memory_space_constraint(a, pltpu.HBM) if pin else a
        for a, pin in zip([*later, *arrays], pinned)
    ]
    values = pl.pallas_call(
        kernel,
        out_shape=[pltpu.HBM(o.shape, o.dtype) if g.pinned else o for g in gives for o in g.outs],
        in_specs=in_specs,
        out_specs=[spec if g.pinned else vmem for g in gives for _ in g.outs],
        scratch_shapes=[pltpu.VMEM(t.dims, t.dtype) for t in takes if not t.direct]
        + [pltpu.VMEM(g.dims, g.dtype) for g in gives if g.dims is not None and g.pinned]
        + [pltpu.VMEM(dims, dtype) for dims, dtype in scratch]
        + [pltpu.SemaphoreType.DMA((n_copies,))],
        compiler_params=pltpu.CompilerParams(vmem_limit_bytes=limit * 2**20),
        cost_estimate=pl.CostEstimate(flops=flops, bytes_accessed=moved, transcendentals=0),
        name=body.__name__,
    )(*operands)
    return list(values)


def dot(a, b):
    return jnp.dot(a, b, preferred_element_type=F32)


def dot_nt(a, b):
    return lax.dot_general(a, b, (((1,), (1,)), ((), ())), preferred_element_type=F32)


def dot_tn(a, b):
    return lax.dot_general(a, b, (((0,), (0,)), ((), ())), preferred_element_type=F32)


def shift_col(x, step):
    rows, lanes = x.shape
    grouped = x.reshape(rows // SIDE, SIDE, lanes)
    rolled = pltpu.roll(grouped, step % SIDE, 1)
    col = lax.broadcasted_iota(jnp.int32, grouped.shape, 1)
    edge = 0 if step > 0 else SIDE - 1
    return jnp.where(col == edge, 0.0, rolled).reshape(rows, lanes)


def shift_row(x, step):
    part = x.shape[0] // SIDE
    blank = jnp.zeros((part, x.shape[1]), x.dtype)
    if step > 0:
        return jnp.concatenate([blank, x[:-part]], axis=0)
    return jnp.concatenate([x[part:], blank], axis=0)


def swap_orders(x, batch):
    pieces = [
        x[(b * SIDE + r) * SIDE : (b * SIDE + r + 1) * SIDE] for r in range(SIDE) for b in range(batch)
    ]
    return jnp.concatenate(pieces, axis=0)


def swap_back(x, batch):
    pieces = [
        x[(r * batch + b) * SIDE : (r * batch + b + 1) * SIDE] for b in range(batch) for r in range(SIDE)
    ]
    return jnp.concatenate(pieces, axis=0)


def col_sum(x):
    return jnp.sum(x, axis=0, keepdims=True)


def lane_sum(x):
    return jnp.sum(col_sum(x), axis=1, keepdims=True)


def rows_of(*rows):
    pad = SIDE - sum(row.shape[0] for row in rows)
    tail = [jnp.zeros((pad, rows[0].shape[1]), F32)] if pad else []
    return jnp.concatenate(list(rows) + tail, axis=0)


def spread_rows(out, rows):
    out[...] = jnp.broadcast_to(rows[None, : out.shape[1]], out.shape)


def mean_inverse(total, squares, count):
    center = total / count
    spread = squares / count - center * center
    return center, lax.rsqrt(spread + epsilon)


def slope(v):
    sigma = jax.nn.sigmoid(v)
    return sigma * (1.0 + v * (1.0 - sigma))


def three_rows(values):
    high = values.astype(BF).astype(F32)
    rest = values - high
    middle = rest.astype(BF).astype(F32)
    low = rest - middle
    blank = jnp.zeros((TAIL - 3 * values.shape[0], values.shape[1]), F32)
    return jnp.concatenate([high, middle, low, blank], axis=0).astype(BF)


def one_row(parts, count):
    parts = parts.astype(F32)
    return parts[:count] + parts[count : 2 * count] + parts[2 * count : 3 * count]


def add_up(pieces):
    total = pieces[0].astype(F32)
    for piece in pieces[1:]:
        total = total + piece.astype(F32)
    return total


def expand_mask(inside):
    images, wide = inside.shape
    dims = (images, SIDE, wide)
    lane = lax.broadcasted_iota(jnp.int32, dims, 2)
    col = lax.broadcasted_iota(jnp.int32, dims, 1)
    picked = jnp.where(lane == col, jnp.broadcast_to(inside[:, None, :], dims), 0.0)
    return jnp.broadcast_to(jnp.sum(picked, axis=2, keepdims=True), dims).reshape(-1, wide)


def widen(mask, wide):
    return jnp.concatenate(
        [mask, jnp.zeros((mask.shape[0], wide - mask.shape[1]), mask.dtype)], axis=1
    )


def lane_row(x):
    return col_sum(x * x)


def pack_weights(w, p, w_next, out, rows):
    depth = p.shape[0]
    w_ref, next_ref = w.ref(), w_next.ref()
    pieces = [w_ref[pl.ds(tap, depth, stride=9), :] for tap in range(9)] + [p[...]]
    depth = w_next.shape[0] // 9
    pieces += [next_ref[pl.ds(tap, depth, stride=9), :] for tap in range(9)]
    out[...] = jnp.concatenate(pieces, axis=0).astype(BF)
    out.send()
    rows[...] = rows_of(lane_row(w[...]), lane_row(p[...]), lane_row(w_next[...]))


def pack_images(images, mask, out, valid_out, scratch):
    groups, count, pix, lanes = images.shape
    wide = valid_out.shape[1]
    half = groups * count * pix // 2
    for k in range(lanes // wide):
        cut = slice(k * wide, (k + 1) * wide)
        scratch[k] = images[:, :, :, cut].astype(F32).reshape(2 * half, wide)
        for col in range(2):
            taken = scratch[k, pl.ds(col, half, stride=2), :].reshape(groups, count, 2, SIDE, wide)
            for row in range(2):
                rows = jnp.concatenate([taken[:, i, row] for i in range(count)], axis=1)
                start = col * lanes + k * wide
                out[:, row, :, start : start + wide] = rows.astype(BF)
    out.send()
    inside = widen(mask[...].astype(F32), wide)
    part = inside.shape[0] * SIDE
    for row in range(SIDE):
        turned = pltpu.roll(inside, (wide - SIDE * row) % wide, 1)
        valid_out[row * part : (row + 1) * part] = expand_mask(turned)


def tap_major(w):
    return w.reshape(-1, 9, w.shape[1]).transpose(1, 0, 2)


def taps_of(w, depth, first=0):
    def taps(*which):
        starts = [first + t * depth for t in which]
        return jnp.concatenate(
            [w[:, a : a + depth].reshape(-1, w.shape[2]) for a in starts], axis=1
        )

    return taps


def phase_of(x, row, col):
    lanes = x.shape[4] // 2
    cut = slice(col * lanes, (col + 1) * lanes)
    pieces = [x[k, r, row, :, cut] for r in range(x.shape[1]) for k in range(x.shape[0])]
    return jnp.concatenate(pieces, axis=0)


def conv_first(w, x, m, n, zb_out, zp_out, sums_out, pay):
    taps = taps_of(w, w.shape[1] // 10)
    wide = w.shape[2]
    y00 = dot(phase_of(x, 0, 0), taps(4, 9))
    y01 = dot(phase_of(x, 0, 1), taps(5, 3))
    y10 = dot(phase_of(x, 1, 0), taps(7, 1))
    y11 = dot(phase_of(x, 1, 1), taps(8, 6, 2, 0))
    here = y00[:, :wide] + y01[:, :wide] + y10[:, :wide] + y11[:, :wide]
    left = y01[:, wide:] + y11[:, wide : 2 * wide]
    above = y10[:, wide:] + y11[:, 2 * wide : 3 * wide]
    corner = y11[:, 3 * wide :]
    z = here + shift_row(above, 1) + shift_col(left + shift_row(corner, 1), 1)
    pix = z.shape[0]
    zb_out[:pix] = z.astype(BF)
    zb_out[pix:] = three_rows(n[0:2])
    zb_out.send()
    zp = y00[:, wide:]
    valid = m[...]
    vz, vzp = valid * z, valid * zp
    spread_rows(pay, rows_of(col_sum(vz), col_sum(vz * z), col_sum(valid)))
    pay.send()
    sums_out[...] = rows_of(col_sum(vzp), col_sum(vzp * zp))
    zp_out[...] = zp


def hand_on(w, *outs):
    w.ref()


def first_norm(z, rows):
    count = rows[2:3]
    center, inverse = mean_inverse(rows[0:1], rows[1:2], count)
    hat = (z - center) * inverse
    return hat, hat * rows[3:4] + rows[4:5], inverse


def conv_second(z, got, m, w, zp, sums, cot, h_out, z2_out, pay, tot_out, m_out, zp_out, cot_out, own_out):
    blocks, wide = z.shape[0], z.shape[2]
    valid = m[...]
    pix = valid.shape[0]
    hidden = []
    for k in range(blocks):
        rows = rows_of(jnp.sum(got[:, k], axis=0)[0:3], one_row(z[k, pix:], 2))
        tot_out[k] = rows
        _, lin, _ = first_norm(z[k, :pix].astype(F32), rows)
        hidden.append((lin * jax.nn.sigmoid(lin) * valid).astype(BF))
        h_out[:, k * wide : (k + 1) * wide] = hidden[-1]
    h_out.send()
    hidden = jnp.concatenate(hidden, axis=1)
    taps = taps_of(w, hidden.shape[1] // w.shape[0])
    moved = []
    for col in range(3):
        y = dot(hidden, taps(col, 3 + col, 6 + col))
        moved.append(
            shift_row(y[:, :wide], 1) + y[:, wide : 2 * wide] + shift_row(y[:, 2 * wide :], -1)
        )
    z2 = moved[1] + shift_col(moved[0], 1) + shift_col(moved[2], -1)
    vz = valid * z2
    spread_rows(pay, rows_of(col_sum(vz), col_sum(vz * z2), sums[0:2]))
    pay.send()
    z2_out[...] = z2
    batch, pix, wide = cot.shape
    m_out[...] = valid
    zp_out[...] = zp[...]
    cot_out[...] = swap_orders(cot[...].astype(F32).reshape(batch * pix, wide), batch)
    own_out[...] = tot_out.local[pl.ds(lax.axis_index("chan"), 1)][0]


def block_output(z2, zp, got, tot1, m, n, cot, out, e_out, hat2_out, hat_p_out, rows_out, pay):
    total, count = jnp.sum(got[...], axis=0), tot1[2:3]
    center2, inverse2 = mean_inverse(total[0:1], total[1:2], count)
    center_p, inverse_p = mean_inverse(total[2:3], total[3:4], count)
    hat2, hat_p = (z2[...] - center2) * inverse2, (zp[...] - center_p) * inverse_p
    hat2_out[...] = hat2
    hat_p_out[...] = hat_p
    rows_out[...] = rows_of(n[2:3] * inverse2, n[4:5] * inverse_p, count)
    summed = hat2 * n[2:3] + n[3:4] + (hat_p * n[4:5] + n[5:6])
    sigma = jax.nn.sigmoid(summed)
    valid = m[...]
    batch, pix, wide = out.shape
    e = cot[...] * valid * (sigma * (1.0 + summed * (1.0 - sigma)))
    spread_rows(pay, rows_of(col_sum(e), col_sum(e * hat2), col_sum(e * hat_p)))
    pay.send()
    e_out[...] = e
    out[...] = swap_back(summed * sigma * valid, batch).astype(BF).reshape(out.shape)


def grad_outputs(e, hat2, hat_p, rows, got, m, g2_out, gp_out, tot_out):
    back, count = jnp.sum(got[...], axis=0), rows[2:3]
    tot_out[...] = rows_of(back)
    valid, e = m[...], e[...]
    loss = valid * ((back[0:1] + hat2[...] * back[1:2]) / count)
    g2_out[...] = (rows[0:1] * (e - loss)).astype(BF)
    g2_out.send()
    loss = valid * ((back[0:1] + hat_p[...] * back[2:3]) / count)
    gp_out[...] = (rows[1:2] * (e - loss)).astype(BF)


def grad_hidden(w, g2, z, gp, tot1, m, b_out, msg, pay):
    blocks, _, wide = g2.shape
    count, part = w.shape[1], w.shape[2] // 9
    depth = count * part
    moved = []
    grads = jnp.concatenate([g2[k] for k in range(blocks)], axis=1)
    for col in range(3):
        starts = [(3 * row + col) * part for row in range(3)]
        taps = [
            jnp.concatenate([w[k, :, a : a + part].reshape(depth, wide) for k in range(blocks)], axis=1)
            for a in starts
        ]
        y = dot_nt(grads, jnp.concatenate(taps, axis=0))
        moved.append(
            shift_row(y[:, :depth], -1) + y[:, depth : 2 * depth] + shift_row(y[:, 2 * depth :], 1)
        )
    gh = moved[1] + shift_col(moved[0], -1) + shift_col(moved[2], 1)
    valid = m[...]
    hat, lin, _ = first_norm(z[: valid.shape[0]].astype(F32), tot1[...])
    b = gh * (slope(lin) * valid)
    shift, scaled = col_sum(b), col_sum(b * hat)
    spread_rows(pay, rows_of(shift, scaled))
    pay.send()
    here = col_sum(valid)
    shift, scaled = shift / here, scaled / here
    pix = b.shape[0]
    msg[:pix] = (b - valid * (shift + hat * scaled)).astype(BF)
    msg[pix : 2 * pix] = gp[...]
    msg[2 * pix :] = three_rows(jnp.concatenate([shift, scaled], axis=0))
    msg.send()
    b_out[...] = b


def make_grad_second(on_ring):
    def grad_second(h, g2, x, gp, g_out):
        groups, rows, wide = g_out.shape
        places = list(range(groups))
        if on_ring:
            last, turn = len(RING) - 1, turn_round()
            places = [RING.index(k) for k in places]
            places = [p + turn * (last - 2 * p) for p in places]
        share = h.shape[1] // groups
        h, g2 = h[...], g2[...].astype(F32)
        moved = [shift_col(g2, step).astype(BF) if step else g2.astype(BF) for step in (-1, 0, 1)]

        def put(rows, g):
            g = g.astype(BF).reshape(groups, -1, wide)
            for k, place in enumerate(places):
                g_out[place, rows] = g[k]

        spread_out = []
        for tap in range(9):
            step = tap // 3 - 1
            spread_out.append(shift_row(moved[tap % 3], step) if step else moved[tap % 3])
        spread_out = dot_tn(h, jnp.concatenate(spread_out, axis=1))
        for tap in range(9):
            g = spread_out[:, tap * wide : (tap + 1) * wide]
            put(slice(tap * share, (tap + 1) * share), g)
        pieces = [x[k, r] for r in range(SIDE) for k in range(x.shape[0])]
        put(slice(9 * share, rows), dot_tn(jnp.concatenate(pieces, axis=0), gp[...]))

    return grad_second


def grad_first(b, z, got, tot1, n, m, x, blocks_out, tot_out):
    own = got[:, pl.ds(lax.axis_index("chan"), 1)]
    back, count = jnp.sum(own, axis=0)[0], tot1[2:3]
    tot_out[...] = rows_of(back)
    hat, _, inverse = first_norm(z[: m.shape[0]].astype(F32), tot1[...])
    g = n[0:1] * inverse * (b[...] - m[...] * ((back[0:1] + hat * back[1:2]) / count))
    here, left = g.astype(BF), shift_col(g, -1).astype(BF)
    wide = here.shape[1]
    groups = blocks_out.shape[0]
    share = x.shape[4] // 2 // groups

    def put(tap, grad):
        rows = grad.astype(BF).reshape(groups, share, wide)
        blocks_out[:, tap * share : (tap + 1) * share] = rows

    above, corner = shift_row(here, -1), shift_row(left, -1)
    for row, col, pairs in (
        (0, 0, ((4, here),)),
        (0, 1, ((5, here), (3, left))),
        (1, 0, ((7, here), (1, above))),
        (1, 1, ((8, here), (6, left), (2, above), (0, corner))),
    ):
        both = jnp.concatenate([grad for _, grad in pairs], axis=1)
        both = dot_tn(phase_of(x, row, col), both)
        for place, (tap, _) in enumerate(pairs):
            put(tap, both[:, place * wide : (place + 1) * wide])


def grad_images(msg, z, got, tot1, m, w, out):
    blocks, count = w.shape[0], w.shape[1]
    depth = w.shape[2] // 10
    half, wide = count * depth, w.shape[3]

    def taps(*which):
        blocks_of = [
            [w[k, :, t * depth : (t + 1) * depth].reshape(half, wide) for k in range(blocks)]
            for t in which
        ]
        return jnp.concatenate([jnp.concatenate(row, axis=1) for row in blocks_of], axis=0)

    grads = []
    valid = m[...]
    pix = valid.shape[0]
    for k in range(blocks):
        rows, back = tot1[k], jnp.sum(got[:, k], axis=0)
        hat, _, inverse = first_norm(z[k, :pix].astype(F32), rows)
        fit = back[0:2] / rows[2:3] - one_row(msg[k, 2 * pix :], 2)
        loss = valid * (fit[0:1] + hat * fit[1:2])
        grads.append((rows[3:4] * inverse * (msg[k, :pix].astype(F32) - loss)).astype(BF))
    grads = jnp.concatenate(grads, axis=1)
    plain, moved = dot_nt(grads, taps(4, 5, 7, 8, 1, 2)), dot_nt(grads, taps(3, 3, 6, 6, 0, 0))
    proj = jnp.concatenate([msg[k, pix : 2 * pix] for k in range(blocks)], axis=1)
    proj = dot_nt(proj, taps(9, 9))
    lane = lax.broadcasted_iota(jnp.int32, moved.shape, 1) % (2 * half)
    total = plain + jnp.where(lane >= half, shift_col(moved, -1), 0.0)
    lane = lax.broadcasted_iota(jnp.int32, proj.shape, 1)
    even = total[:, : 2 * half] + jnp.where(lane < half, proj, 0.0)
    odd = total[:, 2 * half : 4 * half] + shift_row(total[:, 4 * half :], -1)
    for row, value in enumerate((even, odd)):
        out[:, row] = value.astype(BF).reshape(out.shape[0], -1, 2 * half)


def finish_images(x, out, scratch):
    images, pix, half = out.shape
    groups, _, part, wide = x.shape
    count = part // SIDE
    value = x[...].astype(F32).reshape(groups, 2, count, 1, SIDE, wide)
    value = jnp.concatenate([value[:, 0], value[:, 1]], axis=2)
    rows = images * pix // 2
    value = value.reshape(rows, wide)
    scratch[pl.ds(0, rows, stride=2), :] = value
    scratch[pl.ds(1, rows, stride=2), :] = pltpu.roll(value, half, 1)
    out[...] = scratch[...][:, :half].astype(BF).reshape(out.shape)


def put_rows(out, total):
    depth = out.shape[0] // 9
    for tap in range(9):
        out.local[pl.ds(tap, depth, stride=9), :] = total[tap * depth : (tap + 1) * depth]


def reduce_all(second, x, sw, t3, t4, n, g1_out, g2_out, gp_out, pay):
    second = second[...].astype(F32)
    cut = g2_out.shape[0]
    conv, proj = second[:cut], second[cut:]
    parts = [lane_row(conv), lane_row(proj)]
    first = add_up([x[k] for k in range(x.shape[0])])
    rows = [sw[0:1], lane_row(first), sw[2:3], parts[0], sw[1:2], parts[1]]
    nw, gn = n[...], norm_grad(t3, t4)
    blank = jnp.zeros((2, nw.shape[1]), F32)
    cols = [
        jnp.sum(jnp.concatenate(rows + [blank], axis=0), axis=1, keepdims=True),
        jnp.sum(jnp.concatenate([nw * nw, blank], axis=0), axis=1, keepdims=True),
        jnp.sum(jnp.concatenate([gn * gn, blank], axis=0), axis=1, keepdims=True),
    ]
    dims = (SIDE, pay.shape[2])
    lane, row = (lax.broadcasted_iota(jnp.int32, dims, axis) for axis in (1, 0))
    block = jnp.zeros(dims, F32)
    for place, col in enumerate(cols):
        block = jnp.where(lane == SIDE * place + row, col, block)
    spread_rows(pay, col_sum(block))
    pay.send()
    gp_out[...] = proj
    put_rows(g2_out, conv)
    g2_out.send()
    put_rows(g1_out, first)


def norm_grad(t3, t4):
    return jnp.concatenate([t4[1:2], t4[0:1], t3[1:2], t3[0:1], t3[2:3], t3[0:1]], axis=0)


def step_of(w, g, m, a, weight_sq, grad_sq):
    weight_len = jnp.sqrt(weight_sq)
    trust = trust_coef * weight_len / (jnp.sqrt(grad_sq) + weight_decay * weight_len + tiny_term)
    step = trust * (g + weight_decay * w)
    m_new = momentum * m + step
    w_new = w - learn_rate * (step + momentum * m_new)
    return w_new, m_new, avg_decay * a + (1.0 - avg_decay) * w_new


def make_update(dp_count):
    def update(*refs):
        r6, t3, t4 = refs[:3]
        ins, outs = refs[3:18], refs[18:]
        total = jnp.broadcast_to(jnp.sum(r6[...], axis=0), (SIDE, r6.shape[2]))
        lane, row = (lax.broadcasted_iota(jnp.int32, total.shape, axis) for axis in (1, 0))
        total = [
            jnp.sum(jnp.where(lane == SIDE * k + row, total, 0.0), axis=1, keepdims=True)
            for k in range(3)
        ]
        for place in range(3):
            w, g, m, a = (ref[...] for ref in ins[4 * place : 4 * place + 4])
            weight_sq = total[0][2 * place : 2 * place + 1]
            grad_sq = total[0][2 * place + 1 : 2 * place + 2]
            for ref, value in zip(outs[3 * place :], step_of(w, g, m, a, weight_sq, grad_sq)):
                ref[...] = value
                ref.send()
        w, m, a = (ref[...] for ref in ins[12:15])
        weight_sq, grad_sq = total[1][0:6] / dp_count, total[2][0:6] / dp_count
        g = norm_grad(t3, t4)
        for ref, value in zip(outs[9:], step_of(w, g, m, a, weight_sq, grad_sq)):
            ref[...] = value

    return update


def exchange(blocks, axes):
    return lax.all_to_all(blocks, axes, 0, 0)


def rings():
    count = lax.axis_size("chan")
    return [[(d ^ (c % 2)) * count + c for d in RING] for c in range(count)]


def turn_round():
    return lax.axis_index("chan") % 2


def swap(array, axis, bits):
    return lax.ppermute(array, axis, [(i, i ^ bits) for i in range(lax.axis_size(axis))])


def away(axis, k):
    return lambda: lax.axis_index(axis) ^ k


def in_groups(taps, groups):
    return taps.reshape(taps.shape[0], groups, -1, taps.shape[2]).transpose(1, 0, 2, 3)


def regroup(blocks, taps, groups):
    blocks = blocks.reshape(blocks.shape[0], taps, -1, blocks.shape[2]).transpose(1, 0, 2, 3)
    blocks = in_groups(blocks.reshape(taps, -1, blocks.shape[3]), groups)
    return blocks.reshape(groups, -1, blocks.shape[3])


def per_device(
    images, mask, cotangent, w_first, w_second, w_proj, norm_params, mom_first, mom_second,
    mom_proj, mom_norm, avg_first, avg_second, avg_proj, avg_norm,
):
    everyone = ("dp", "chan")
    dp_count, ch_count = lax.axis_size("dp"), lax.axis_size("chan")
    n_all = dp_count * ch_count
    batch = mask.shape[0]
    pix_here, d_in = images.shape[1], images.shape[2]
    wide = w_first.shape[1]
    d_out = wide * ch_count
    part = batch * SIDE
    pix = SIDE * part
    share = batch // ch_count
    eight = dp_count == SIDE and pix_here == 4 * SIDE
    groups = SIDE
    first_rows, second_rows = 10 * d_in // groups, 9 * d_out // groups
    square_rows = result((SIDE, wide))
    four = result((dp_count, 4, wide), pinned=False)
    passing, few = (result((n, wide), pinned=False) for n in (pix, SIDE))

    def slot_dp(k):
        return lax.axis_index("dp") ^ k

    def slot_ch(k):
        return lax.axis_index("chan") ^ k

    def share_out(own):
        far = swap(own, "chan", 2)
        return [own, swap(own, "chan", 1), far, swap(far, "chan", 1)]

    if eight:
        own, squares = call(
            pack_weights,
            [w_first, w_proj, w_second],
            [result((first_rows + second_rows, wide), BF), square_rows],
        )
        gathered = lax.all_gather(own, everyone, axis_index_groups=rings())
        order = [lambda d=d: d ^ turn_round() for d in RING]
        mine, valid = call(
            pack_images,
            [quarter(images, dp_count, share), mask],
            [result((dp_count, 2, share * SIDE, 2 * d_in), BF), result((pix, wide))],
            scratch=[((d_in // wide, dp_count * share * pix_here, wide), F32)],
            later=[own],
        )
        pixels, slot = share_out(exchange(mine, "dp")), slot_ch
    else:
        valid = mask.reshape(batch, SIDE, SIDE).transpose(1, 0, 2).reshape(pix, 1).astype(F32)
        valid = jnp.broadcast_to(valid, (pix, wide))
        own = jnp.concatenate([tap_major(w_first), w_proj[None]], axis=0).astype(BF)
        own = lax.all_gather(own, "dp", axis=1, tiled=True)
        next = lax.all_gather(tap_major(w_second).astype(BF), "dp", axis=1, tiled=True)
        gathered = [in_groups(taps, groups).reshape(groups, -1, wide) for taps in (own, next)]
        gathered = jnp.concatenate(gathered, axis=1)
        order = [lambda g=g: g for g in range(groups)]
        squares = [jnp.sum(w * w, axis=0) for w in (w_first, w_proj, w_second)]
        squares = jnp.zeros((SIDE, wide), F32).at[:3].set(jnp.stack(squares))
        mine = images.reshape(dp_count, ch_count, share, pix_here, d_in)
        mine = lax.dynamic_index_in_dim(mine, lax.axis_index("chan"), 1, keepdims=False)
        pixels = lax.all_gather(exchange(mine, "dp"), "chan")
        cols = pix_here // 2
        pixels = pixels.reshape(ch_count, SIDE, 2, SIDE // cols, share, cols, 2 * d_in)
        pixels = pixels.transpose(0, 1, 2, 4, 3, 5, 6)
        pixels = pixels.reshape(ch_count, SIDE, 2, share * SIDE, 2 * d_in)
        pixels, slot = [pixels[k] for k in range(ch_count)], lambda k: k

    macs = pix * 9 * wide * d_in
    per_block = groups // ch_count
    block_slots = [lambda k=k: (lax.axis_index("chan") ^ k) * per_block for k in range(ch_count)]
    z_own, z_proj, sums_proj, pay = call(
        conv_first,
        [spread(gathered, order, 0, first_rows), stack(pixels, slot), valid, norm_params],
        [
            result((pix + TAIL, wide), BF),
            result((pix, wide)),
            square_rows,
            result((n_all, 4, wide)),
        ],
        flops=2 * macs,
    )
    turned = call(
        hand_on,
        [spread(gathered, order, 0, first_rows + second_rows)],
        [parts_of(0, block_slots, per_block, 0, first_rows + second_rows, gathered)],
        later=[z_own],
    )
    got1 = exchange(pay, everyone).reshape(dp_count, ch_count, 4, wide)
    z_all = [swap(z_own, "chan", k) for k in range(1, ch_count)]
    got1, *both = lax.optimization_barrier((got1, *z_all, *turned))
    z_all, turned = [z_own, *both[: ch_count - 1]], both[ch_count - 1 :]

    hidden, z_second, pay, total1, *near = call(
        conv_second,
        [
            stack(z_all, slot_ch, 3),
            fresh(got1),
            valid,
            spread(gathered, order, first_rows, second_rows),
            z_proj,
            sums_proj,
            cotangent,
        ],
        [
            result((pix, d_out), BF, pinned=False),
            passing,
            four,
            result((ch_count, SIDE, wide)),
            passing,
            passing,
            passing,
            few,
        ],
        flops=4 * macs,
    )
    turned = turned[:1] + [swap(block, "chan", k) for k, block in enumerate(turned) if k]
    total1_own = pick(total1, away("chan", 0))
    got2 = exchange(pay, "dp")
    near_valid, near_proj, near_cot, near_total = (fresh(array) for array in near)
    output, e, hat_second, hat_proj, near_rows, pay = call(
        block_output,
        [fresh(z_second), near_proj, fresh(got2), near_total, near_valid, norm_params, near_cot],
        [result((batch, SIDE * SIDE, wide), BF), passing, passing, passing, few, four],
    )
    got3 = exchange(pay, "dp")

    g_second_out, g_proj_out, total3 = call(
        grad_outputs,
        [fresh(e), fresh(hat_second), fresh(hat_proj), fresh(near_rows), fresh(got3), near_valid],
        [result((pix, wide), BF), result((pix, wide), BF), square_rows],
        later=turned[1:],
    )
    rows = second_rows + d_in // groups
    (grads,) = call(
        make_grad_second(eight),
        [fresh(hidden), g_second_out, even_phase(pixels, slot), g_proj_out],
        [result((groups, rows, wide), BF)],
        flops=4 * macs,
    )
    far = swap(g_second_out, "chan", 2)
    far, grads = lax.optimization_barrier((far, grads))
    g_all = [g_second_out, swap(g_second_out, "chan", 1), far, swap(far, "chan", 1)]
    if eight:
        grads_second = lax.psum_scatter(
            grads.reshape(groups * rows, wide),
            everyone,
            scatter_dimension=0,
            axis_index_groups=rings(),
            tiled=True,
        )
    else:
        grads = [
            regroup(grads[:, :second_rows], 9, dp_count),
            regroup(grads[:, second_rows:], 1, dp_count),
        ]
        grads = jnp.concatenate(grads, axis=1)
        grads_second = jnp.sum(exchange(grads, "dp").astype(F32), axis=0)

    back, msg, pay = call(
        grad_hidden,
        [stack_rows(turned, slot_ch, first_rows, second_rows, 3), stack(g_all, slot_ch, 3)]
        + [z_own, g_proj_out, total1_own, valid],
        [passing, result((2 * pix + TAIL, wide), BF), result((n_all, 2, wide), pinned=False)],
        flops=4 * macs,
    )
    got4 = exchange(pay, everyone).reshape(dp_count, ch_count, 2, wide)
    far = swap(msg, "chan", 2)
    far, got4 = lax.optimization_barrier((far, got4))
    messages = [msg, swap(msg, "chan", 1), far, swap(far, "chan", 1)]

    grads, total4 = call(
        grad_first,
        [fresh(back), z_own, fresh(got4), total1_own, norm_params, valid, stack(pixels, slot)],
        [result((groups, 9 * (d_in // groups), wide), BF), square_rows],
        flops=2 * macs,
    )
    if not eight:
        grads = regroup(grads, 9, dp_count)
    got_first = exchange(grads, "dp")

    half = wide // 2
    takes = [
        stack(messages, slot_ch, 3),
        stack(z_all, slot_ch, 3),
        fresh(got4),
        total1,
        valid,
        stack_rows(turned, slot_ch, 0, first_rows, 3),
    ]
    dims = (SIDE, 2, part, wide)
    if eight:
        rows = call(
            grad_images,
            takes,
            [split([away("dp", k) for k in range(SIDE)], dims, BF)],
            flops=2 * macs,
        )
        rows = rows[:1] + [swap(row, "dp", k) for k, row in enumerate(rows) if k]
    else:
        (rows,) = call(grad_images, takes, [result(dims, BF)], flops=2 * macs)
        cols = pix_here // 2
        rows = rows.reshape(SIDE, 2, batch, SIDE // cols, cols, wide)
        rows = rows.transpose(0, 1, 3, 2, 4, 5).reshape(dp_count, batch, cols, wide)
        rows = [exchange(rows, "dp")]
    reduced_first, reduced_second, reduced_proj, pay = call(
        reduce_all,
        [grads_second, fresh(got_first), squares, total3, total4, norm_params],
        [
            result(w_first.shape),
            result(w_second.shape),
            result(w_proj.shape),
            result((n_all, 1, wide)),
        ],
    )
    if eight:
        order = (0, 1, 2, 4, 5, 7, 3, 6)
        *sent, pay = lax.optimization_barrier((*(rows[k] for k in order), pay))
        rows = [sent[order.index(k)] for k in range(SIDE)]
    else:
        pay, *rows = lax.optimization_barrier((pay, *rows))
    got6 = exchange(pay, everyone)

    conv = (
        (w_first, reduced_first, mom_first, avg_first),
        (w_second, reduced_second, mom_second, avg_second),
        (w_proj, reduced_proj, mom_proj, avg_proj),
    )
    results = call(
        make_update(dp_count),
        [fresh(got6), total3, total4, *(array for group in conv for array in group)]
        + [norm_params, mom_norm, avg_norm],
        [result(group[0].shape) for group in conv for _ in range(3)]
        + [result(norm_params.shape)] * 3,
    )
    if eight:
        (grad_pixels,) = call(
            finish_images,
            [stack(rows, slot_dp, 7)],
            [result((images.shape[0], pix_here, half), BF)],
            scratch=[((images.shape[0] * pix_here, wide), F32)],
        )
    else:
        grad_pixels = rows[0].reshape(dp_count * batch, pix_here, half)
    return (output, grad_pixels, *results)


def solution(mesh):
    rows, cols, batch = P("dp", "chan"), P(None, "chan"), P("dp", None, "chan")
    weights = (rows, rows, rows, cols)
    in_specs = (P(None, "dp", None), P("dp", None), batch) + weights * 3
    out_specs = (batch, P(None, "dp", "chan")) + (rows,) * 9 + (cols,) * 3
    return jax.shard_map(
        per_device, mesh=mesh, in_specs=in_specs, out_specs=out_specs, check_vma=False
    )
```

```python
import jax
import jax.numpy as jnp
from jax import lax
from jax.experimental import pallas as pl
from jax.experimental.pallas import tpu as pltpu
from jax.sharding import PartitionSpec as P

BF = jnp.bfloat16
F32 = jnp.float32

epsilon = 1e-05
learn_rate = 0.4
trust_coef = 0.5
momentum = 0.5
avg_decay = 0.6
weight_decay = 5e-05
tiny_term = 1e-06

SIDE = 8
TAIL = 16
RING = [0, 2, 4, 6, 7, 5, 3, 1]


class whole:
    loose = 0
    direct = False

    def __init__(self, array):
        self.arrays, self.dims, self.dtype = [array], array.shape, array.dtype

    def copies(self):
        return len(self.arrays)

    def plan(self, refs, local):
        return [(refs[0], local)]


class fresh(whole):
    loose = 1
    direct = True

    def copies(self):
        return 0

    def plan(self, refs, local):
        return []


class stack(whole):
    def __init__(self, arrays, slot, loose=0):
        self.arrays, self.dtype, self.loose = list(arrays), arrays[0].dtype, loose
        self.dims, self.slot = (len(arrays),) + arrays[0].shape, slot

    def plan(self, refs, local):
        return [(ref, local.at[self.slot(k)]) for k, ref in enumerate(refs)]


class pick(whole):
    def __init__(self, array, index):
        self.arrays, self.dtype, self.index = [array], array.dtype, index
        self.dims = array.shape[1:]

    def plan(self, refs, local):
        return [(refs[0].at[self.index()], local)]


class spread(whole):
    def __init__(self, array, order, first, rows):
        self.arrays, self.dtype, self.order = [array], array.dtype, order
        self.first, self.rows = first, rows
        self.dims = (array.shape[0], rows) + array.shape[2:]

    def copies(self):
        return self.dims[0]

    def plan(self, refs, local):
        cut = pl.ds(self.first, self.rows)
        return [(refs[0].at[k, cut], local.at[place()]) for k, place in enumerate(self.order)]


class stack_rows(stack):
    def __init__(self, arrays, slot, first, rows, loose=0):
        super().__init__(arrays, slot, loose)
        self.cut = pl.ds(first, rows)
        self.dims = self.dims[:2] + (rows,) + self.dims[3:]

    def plan(self, refs, local):
        return [(ref.at[:, self.cut], local.at[self.slot(k)]) for k, ref in enumerate(refs)]


class quarter(whole):
    def __init__(self, images, groups, count):
        self.arrays, self.dtype = [images], images.dtype
        self.per, self.count = images.shape[0] // groups, count
        self.dims = (groups, count) + images.shape[1:]

    def copies(self):
        return self.dims[0]

    def plan(self, refs, local):
        mine = lax.axis_index("chan") * self.count
        return [
            (refs[0].at[pl.ds(g * self.per + mine, self.count)], local.at[g])
            for g in range(self.dims[0])
        ]


class even_phase(stack):
    def __init__(self, arrays, slot):
        super().__init__(arrays, slot)
        self.lanes = arrays[0].shape[3] // 2
        self.dims = (len(arrays), arrays[0].shape[0], arrays[0].shape[2], self.lanes)

    def plan(self, refs, local):
        lanes = pl.ds(0, self.lanes)
        return [(ref.at[:, 0, :, lanes], local.at[self.slot(k)]) for k, ref in enumerate(refs)]


class result:
    pinned = True

    def __init__(self, dims, dtype=F32, pinned=True):
        self.dims, self.dtype, self.pinned = tuple(dims), dtype, pinned
        self.outs = [jax.ShapeDtypeStruct(self.dims, dtype)]

    def copies(self):
        return len(self.outs)

    def plan(self, local, refs):
        return [(local, refs[0])]


class split(result):
    def __init__(self, slots, dims, dtype=F32, part=None):
        self.dims, self.dtype, self.slots = tuple(dims), dtype, slots
        self.outs = [jax.ShapeDtypeStruct(self.dims[1:], dtype) for _ in slots]

    def plan(self, local, refs):
        return [(local.at[slot()], ref) for slot, ref in zip(self.slots, refs)]


class parts_of(result):
    dims = None

    def __init__(self, source, slots, count, first, rows, array):
        self.source, self.slots, self.count, self.cut = source, slots, count, pl.ds(first, rows)
        dims = (count, rows) + array.shape[2:]
        self.outs = [jax.ShapeDtypeStruct(dims, array.dtype) for _ in slots]

    def plan(self, local, refs):
        return [
            (local.at[pl.ds(slot(), self.count), self.cut], ref)
            for slot, ref in zip(self.slots, refs)
        ]


class Taken:
    def __init__(self, local, copies):
        self.local, self.copies, self.waited = local, copies, False

    def ref(self):
        if not self.waited:
            for copy in self.copies:
                copy.wait()
            self.waited = True
        return self.local

    def __getitem__(self, index):
        return self.ref()[index]

    @property
    def shape(self):
        return self.local.shape


class Given:
    def __init__(self, local, copies):
        self.local, self.copies, self.sent = local, copies, False

    def send(self):
        if not self.sent:
            for copy in self.copies:
                copy.start()
            self.sent = True

    def __setitem__(self, index, value):
        self.local[index] = value

    @property
    def shape(self):
        return self.local.shape


def call(body, takes, gives, scratch=(), flops=0, limit=40, later=()):
    takes = [t if isinstance(t, whole) else whole(t) for t in takes]
    arrays = [a for t in takes for a in t.arrays]
    spec = pl.BlockSpec(memory_space=pltpu.HBM)
    loose, vmem = pl.BlockSpec(memory_space=pl.ANY), pl.BlockSpec(memory_space=pltpu.VMEM)
    pinned = [False] * len(later)
    in_specs = [loose] * len(later)
    for t in takes:
        pinned += [True] * (len(t.arrays) - t.loose) + [False] * t.loose
        in_specs += [spec] * (len(t.arrays) - t.loose) + [vmem if t.direct else loose] * t.loose
    outs = [o for g in gives for o in g.outs]
    n_later, n_in, n_out = len(later), len(arrays), len(outs)
    n_copies = sum(t.copies() for t in takes) + sum(g.copies() for g in gives if g.pinned)

    def kernel(*refs):
        refs = refs[n_later:]
        ins, res = list(refs[:n_in]), list(refs[n_in : n_in + n_out])
        local = list(refs[n_in + n_out : -1])
        sems = refs[-1]
        used = 0
        taken, given = [], []
        for t in takes:
            mine, ins = ins[: len(t.arrays)], ins[len(t.arrays) :]
            place = mine[0] if t.direct else local.pop(0)
            copies = []
            for a, b in t.plan(mine, place):
                copies.append(pltpu.make_async_copy(a, b, sems.at[used]))
                used += 1
            for copy in copies:
                copy.start()
            taken.append(Taken(place, copies))
        for g in gives:
            mine, res = res[: len(g.outs)], res[len(g.outs) :]
            if g.dims is None:
                place = taken[g.source].local
            else:
                place = local.pop(0) if g.pinned else mine[0]
            copies = []
            for a, b in g.plan(place, mine) if g.pinned else ():
                copies.append(pltpu.make_async_copy(a, b, sems.at[used]))
                used += 1
            given.append(Given(place, copies))
        body(*taken, *given, *local)
        for t in taken:
            t.ref()
        for g in given:
            g.send()
        for g in given:
            for copy in g.copies:
                copy.wait()

    moved = sum(a.size * a.dtype.itemsize for a in arrays + outs)
    operands = [
        pltpu.with_memory_space_constraint(a, pltpu.HBM) if pin else a
        for a, pin in zip([*later, *arrays], pinned)
    ]
    values = pl.pallas_call(
        kernel,
        out_shape=[pltpu.HBM(o.shape, o.dtype) if g.pinned else o for g in gives for o in g.outs],
        in_specs=in_specs,
        out_specs=[spec if g.pinned else vmem for g in gives for _ in g.outs],
        scratch_shapes=[pltpu.VMEM(t.dims, t.dtype) for t in takes if not t.direct]
        + [pltpu.VMEM(g.dims, g.dtype) for g in gives if g.dims is not None and g.pinned]
        + [pltpu.VMEM(dims, dtype) for dims, dtype in scratch]
        + [pltpu.SemaphoreType.DMA((n_copies,))],
        compiler_params=pltpu.CompilerParams(vmem_limit_bytes=limit * 2**20),
        cost_estimate=pl.CostEstimate(flops=flops, bytes_accessed=moved, transcendentals=0),
        name=body.__name__,
    )(*operands)
    return list(values)


def dot(a, b):
    return jnp.dot(a, b, preferred_element_type=F32)


def dot_nt(a, b):
    return lax.dot_general(a, b, (((1,), (1,)), ((), ())), preferred_element_type=F32)


def dot_tn(a, b):
    return lax.dot_general(a, b, (((0,), (0,)), ((), ())), preferred_element_type=F32)


def shift_col(x, step):
    rows, lanes = x.shape
    grouped = x.reshape(rows // SIDE, SIDE, lanes)
    rolled = pltpu.roll(grouped, step % SIDE, 1)
    col = lax.broadcasted_iota(jnp.int32, grouped.shape, 1)
    edge = 0 if step > 0 else SIDE - 1
    return jnp.where(col == edge, 0.0, rolled).reshape(rows, lanes)


def shift_row(x, step):
    part = x.shape[0] // SIDE
    blank = jnp.zeros((part, x.shape[1]), x.dtype)
    if step > 0:
        return jnp.concatenate([blank, x[:-part]], axis=0)
    return jnp.concatenate([x[part:], blank], axis=0)


def swap_orders(x, batch):
    pieces = [
        x[(b * SIDE + r) * SIDE : (b * SIDE + r + 1) * SIDE] for r in range(SIDE) for b in range(batch)
    ]
    return jnp.concatenate(pieces, axis=0)


def swap_back(x, batch):
    pieces = [
        x[(r * batch + b) * SIDE : (r * batch + b + 1) * SIDE] for b in range(batch) for r in range(SIDE)
    ]
    return jnp.concatenate(pieces, axis=0)


def col_sum(x):
    return jnp.sum(x, axis=0, keepdims=True)


def lane_sum(x):
    return jnp.sum(col_sum(x), axis=1, keepdims=True)


def rows_of(*rows):
    pad = SIDE - sum(row.shape[0] for row in rows)
    tail = [jnp.zeros((pad, rows[0].shape[1]), F32)] if pad else []
    return jnp.concatenate(list(rows) + tail, axis=0)


def spread_rows(out, rows):
    out[...] = jnp.broadcast_to(rows[None, : out.shape[1]], out.shape)


def mean_inverse(total, squares, count):
    center = total / count
    spread = squares / count - center * center
    return center, lax.rsqrt(spread + epsilon)


def slope(v):
    sigma = jax.nn.sigmoid(v)
    return sigma * (1.0 + v * (1.0 - sigma))


def three_rows(values):
    high = values.astype(BF).astype(F32)
    rest = values - high
    middle = rest.astype(BF).astype(F32)
    low = rest - middle
    blank = jnp.zeros((TAIL - 3 * values.shape[0], values.shape[1]), F32)
    return jnp.concatenate([high, middle, low, blank], axis=0).astype(BF)


def one_row(parts, count):
    parts = parts.astype(F32)
    return parts[:count] + parts[count : 2 * count] + parts[2 * count : 3 * count]


def add_up(pieces):
    total = pieces[0].astype(F32)
    for piece in pieces[1:]:
        total = total + piece.astype(F32)
    return total


def expand_mask(inside):
    images, wide = inside.shape
    dims = (images, SIDE, wide)
    lane = lax.broadcasted_iota(jnp.int32, dims, 2)
    col = lax.broadcasted_iota(jnp.int32, dims, 1)
    picked = jnp.where(lane == col, jnp.broadcast_to(inside[:, None, :], dims), 0.0)
    return jnp.broadcast_to(jnp.sum(picked, axis=2, keepdims=True), dims).reshape(-1, wide)


def widen(mask, wide):
    return jnp.concatenate(
        [mask, jnp.zeros((mask.shape[0], wide - mask.shape[1]), mask.dtype)], axis=1
    )


def lane_row(x):
    return col_sum(x * x)


def pack_weights(w, p, w_next, out, rows):
    depth = p.shape[0]
    w_ref, next_ref = w.ref(), w_next.ref()
    pieces = [w_ref[pl.ds(tap, depth, stride=9), :] for tap in range(9)] + [p[...]]
    depth = w_next.shape[0] // 9
    pieces += [next_ref[pl.ds(tap, depth, stride=9), :] for tap in range(9)]
    out[...] = jnp.concatenate(pieces, axis=0).astype(BF)
    out.send()
    rows[...] = rows_of(lane_row(w[...]), lane_row(p[...]), lane_row(w_next[...]))


def pack_images(images, mask, out, valid_out, scratch):
    groups, count, pix, lanes = images.shape
    wide = valid_out.shape[1]
    half = groups * count * pix // 2
    for k in range(lanes // wide):
        cut = slice(k * wide, (k + 1) * wide)
        scratch[k] = images[:, :, :, cut].astype(F32).reshape(2 * half, wide)
        for col in range(2):
            taken = scratch[k, pl.ds(col, half, stride=2), :].reshape(groups, count, 2, SIDE, wide)
            for row in range(2):
                rows = jnp.concatenate([taken[:, i, row] for i in range(count)], axis=1)
                start = col * lanes + k * wide
                out[:, row, :, start : start + wide] = rows.astype(BF)
    out.send()
    inside = widen(mask[...].astype(F32), wide)
    part = inside.shape[0] * SIDE
    for row in range(SIDE):
        turned = pltpu.roll(inside, (wide - SIDE * row) % wide, 1)
        valid_out[row * part : (row + 1) * part] = expand_mask(turned)


def tap_major(w):
    return w.reshape(-1, 9, w.shape[1]).transpose(1, 0, 2)


def taps_of(w, depth, first=0):
    def taps(*which):
        starts = [first + t * depth for t in which]
        return jnp.concatenate(
            [w[:, a : a + depth].reshape(-1, w.shape[2]) for a in starts], axis=1
        )

    return taps


def phase_of(x, row, col):
    lanes = x.shape[4] // 2
    cut = slice(col * lanes, (col + 1) * lanes)
    pieces = [x[k, r, row, :, cut] for r in range(x.shape[1]) for k in range(x.shape[0])]
    return jnp.concatenate(pieces, axis=0)


def conv_first(w, x, m, n, zb_out, zp_out, sums_out, pay):
    taps = taps_of(w, w.shape[1] // 10)
    wide = w.shape[2]
    y00 = dot(phase_of(x, 0, 0), taps(4, 9))
    y01 = dot(phase_of(x, 0, 1), taps(5, 3))
    y10 = dot(phase_of(x, 1, 0), taps(7, 1))
    y11 = dot(phase_of(x, 1, 1), taps(8, 6, 2, 0))
    here = y00[:, :wide] + y01[:, :wide] + y10[:, :wide] + y11[:, :wide]
    left = y01[:, wide:] + y11[:, wide : 2 * wide]
    above = y10[:, wide:] + y11[:, 2 * wide : 3 * wide]
    corner = y11[:, 3 * wide :]
    z = here + shift_row(above, 1) + shift_col(left + shift_row(corner, 1), 1)
    pix = z.shape[0]
    zb_out[:pix] = z.astype(BF)
    zb_out[pix:] = three_rows(n[0:2])
    zb_out.send()
    zp = y00[:, wide:]
    valid = m[...]
    vz, vzp = valid * z, valid * zp
    spread_rows(pay, rows_of(col_sum(vz), col_sum(vz * z), col_sum(valid)))
    pay.send()
    sums_out[...] = rows_of(col_sum(vzp), col_sum(vzp * zp))
    zp_out[...] = zp


def hand_on(w, *outs):
    w.ref()


def first_norm(z, rows):
    count = rows[2:3]
    center, inverse = mean_inverse(rows[0:1], rows[1:2], count)
    hat = (z - center) * inverse
    return hat, hat * rows[3:4] + rows[4:5], inverse


def conv_second(z, got, m, w, zp, sums, cot, h_out, z2_out, pay, tot_out, m_out, zp_out, cot_out, own_out):
    blocks, wide = z.shape[0], z.shape[2]
    valid = m[...]
    pix = valid.shape[0]
    hidden = []
    for k in range(blocks):
        rows = rows_of(jnp.sum(got[:, k], axis=0)[0:3], one_row(z[k, pix:], 2))
        tot_out[k] = rows
        _, lin, _ = first_norm(z[k, :pix].astype(F32), rows)
        hidden.append((lin * jax.nn.sigmoid(lin) * valid).astype(BF))
        h_out[:, k * wide : (k + 1) * wide] = hidden[-1]
    h_out.send()
    hidden = jnp.concatenate(hidden, axis=1)
    taps = taps_of(w, hidden.shape[1] // w.shape[0])
    moved = []
    for col in range(3):
        y = dot(hidden, taps(col, 3 + col, 6 + col))
        moved.append(
            shift_row(y[:, :wide], 1) + y[:, wide : 2 * wide] + shift_row(y[:, 2 * wide :], -1)
        )
    z2 = moved[1] + shift_col(moved[0], 1) + shift_col(moved[2], -1)
    vz = valid * z2
    spread_rows(pay, rows_of(col_sum(vz), col_sum(vz * z2), sums[0:2]))
    pay.send()
    z2_out[...] = z2
    batch, pix, wide = cot.shape
    m_out[...] = valid
    zp_out[...] = zp[...]
    cot_out[...] = swap_orders(cot[...].astype(F32).reshape(batch * pix, wide), batch)
    own_out[...] = tot_out.local[pl.ds(lax.axis_index("chan"), 1)][0]


def block_output(z2, zp, got, tot1, m, n, cot, out, e_out, hat2_out, hat_p_out, rows_out, pay):
    total, count = jnp.sum(got[...], axis=0), tot1[2:3]
    center2, inverse2 = mean_inverse(total[0:1], total[1:2], count)
    center_p, inverse_p = mean_inverse(total[2:3], total[3:4], count)
    hat2, hat_p = (z2[...] - center2) * inverse2, (zp[...] - center_p) * inverse_p
    hat2_out[...] = hat2
    hat_p_out[...] = hat_p
    rows_out[...] = rows_of(n[2:3] * inverse2, n[4:5] * inverse_p, count)
    summed = hat2 * n[2:3] + n[3:4] + (hat_p * n[4:5] + n[5:6])
    sigma = jax.nn.sigmoid(summed)
    valid = m[...]
    batch, pix, wide = out.shape
    e = cot[...] * valid * (sigma * (1.0 + summed * (1.0 - sigma)))
    spread_rows(pay, rows_of(col_sum(e), col_sum(e * hat2), col_sum(e * hat_p)))
    pay.send()
    e_out[...] = e
    out[...] = swap_back(summed * sigma * valid, batch).astype(BF).reshape(out.shape)


def grad_outputs(e, hat2, hat_p, rows, got, m, g2_out, gp_out, tot_out):
    back, count = jnp.sum(got[...], axis=0), rows[2:3]
    tot_out[...] = rows_of(back)
    valid, e = m[...], e[...]
    loss = valid * ((back[0:1] + hat2[...] * back[1:2]) / count)
    g2_out[...] = (rows[0:1] * (e - loss)).astype(BF)
    g2_out.send()
    loss = valid * ((back[0:1] + hat_p[...] * back[2:3]) / count)
    gp_out[...] = (rows[1:2] * (e - loss)).astype(BF)


def grad_hidden(w, g2, z, gp, tot1, m, b_out, msg, pay):
    blocks, _, wide = g2.shape
    count, part = w.shape[1], w.shape[2] // 9
    depth = count * part
    moved = []
    grads = jnp.concatenate([g2[k] for k in range(blocks)], axis=1)
    for col in range(3):
        starts = [(3 * row + col) * part for row in range(3)]
        taps = [
            jnp.concatenate([w[k, :, a : a + part].reshape(depth, wide) for k in range(blocks)], axis=1)
            for a in starts
        ]
        y = dot_nt(grads, jnp.concatenate(taps, axis=0))
        moved.append(
            shift_row(y[:, :depth], -1) + y[:, depth : 2 * depth] + shift_row(y[:, 2 * depth :], 1)
        )
    gh = moved[1] + shift_col(moved[0], -1) + shift_col(moved[2], 1)
    valid = m[...]
    hat, lin, _ = first_norm(z[: valid.shape[0]].astype(F32), tot1[...])
    b = gh * (slope(lin) * valid)
    shift, scaled = col_sum(b), col_sum(b * hat)
    spread_rows(pay, rows_of(shift, scaled))
    pay.send()
    here = col_sum(valid)
    shift, scaled = shift / here, scaled / here
    pix = b.shape[0]
    msg[:pix] = (b - valid * (shift + hat * scaled)).astype(BF)
    msg[pix : 2 * pix] = gp[...]
    msg[2 * pix :] = three_rows(jnp.concatenate([shift, scaled], axis=0))
    msg.send()
    b_out[...] = b


def make_grad_second(on_ring):
    def grad_second(h, g2, x, gp, g_out):
        groups, rows, wide = g_out.shape
        places = list(range(groups))
        if on_ring:
            last, turn = len(RING) - 1, turn_round()
            places = [RING.index(k) for k in places]
            places = [p + turn * (last - 2 * p) for p in places]
        share = h.shape[1] // groups
        h, g2 = h[...], g2[...].astype(F32)
        moved = [shift_col(g2, step).astype(BF) if step else g2.astype(BF) for step in (-1, 0, 1)]

        def put(rows, g):
            g = g.astype(BF).reshape(groups, -1, wide)
            for k, place in enumerate(places):
                g_out[place, rows] = g[k]

        spread_out = []
        for tap in range(9):
            step = tap // 3 - 1
            spread_out.append(shift_row(moved[tap % 3], step) if step else moved[tap % 3])
        spread_out = dot_tn(h, jnp.concatenate(spread_out, axis=1))
        for tap in range(9):
            g = spread_out[:, tap * wide : (tap + 1) * wide]
            put(slice(tap * share, (tap + 1) * share), g)
        pieces = [x[k, r] for r in range(SIDE) for k in range(x.shape[0])]
        put(slice(9 * share, rows), dot_tn(jnp.concatenate(pieces, axis=0), gp[...]))

    return grad_second


def grad_first(b, z, got, tot1, n, m, x, blocks_out, tot_out):
    own = got[:, pl.ds(lax.axis_index("chan"), 1)]
    back, count = jnp.sum(own, axis=0)[0], tot1[2:3]
    tot_out[...] = rows_of(back)
    hat, _, inverse = first_norm(z[: m.shape[0]].astype(F32), tot1[...])
    g = n[0:1] * inverse * (b[...] - m[...] * ((back[0:1] + hat * back[1:2]) / count))
    here, left = g.astype(BF), shift_col(g, -1).astype(BF)
    wide = here.shape[1]
    groups = blocks_out.shape[0]
    share = x.shape[4] // 2 // groups

    def put(tap, grad):
        rows = grad.astype(BF).reshape(groups, share, wide)
        blocks_out[:, tap * share : (tap + 1) * share] = rows

    above, corner = shift_row(here, -1), shift_row(left, -1)
    for row, col, pairs in (
        (0, 0, ((4, here),)),
        (0, 1, ((5, here), (3, left))),
        (1, 0, ((7, here), (1, above))),
        (1, 1, ((8, here), (6, left), (2, above), (0, corner))),
    ):
        both = jnp.concatenate([grad for _, grad in pairs], axis=1)
        both = dot_tn(phase_of(x, row, col), both)
        for place, (tap, _) in enumerate(pairs):
            put(tap, both[:, place * wide : (place + 1) * wide])


def grad_images(msg, z, got, tot1, m, w, out):
    blocks, count = w.shape[0], w.shape[1]
    depth = w.shape[2] // 10
    half, wide = count * depth, w.shape[3]

    def taps(*which):
        blocks_of = [
            [w[k, :, t * depth : (t + 1) * depth].reshape(half, wide) for k in range(blocks)]
            for t in which
        ]
        return jnp.concatenate([jnp.concatenate(row, axis=1) for row in blocks_of], axis=0)

    grads = []
    valid = m[...]
    pix = valid.shape[0]
    for k in range(blocks):
        rows, back = tot1[k], jnp.sum(got[:, k], axis=0)
        hat, _, inverse = first_norm(z[k, :pix].astype(F32), rows)
        fit = back[0:2] / rows[2:3] - one_row(msg[k, 2 * pix :], 2)
        loss = valid * (fit[0:1] + hat * fit[1:2])
        grads.append((rows[3:4] * inverse * (msg[k, :pix].astype(F32) - loss)).astype(BF))
    grads = jnp.concatenate(grads, axis=1)
    plain, moved = dot_nt(grads, taps(4, 5, 7, 8, 1, 2)), dot_nt(grads, taps(3, 3, 6, 6, 0, 0))
    proj = jnp.concatenate([msg[k, pix : 2 * pix] for k in range(blocks)], axis=1)
    proj = dot_nt(proj, taps(9, 9))
    lane = lax.broadcasted_iota(jnp.int32, moved.shape, 1) % (2 * half)
    total = plain + jnp.where(lane >= half, shift_col(moved, -1), 0.0)
    lane = lax.broadcasted_iota(jnp.int32, proj.shape, 1)
    even = total[:, : 2 * half] + jnp.where(lane < half, proj, 0.0)
    odd = total[:, 2 * half : 4 * half] + shift_row(total[:, 4 * half :], -1)
    for row, value in enumerate((even, odd)):
        out[:, row] = value.astype(BF).reshape(out.shape[0], -1, 2 * half)


def finish_images(x, out, scratch):
    images, pix, half = out.shape
    groups, _, part, wide = x.shape
    count = part // SIDE
    value = x[...].astype(F32).reshape(groups, 2, count, 1, SIDE, wide)
    value = jnp.concatenate([value[:, 0], value[:, 1]], axis=2)
    rows = images * pix // 2
    value = value.reshape(rows, wide)
    scratch[pl.ds(0, rows, stride=2), :] = value
    scratch[pl.ds(1, rows, stride=2), :] = pltpu.roll(value, half, 1)
    out[...] = scratch[...][:, :half].astype(BF).reshape(out.shape)


def put_rows(out, total):
    depth = out.shape[0] // 9
    for tap in range(9):
        out.local[pl.ds(tap, depth, stride=9), :] = total[tap * depth : (tap + 1) * depth]


def reduce_all(second, x, sw, t3, t4, n, g1_out, g2_out, gp_out, pay):
    second = second[...].astype(F32)
    cut = g2_out.shape[0]
    conv, proj = second[:cut], second[cut:]
    parts = [lane_row(conv), lane_row(proj)]
    first = add_up([x[k] for k in range(x.shape[0])])
    rows = [sw[0:1], lane_row(first), sw[2:3], parts[0], sw[1:2], parts[1]]
    nw, gn = n[...], norm_grad(t3, t4)
    blank = jnp.zeros((2, nw.shape[1]), F32)
    cols = [
        jnp.sum(jnp.concatenate(rows + [blank], axis=0), axis=1, keepdims=True),
        jnp.sum(jnp.concatenate([nw * nw, blank], axis=0), axis=1, keepdims=True),
        jnp.sum(jnp.concatenate([gn * gn, blank], axis=0), axis=1, keepdims=True),
    ]
    dims = (SIDE, pay.shape[2])
    lane, row = (lax.broadcasted_iota(jnp.int32, dims, axis) for axis in (1, 0))
    block = jnp.zeros(dims, F32)
    for place, col in enumerate(cols):
        block = jnp.where(lane == SIDE * place + row, col, block)
    spread_rows(pay, col_sum(block))
    pay.send()
    gp_out[...] = proj
    put_rows(g2_out, conv)
    g2_out.send()
    put_rows(g1_out, first)


def norm_grad(t3, t4):
    return jnp.concatenate([t4[1:2], t4[0:1], t3[1:2], t3[0:1], t3[2:3], t3[0:1]], axis=0)


def step_of(w, g, m, a, weight_sq, grad_sq):
    weight_len = jnp.sqrt(weight_sq)
    trust = trust_coef * weight_len / (jnp.sqrt(grad_sq) + weight_decay * weight_len + tiny_term)
    step = trust * (g + weight_decay * w)
    m_new = momentum * m + step
    w_new = w - learn_rate * (step + momentum * m_new)
    return w_new, m_new, avg_decay * a + (1.0 - avg_decay) * w_new


def make_update(dp_count):
    def update(*refs):
        r6, t3, t4 = refs[:3]
        ins, outs = refs[3:18], refs[18:]
        total = jnp.broadcast_to(jnp.sum(r6[...], axis=0), (SIDE, r6.shape[2]))
        lane, row = (lax.broadcasted_iota(jnp.int32, total.shape, axis) for axis in (1, 0))
        total = [
            jnp.sum(jnp.where(lane == SIDE * k + row, total, 0.0), axis=1, keepdims=True)
            for k in range(3)
        ]
        for place in range(3):
            w, g, m, a = (ref[...] for ref in ins[4 * place : 4 * place + 4])
            weight_sq = total[0][2 * place : 2 * place + 1]
            grad_sq = total[0][2 * place + 1 : 2 * place + 2]
            for ref, value in zip(outs[3 * place :], step_of(w, g, m, a, weight_sq, grad_sq)):
                ref[...] = value
                ref.send()
        w, m, a = (ref[...] for ref in ins[12:15])
        weight_sq, grad_sq = total[1][0:6] / dp_count, total[2][0:6] / dp_count
        g = norm_grad(t3, t4)
        for ref, value in zip(outs[9:], step_of(w, g, m, a, weight_sq, grad_sq)):
            ref[...] = value

    return update


def exchange(blocks, axes):
    return lax.all_to_all(blocks, axes, 0, 0)


def rings():
    count = lax.axis_size("chan")
    return [[(d ^ (c % 2)) * count + c for d in RING] for c in range(count)]


def turn_round():
    return lax.axis_index("chan") % 2


def swap(array, axis, bits):
    return lax.ppermute(array, axis, [(i, i ^ bits) for i in range(lax.axis_size(axis))])


def away(axis, k):
    return lambda: lax.axis_index(axis) ^ k


def in_groups(taps, groups):
    return taps.reshape(taps.shape[0], groups, -1, taps.shape[2]).transpose(1, 0, 2, 3)


def regroup(blocks, taps, groups):
    blocks = blocks.reshape(blocks.shape[0], taps, -1, blocks.shape[2]).transpose(1, 0, 2, 3)
    blocks = in_groups(blocks.reshape(taps, -1, blocks.shape[3]), groups)
    return blocks.reshape(groups, -1, blocks.shape[3])


def per_device(
    images, mask, cotangent, w_first, w_second, w_proj, norm_params, mom_first, mom_second,
    mom_proj, mom_norm, avg_first, avg_second, avg_proj, avg_norm,
):
    everyone = ("dp", "chan")
    dp_count, ch_count = lax.axis_size("dp"), lax.axis_size("chan")
    n_all = dp_count * ch_count
    batch = mask.shape[0]
    pix_here, d_in = images.shape[1], images.shape[2]
    wide = w_first.shape[1]
    d_out = wide * ch_count
    part = batch * SIDE
    pix = SIDE * part
    share = batch // ch_count
    eight = dp_count == SIDE and pix_here == 4 * SIDE
    groups = SIDE
    first_rows, second_rows = 10 * d_in // groups, 9 * d_out // groups
    square_rows = result((SIDE, wide))
    four = result((dp_count, 4, wide), pinned=False)
    passing, few = (result((n, wide), pinned=False) for n in (pix, SIDE))

    def slot_dp(k):
        return lax.axis_index("dp") ^ k

    def slot_ch(k):
        return lax.axis_index("chan") ^ k

    def share_out(own):
        far = swap(own, "chan", 2)
        return [own, swap(own, "chan", 1), far, swap(far, "chan", 1)]

    if eight:
        own, squares = call(
            pack_weights,
            [w_first, w_proj, w_second],
            [result((first_rows + second_rows, wide), BF), square_rows],
        )
        gathered = lax.all_gather(own, everyone, axis_index_groups=rings())
        order = [lambda d=d: d ^ turn_round() for d in RING]
        mine, valid = call(
            pack_images,
            [quarter(images, dp_count, share), mask],
            [result((dp_count, 2, share * SIDE, 2 * d_in), BF), result((pix, wide))],
            scratch=[((d_in // wide, dp_count * share * pix_here, wide), F32)],
            later=[own],
        )
        pixels, slot = share_out(exchange(mine, "dp")), slot_ch
    else:
        valid = mask.reshape(batch, SIDE, SIDE).transpose(1, 0, 2).reshape(pix, 1).astype(F32)
        valid = jnp.broadcast_to(valid, (pix, wide))
        own = jnp.concatenate([tap_major(w_first), w_proj[None]], axis=0).astype(BF)
        own = lax.all_gather(own, "dp", axis=1, tiled=True)
        next = lax.all_gather(tap_major(w_second).astype(BF), "dp", axis=1, tiled=True)
        gathered = [in_groups(taps, groups).reshape(groups, -1, wide) for taps in (own, next)]
        gathered = jnp.concatenate(gathered, axis=1)
        order = [lambda g=g: g for g in range(groups)]
        squares = [jnp.sum(w * w, axis=0) for w in (w_first, w_proj, w_second)]
        squares = jnp.zeros((SIDE, wide), F32).at[:3].set(jnp.stack(squares))
        mine = images.reshape(dp_count, ch_count, share, pix_here, d_in)
        mine = lax.dynamic_index_in_dim(mine, lax.axis_index("chan"), 1, keepdims=False)
        pixels = lax.all_gather(exchange(mine, "dp"), "chan")
        cols = pix_here // 2
        pixels = pixels.reshape(ch_count, SIDE, 2, SIDE // cols, share, cols, 2 * d_in)
        pixels = pixels.transpose(0, 1, 2, 4, 3, 5, 6)
        pixels = pixels.reshape(ch_count, SIDE, 2, share * SIDE, 2 * d_in)
        pixels, slot = [pixels[k] for k in range(ch_count)], lambda k: k

    macs = pix * 9 * wide * d_in
    per_block = groups // ch_count
    block_slots = [lambda k=k: (lax.axis_index("chan") ^ k) * per_block for k in range(ch_count)]
    z_own, z_proj, sums_proj, pay = call(
        conv_first,
        [spread(gathered, order, 0, first_rows), stack(pixels, slot), valid, norm_params],
        [
            result((pix + TAIL, wide), BF),
            result((pix, wide)),
            square_rows,
            result((n_all, 4, wide)),
        ],
        flops=2 * macs,
    )
    turned = call(
        hand_on,
        [spread(gathered, order, 0, first_rows + second_rows)],
        [parts_of(0, block_slots, per_block, 0, first_rows + second_rows, gathered)],
        later=[z_own],
    )
    got1 = exchange(pay, everyone).reshape(dp_count, ch_count, 4, wide)
    z_all = [swap(z_own, "chan", k) for k in range(1, ch_count)]
    got1, *both = lax.optimization_barrier((got1, *z_all, *turned))
    z_all, turned = [z_own, *both[: ch_count - 1]], both[ch_count - 1 :]

    hidden, z_second, pay, total1, *near = call(
        conv_second,
        [
            stack(z_all, slot_ch, 3),
            fresh(got1),
            valid,
            spread(gathered, order, first_rows, second_rows),
            z_proj,
            sums_proj,
            cotangent,
        ],
        [
            result((pix, d_out), BF, pinned=False),
            passing,
            four,
            result((ch_count, SIDE, wide)),
            passing,
            passing,
            passing,
            few,
        ],
        flops=4 * macs,
    )
    turned = turned[:1] + [swap(block, "chan", k) for k, block in enumerate(turned) if k]
    total1_own = pick(total1, away("chan", 0))
    got2 = exchange(pay, "dp")
    near_valid, near_proj, near_cot, near_total = (fresh(array) for array in near)
    output, e, hat_second, hat_proj, near_rows, pay = call(
        block_output,
        [fresh(z_second), near_proj, fresh(got2), near_total, near_valid, norm_params, near_cot],
        [result((batch, SIDE * SIDE, wide), BF), passing, passing, passing, few, four],
    )
    got3 = exchange(pay, "dp")

    g_second_out, g_proj_out, total3 = call(
        grad_outputs,
        [fresh(e), fresh(hat_second), fresh(hat_proj), fresh(near_rows), fresh(got3), near_valid],
        [result((pix, wide), BF), result((pix, wide), BF), square_rows],
        later=turned[1:],
    )
    rows = second_rows + d_in // groups
    (grads,) = call(
        make_grad_second(eight),
        [fresh(hidden), g_second_out, even_phase(pixels, slot), g_proj_out],
        [result((groups, rows, wide), BF)],
        flops=4 * macs,
    )
    far = swap(g_second_out, "chan", 2)
    far, grads = lax.optimization_barrier((far, grads))
    g_all = [g_second_out, swap(g_second_out, "chan", 1), far, swap(far, "chan", 1)]
    if eight:
        grads_second = lax.psum_scatter(
            grads.reshape(groups * rows, wide),
            everyone,
            scatter_dimension=0,
            axis_index_groups=rings(),
            tiled=True,
        )
    else:
        grads = [
            regroup(grads[:, :second_rows], 9, dp_count),
            regroup(grads[:, second_rows:], 1, dp_count),
        ]
        grads = jnp.concatenate(grads, axis=1)
        grads_second = jnp.sum(exchange(grads, "dp").astype(F32), axis=0)

    back, msg, pay = call(
        grad_hidden,
        [stack_rows(turned, slot_ch, first_rows, second_rows, 3), stack(g_all, slot_ch, 3)]
        + [z_own, g_proj_out, total1_own, valid],
        [passing, result((2 * pix + TAIL, wide), BF), result((n_all, 2, wide), pinned=False)],
        flops=4 * macs,
    )
    got4 = exchange(pay, everyone).reshape(dp_count, ch_count, 2, wide)
    far = swap(msg, "chan", 2)
    far, got4 = lax.optimization_barrier((far, got4))
    messages = [msg, swap(msg, "chan", 1), far, swap(far, "chan", 1)]

    grads, total4 = call(
        grad_first,
        [fresh(back), z_own, fresh(got4), total1_own, norm_params, valid, stack(pixels, slot)],
        [result((groups, 9 * (d_in // groups), wide), BF), square_rows],
        flops=2 * macs,
    )
    if not eight:
        grads = regroup(grads, 9, dp_count)
    got_first = exchange(grads, "dp")

    half = wide // 2
    takes = [
        stack(messages, slot_ch, 3),
        stack(z_all, slot_ch, 3),
        fresh(got4),
        total1,
        valid,
        stack_rows(turned, slot_ch, 0, first_rows, 3),
    ]
    dims = (SIDE, 2, part, wide)
    if eight:
        rows = call(
            grad_images,
            takes,
            [split([away("dp", k) for k in range(SIDE)], dims, BF)],
            flops=2 * macs,
        )
        rows = rows[:1] + [swap(row, "dp", k) for k, row in enumerate(rows) if k]
    else:
        (rows,) = call(grad_images, takes, [result(dims, BF)], flops=2 * macs)
        cols = pix_here // 2
        rows = rows.reshape(SIDE, 2, batch, SIDE // cols, cols, wide)
        rows = rows.transpose(0, 1, 3, 2, 4, 5).reshape(dp_count, batch, cols, wide)
        rows = [exchange(rows, "dp")]
    reduced_first, reduced_second, reduced_proj, pay = call(
        reduce_all,
        [grads_second, fresh(got_first), squares, total3, total4, norm_params],
        [
            result(w_first.shape),
            result(w_second.shape),
            result(w_proj.shape),
            result((n_all, 1, wide)),
        ],
    )
    if eight:
        order = (0, 1, 2, 5, 4, 7, 3, 6)
        *sent, pay = lax.optimization_barrier((*(rows[k] for k in order), pay))
        rows = [sent[order.index(k)] for k in range(SIDE)]
    else:
        pay, *rows = lax.optimization_barrier((pay, *rows))
    got6 = exchange(pay, everyone)

    conv = (
        (w_first, reduced_first, mom_first, avg_first),
        (w_second, reduced_second, mom_second, avg_second),
        (w_proj, reduced_proj, mom_proj, avg_proj),
    )
    results = call(
        make_update(dp_count),
        [fresh(got6), total3, total4, *(array for group in conv for array in group)]
        + [norm_params, mom_norm, avg_norm],
        [result(group[0].shape) for group in conv for _ in range(3)]
        + [result(norm_params.shape)] * 3,
    )
    if eight:
        (grad_pixels,) = call(
            finish_images,
            [stack(rows, slot_dp, 7)],
            [result((images.shape[0], pix_here, half), BF)],
            scratch=[((images.shape[0] * pix_here, wide), F32)],
        )
    else:
        grad_pixels = rows[0].reshape(dp_count * batch, pix_here, half)
    return (output, grad_pixels, *results)


def solution(mesh):
    rows, cols, batch = P("dp", "chan"), P(None, "chan"), P("dp", None, "chan")
    weights = (rows, rows, rows, cols)
    in_specs = (P(None, "dp", None), P("dp", None), batch) + weights * 3
    out_specs = (batch, P(None, "dp", "chan")) + (rows,) * 9 + (cols,) * 3
    return jax.shard_map(
        per_device, mesh=mesh, in_specs=in_specs, out_specs=out_specs, check_vma=False
    )
```
